32 devices in a mesh: parts: 2 (over x), seq: 8 (over z, y), head: 2 (over core).
Axes of the slice: x: 2, y: 2, z: 4, core: 2. Of those that a mesh axis runs over, the one named last changes fastest.
Arguments:
- latents: bfloat16 [8192, 2112], P(('parts', 'seq', 'head')), parts along dimension 0, may hold values from -400 to 400
- q_gain: float32 [1536], replicated, may hold values from 0.25 to 1.75
- kv_gain: float32 [512], replicated, may hold values from 0.25 to 1.75
- q_weight: bfloat16 [2, 1536, 32, 192], P('head', None, 'seq'), may hold values from -0.15625 to 0.15625
- kv_weight: bfloat16 [2, 512, 32, 256], P('head', None, 'seq'), may hold values from -0.25 to 0.25
- lengths: int32 [16, 8], P('parts'), parts along dimension 0, may hold values from 0 to 512, as said below
Outputs:
- attended: bfloat16 [8192, 8192], P(('parts', 'seq'), 'head'), parts along dimension 0
The draws below stay inside these ranges and needn't reach their ends.
There are 2 independent parts, one for each index of `parts`. The reference program is written for one: setup_inputs(seed, part) draws one part's arguments, and reference() takes and returns one part's arrays. A program takes and returns all parts, laid end to end along the dimension named above; an argument that names none is the same for every part. Nothing has to cross between parts.
Inputs may be any that keep to these rules, and one draw needn't show every extreme that they name: Row g lists the lengths of the sequences packed in order in group g: they sum to 512, each is a multiple of 64, the nonzero ones come first. Some group holds a single sequence of 512 tokens; the group after it holds two sequences of 256 tokens, and the group 8 / 2 after that one holds 8 sequences of 64 tokens.
All inputs are finite; a program needn't handle non-finite values.
Results may differ from the reference program's by a relative error of at most 0.011.
Values may be sent and summed in bfloat16 or wider, within the bound.
No kernel may reach another device: no remote copies, remote signals or barrier semaphores. Data moves between devices by JAX's collectives and lax.ppermute only.
A program may use at most 128 MiB of HBM per device.

```python
import jax
import jax.numpy as jnp
from jax import lax

Q_LAT = 1536
KV_LAT = 512
ROPE = 64
NOPE = 128
VD = 128
H = 64
SLOTS = 8
TOK_DEV = 512
GROUPS = 8
HSH = 2
TOKENS = 4096


def draw_latents(key, part):
    key_base = jax.random.fold_in(key, 0)
    width_all = Q_LAT + KV_LAT + ROPE
    base_draw = jax.random.truncated_normal(key_base, -5.0, 5.0, (TOKENS, width_all), jnp.float32)
    return jnp.clip(base_draw, -400.0, 400.0).astype(jnp.bfloat16)


def draw_lengths(key, part):
    key_rate, key_bits, key_single = jax.random.split(key, 3)
    cut_rate = jax.random.randint(key_rate, (GROUPS, 1), 0, SLOTS)
    cut_bits = jax.random.randint(key_bits, (GROUPS, SLOTS - 1), 0, SLOTS) < cut_rate
    single_group = jax.random.randint(key_single, (), 0, GROUPS)
    cut_bits = cut_bits & (jnp.arange(GROUPS)[:, None] != single_group)
    ones_col = jnp.ones((GROUPS, 1), jnp.int32)
    edge_marks = jnp.concatenate([ones_col, cut_bits.astype(jnp.int32), ones_col], axis=1)
    edge_rank = jnp.cumsum(edge_marks, axis=1)
    slot_ids = jnp.arange(SLOTS + 1)
    hits = (edge_marks[:, :, None] == 1) & (edge_rank[:, :, None] == slot_ids[None, None, :] + 1)
    edge_where = jnp.sum(jnp.where(hits, slot_ids[None, :, None], 0), axis=1)
    edge_count = edge_rank[:, -1]
    order_ids = jnp.arange(SLOTS)
    valid = order_ids[None, :] + 1 < edge_count[:, None]
    span_sizes = edge_where[:, 1:] - edge_where[:, :-1]
    drawn = (jnp.where(valid, span_sizes, 0) * (TOK_DEV // SLOTS)).astype(jnp.int32)
    heavy_group = (single_group + 1) % GROUPS
    light_group = (heavy_group + GROUPS // 2) % GROUPS
    heavy_row = jnp.where(order_ids < 2, TOK_DEV // 2, 0).astype(jnp.int32)
    light_row = jnp.full((SLOTS,), TOK_DEV // SLOTS, jnp.int32)
    group_ids = jnp.arange(GROUPS)[:, None]
    drawn = jnp.where(group_ids == heavy_group, heavy_row[None, :], drawn)
    drawn = jnp.where(group_ids == light_group, light_row[None, :], drawn)
    return drawn.astype(jnp.int32)


def block_levels(key, shape, cuts, low, high):
    factor_of, own = 1.0, jax.random.fold_in(key, 6)
    for axis_at, blocks in cuts:
        steps = jnp.exp(jax.random.uniform(jax.random.fold_in(own, axis_at), (blocks,), jnp.float32, low / len(cuts), high / len(cuts)))
        factor_of = factor_of * jnp.repeat(steps, shape[axis_at] // blocks).reshape([-1 if axis == axis_at else 1 for axis in range(len(shape))])
    return factor_of


def centred(key, shape, width, most, cuts=(), kind=jnp.bfloat16):
    loudness = block_levels(key, shape, cuts, -0.22, 0.18) if cuts else 1.0
    values = jax.random.normal(key, shape, jnp.float32) * width * loudness
    return jnp.minimum(jnp.maximum(values, -most), most).astype(kind)


def setup_inputs(seed: int = 0, part: int = 0) -> dict:
    key_list = jax.random.split(jax.random.key(seed), 7)
    own_keys = jax.random.split(jax.random.fold_in(key_list[6], part), 7)
    latents = draw_latents(jax.random.fold_in(jax.random.fold_in(key_list[6], part), 71), part)
    q_gain = jnp.clip(1.0 + 0.15 * jax.random.normal(key_list[1], (Q_LAT,), jnp.float32), 0.25, 1.75)
    kv_gain = jnp.clip(1.0 + 0.15 * jax.random.normal(key_list[2], (KV_LAT,), jnp.float32), 0.25, 1.75)
    q_weight = centred(key_list[3], (HSH, Q_LAT, H // HSH, NOPE + ROPE), Q_LAT ** -0.5, 0.15625, ((0, 2), (2, 8)))
    kv_weight = centred(key_list[4], (HSH, KV_LAT, H // HSH, NOPE + VD), KV_LAT ** -0.5, 0.25, ((0, 2), (2, 8)))
    lengths = draw_lengths(jax.random.fold_in(jax.random.fold_in(key_list[6], part), 71), part)
    return {"latents": latents, "q_gain": q_gain, "kv_gain": kv_gain, "q_weight": q_weight, "kv_weight": kv_weight, "lengths": lengths}


epsilon = 1e-06

def rotary(values, positions):
    half_width = values.shape[-1] // 2
    freq_table = jnp.exp(jnp.arange(half_width, dtype=jnp.float32) * (-2.0 * jnp.log(10000.0) / values.shape[-1]))
    angles = positions.astype(jnp.float32)[:, None] * freq_table[None, :]
    if values.ndim == 3:
        angles = angles[:, None, :]
    cosine = jnp.cos(angles)
    sine_part = jnp.sin(angles)
    first_half = values[..., :half_width]
    second_half = values[..., half_width:]
    return jnp.concatenate([first_half * cosine - second_half * sine_part, second_half * cosine + first_half * sine_part], axis=-1)

def normalize(part_values, gain_vec):
    squares = lax.optimization_barrier(jnp.mean(part_values * part_values, axis=-1, keepdims=True))
    return (part_values * lax.rsqrt(squares + epsilon) * gain_vec).astype(jnp.bfloat16)

def seq_starts(length_row, token_count):
    seq_ends = jnp.cumsum(length_row).astype(jnp.int32)
    begins = (seq_ends - length_row).astype(jnp.int32)
    token_ids = jnp.arange(token_count, dtype=jnp.int32)
    inside = (token_ids[:, None] >= begins[None, :]) & (token_ids[:, None] < seq_ends[None, :])
    return lax.optimization_barrier(jnp.sum(jnp.where(inside, begins[None, :], 0), axis=1)).astype(jnp.int32)

def prepare(block_rows, q_gain, kv_gain, positions):
    q_width = q_gain.shape[0]
    kv_width = kv_gain.shape[0]
    q_part = block_rows[:, :q_width].astype(jnp.float32)
    kv_part = block_rows[:, q_width:q_width + kv_width].astype(jnp.float32)
    rope_part = block_rows[:, q_width + kv_width:].astype(jnp.float32)
    return (normalize(q_part, q_gain), normalize(kv_part, kv_gain), rotary(rope_part, positions).astype(jnp.bfloat16))

def dense_attention(queries, key_values, rope_keys, begins):
    token_count = queries.shape[0]
    rope_width = rope_keys.shape[1]
    nope_width = queries.shape[2] - rope_width
    score_scale = queries.shape[2] ** (-0.5)
    query_full = queries.astype(jnp.float32)
    pair_full = key_values.astype(jnp.float32)
    scores = jnp.einsum('qhd,khd->hqk', query_full[:, :, :nope_width], pair_full[:, :, :nope_width])
    scores = scores + jnp.einsum('qhd,kd->hqk', query_full[:, :, nope_width:], rope_keys.astype(jnp.float32))
    token_ids = jnp.arange(token_count, dtype=jnp.int32)
    allowed = (begins[:, None] <= token_ids[None, :]) & (token_ids[None, :] <= token_ids[:, None])
    scores = jnp.where(allowed[None], scores * score_scale, -jnp.inf)
    maxima = lax.optimization_barrier(jnp.max(scores, axis=-1, keepdims=True))
    exp_terms = jnp.exp(scores - maxima)
    totals = lax.optimization_barrier(jnp.sum(exp_terms, axis=-1))
    softmax_num = lax.optimization_barrier(exp_terms.astype(jnp.bfloat16)).astype(jnp.float32)
    mixed_out = jnp.einsum('hqk,khd->qhd', softmax_num, pair_full[:, :, nope_width:])
    return (mixed_out / totals.T[:, :, None]).astype(jnp.bfloat16)

def reference(latents, q_gain, kv_gain, q_weight, kv_weight, lengths):
    shard_count = q_weight.shape[0]
    per_shard = q_weight.shape[2]
    head_total = shard_count * per_shard
    query_table = jnp.transpose(q_weight, (1, 0, 2, 3)).reshape(q_weight.shape[1], head_total, q_weight.shape[3]).astype(jnp.float32)
    pair_table = jnp.transpose(kv_weight, (1, 0, 2, 3)).reshape(kv_weight.shape[1], head_total, kv_weight.shape[3]).astype(jnp.float32)
    group_count = lengths.shape[0]
    token_count = latents.shape[0] // group_count
    group_blocks = latents.reshape(group_count, token_count, latents.shape[1])

    def one_group(group_args):
        block_rows, length_row = group_args
        begins = seq_starts(length_row, token_count)
        positions = jnp.arange(token_count, dtype=jnp.int32) - begins
        q_normed, kv_normed, rope_keys = prepare(block_rows, q_gain, kv_gain, positions)
        projected = jnp.einsum('tc,chd->thd', q_normed.astype(jnp.float32), query_table)
        nope_width = projected.shape[2] - rope_keys.shape[1]
        queries = jnp.concatenate([projected[:, :, :nope_width], rotary(projected[:, :, nope_width:], positions)], axis=-1).astype(jnp.bfloat16)
        key_values = jnp.einsum('tc,chd->thd', kv_normed.astype(jnp.float32), pair_table).astype(jnp.bfloat16)
        mixed_out = dense_attention(queries, key_values, rope_keys, begins)
        return mixed_out.reshape(token_count, -1)
    return lax.map(one_group, (group_blocks, lengths)).reshape(latents.shape[0], -1)
```

```python
from functools import partial
import math

import jax
import jax.numpy as jnp
from jax import lax
from jax.experimental import pallas as pl
from jax.experimental.pallas import tpu as pltpu
from jax.sharding import PartitionSpec as P

epsilon = 1e-06
VMEM_LIMIT = 48 * 1024 * 1024
NT = (((1,), (1,)), ((), ()))
NN = (((1,), (0,)), ((), ()))


def frequencies(lane, half_width):
    steps = lax.rem(lane, half_width).astype(jnp.float32)
    return jnp.exp(steps * (-math.log(10000.0) / half_width))


def begins_of(lengths_ref, group, token_ids):
    begin = jnp.zeros_like(token_ids)
    start = jnp.int32(0)
    for slot in range(lengths_ref.shape[1]):
        begin = jnp.where(token_ids >= start, start, begin)
        start = start + lengths_ref[group, slot]
    return begin


def prepare_kernel(q_width, kv_width, place_ref, lengths_ref, latents_ref, q_gain_ref, kv_gain_ref, out_ref):
    rows = latents_ref.shape[1]
    rope_width = latents_ref.shape[0] - q_width - kv_width
    half_width = rope_width // 2

    def normalized(low, width, gain_ref):
        part = latents_ref[low : low + width, :].astype(jnp.float32)
        scale = lax.rsqrt(jnp.mean(part * part, axis=0, keepdims=True) + epsilon)
        return (jnp.transpose(part * scale) * gain_ref[...]).astype(jnp.bfloat16)

    out_ref[:, :q_width] = normalized(0, q_width, q_gain_ref)
    out_ref[:, q_width : q_width + kv_width] = normalized(q_width, kv_width, kv_gain_ref)
    token_ids = lax.broadcasted_iota(jnp.int32, (1, rows), 1) + place_ref[1] * rows
    position = (token_ids - begins_of(lengths_ref, place_ref[0], token_ids)).astype(jnp.float32)
    angle = position * frequencies(lax.broadcasted_iota(jnp.int32, (half_width, rows), 0), half_width)
    cosine, sine = jnp.cos(angle), jnp.sin(angle)
    rope = latents_ref[q_width + kv_width :, :].astype(jnp.float32)
    first, second = rope[:half_width], rope[half_width:]
    turned = jnp.concatenate([first * cosine - second * sine, second * cosine + first * sine], axis=0)
    spare = out_ref.shape[1] - q_width - kv_width - rope_width
    if spare:
        turned = jnp.concatenate([turned, jnp.zeros((spare, rows), jnp.float32)], axis=0)
    out_ref[:, q_width + kv_width :] = jnp.transpose(turned).astype(jnp.bfloat16)


def prepare(latents, q_gain, kv_gain, lengths, place):
    rows = latents.shape[0]
    width = -(-latents.shape[1] // 128) * 128
    smem = pl.BlockSpec(memory_space=pltpu.SMEM)
    vmem = pl.BlockSpec(memory_space=pltpu.VMEM)
    return pl.pallas_call(
        partial(prepare_kernel, q_gain.shape[0], kv_gain.shape[0]),
        out_shape=jax.ShapeDtypeStruct((rows, width), jnp.bfloat16),
        in_specs=[smem, smem, vmem, vmem, vmem],
        out_specs=vmem,
        compiler_params=pltpu.CompilerParams(vmem_limit_bytes=VMEM_LIMIT),
        cost_estimate=pl.CostEstimate(flops=8 * rows * width, bytes_accessed=4 * rows * width, transcendentals=rows * 64),
        name="prepare",
    )(place, lengths, jnp.transpose(latents), q_gain[None, :], kv_gain[None, :])


def attend_kernel(sizes, place_ref, lengths_ref, table_ref, q_weight_ref, kv_weight_ref, *refs):
    slots, heads, q_width, kv_width, nope_width, rope_width, value_width = sizes
    same_refs, other_refs, out_refs = refs[:slots], refs[slots : 2 * slots], refs[2 * slots : 3 * slots]
    query_ref, key_ref, value_ref, turn_ref, bias_ref = refs[3 * slots :]
    core = place_ref[0]
    rows = same_refs[0].shape[0]
    half_width = rope_width // 2
    score_scale = (nope_width + rope_width) ** -0.5
    slot_count = lengths_ref.shape[1]
    block = 2 * rows // slot_count
    for slot in range(slots):
        group = place_ref[1 + slot]
        starts, start = [], jnp.int32(0)
        for index in range(slot_count):
            starts.append(start)
            start = start + lengths_ref[group, index]
        for index in range(slot_count):
            begin = jnp.int32(0)
            for entry in starts:
                begin = jnp.where(entry <= index * block, entry, begin)
            position = pl.multiple_of(index * block - begin, block)
            turn_ref[index * block : (index + 1) * block, :] = table_ref[pl.ds(position, block), :]
        row_ids = lax.broadcasted_iota(jnp.int32, (2 * rows, 1), 0)
        begins = begins_of(lengths_ref, group, row_ids)
        col_ids = lax.broadcasted_iota(jnp.int32, (2 * rows, 2 * rows), 1)
        allowed = (col_ids <= row_ids) & (col_ids >= begins)
        bias_ref[...] = jnp.where(allowed, 0.0, -jnp.inf)
        for head in range(heads):
            for tokens_ref, half in ((same_refs[slot], core), (other_refs[slot], 1 - core)):
                span = pl.ds(pl.multiple_of(half * rows, rows), rows)
                projected = lax.dot_general(
                    tokens_ref[:, :q_width], q_weight_ref[head], NT, preferred_element_type=jnp.float32
                )
                rope = projected[:, nope_width:]
                swapped = jnp.concatenate([rope[:, half_width:], rope[:, :half_width]], axis=1)
                turned = rope * turn_ref[span, :rope_width] + swapped * turn_ref[span, rope_width : 2 * rope_width]
                query_ref[head, span, :nope_width] = projected[:, :nope_width].astype(jnp.bfloat16)
                query_ref[head, span, nope_width:] = turned.astype(jnp.bfloat16)
                pair = lax.dot_general(
                    tokens_ref[:, q_width : q_width + kv_width],
                    kv_weight_ref[head],
                    NN,
                    preferred_element_type=jnp.float32,
                ).astype(jnp.bfloat16)
                key_ref[head, span, :nope_width] = pair[:, :nope_width]
                key_ref[head, span, nope_width:] = tokens_ref[:, q_width + kv_width : q_width + kv_width + rope_width]
                value_ref[head, span, :] = pair[:, nope_width:]
            for half in range(2):
                low, high = half * rows, (half + 1) * rows
                scores = lax.dot_general(
                    query_ref[head, low:high], key_ref[head, :high], NT, preferred_element_type=jnp.float32
                )
                scores = scores * score_scale + bias_ref[low:high, :high]
                terms = jnp.exp(scores - jnp.max(scores, axis=1, keepdims=True))
                totals = jnp.sum(terms, axis=1, keepdims=True)
                mixed = lax.dot_general(
                    terms.astype(jnp.bfloat16), value_ref[head, :high], NN, preferred_element_type=jnp.float32
                )
                out_refs[slot][low:high, head * value_width : (head + 1) * value_width] = (mixed / totals).astype(
                    jnp.bfloat16
                )


def attend(same, other, groups, core, q_weight, kv_weight, table, lengths, rope_width):
    slots = len(same)
    rows = same[0].shape[0]
    heads, query_width, q_width = q_weight.shape
    kv_width, pair_width = kv_weight.shape[1:]
    nope_width = query_width - rope_width
    value_width = pair_width - nope_width
    smem = pl.BlockSpec(memory_space=pltpu.SMEM)
    vmem = pl.BlockSpec(memory_space=pltpu.VMEM)
    place = jnp.stack([core] + groups).astype(jnp.int32)
    sizes = (slots, heads, q_width, kv_width, nope_width, rope_width, value_width)
    tokens = 2 * rows
    flops = 2 * slots * heads * tokens * (q_width * query_width + kv_width * pair_width + tokens * (query_width + value_width))
    out_shape = jax.ShapeDtypeStruct((tokens, heads * value_width), jnp.bfloat16)
    return pl.pallas_call(
        partial(attend_kernel, sizes),
        out_shape=[out_shape] * slots,
        in_specs=[smem, smem] + [vmem] * (3 + 2 * slots),
        out_specs=[vmem] * slots,
        scratch_shapes=[
            pltpu.VMEM((heads, tokens, query_width), jnp.bfloat16),
            pltpu.VMEM((heads, tokens, query_width), jnp.bfloat16),
            pltpu.VMEM((heads, tokens, value_width), jnp.bfloat16),
            pltpu.VMEM((tokens, 2 * rope_width), jnp.float32),
            pltpu.VMEM((tokens, tokens), jnp.float32),
        ],
        compiler_params=pltpu.CompilerParams(vmem_limit_bytes=VMEM_LIMIT),
        cost_estimate=pl.CostEstimate(
            flops=flops,
            bytes_accessed=2 * slots * rows * (q_width + kv_width) * 2 + 2 * heads * (query_width * q_width + kv_width * pair_width),
            transcendentals=slots * heads * tokens * tokens,
        ),
        name="attend",
    )(place, lengths, table, q_weight, kv_weight, *same, *other)


def place_kernel(count, offsets_ref, *refs):
    pieces, out_ref, sems = refs[:count], refs[-2], refs[-1]
    copies = []
    for index, piece in enumerate(pieces):
        width = piece.shape[1]
        columns = pl.ds(pl.multiple_of(offsets_ref[index], 128), width)
        copies.append(pltpu.make_async_copy(piece, out_ref.at[:, columns], sems.at[index]))
        copies[-1].start()
    for copy in copies:
        copy.wait()


def place_pieces(pieces, offsets, width, held=None):
    count = len(pieces)
    any_space = pl.BlockSpec(memory_space=pl.ANY)
    operands = [jnp.stack(offsets).astype(jnp.int32), *pieces]
    aliases = {}
    if held is not None:
        aliases = {len(operands): 0}
        operands.append(held)
    return pl.pallas_call(
        partial(place_kernel, count),
        out_shape=jax.ShapeDtypeStruct((pieces[0].shape[0], width), pieces[0].dtype),
        in_specs=[pl.BlockSpec(memory_space=pltpu.SMEM)] + [any_space] * (len(operands) - 1),
        out_specs=any_space,
        scratch_shapes=[pltpu.SemaphoreType.DMA((count,))],
        input_output_aliases=aliases,
        name="place_pieces",
    )(*operands)


def shards(latents, q_gain, kv_gain, q_weight, kv_weight, lengths):
    rope_width = latents.shape[1] - q_gain.shape[0] - kv_gain.shape[0]
    places = lax.axis_size("seq")
    parts = lax.axis_size("parts")
    half_places = places // 2
    place = lax.axis_index("seq")
    core = lax.axis_index("head")
    part = lax.axis_index("parts")
    tokens = 2 * latents.shape[0]
    local_heads = q_weight.shape[2]
    value_width = kv_weight.shape[3] - (q_weight.shape[3] - rope_width)
    block_width = local_heads * value_width

    def across(value, distance):
        return lax.ppermute(value, "seq", [(s, s ^ distance) for s in range(places)])

    def sibling(value):
        return lax.ppermute(value, "head", [(0, 1), (1, 0)])

    def other_part(value):
        return lax.ppermute(value, "parts", [(p, p ^ 1) for p in range(parts)])

    same = [prepare(latents, q_gain, kv_gain, lengths, jnp.stack([place, core]).astype(jnp.int32))]
    other = [sibling(same[0])]
    for distance in range(1, half_places):
        low_bit = distance & -distance
        same.append(across(same[distance ^ low_bit], low_bit))
        other.append(sibling(same[distance]))
    groups = [place ^ distance for distance in range(half_places)]

    own_query = jnp.transpose(q_weight[0], (1, 2, 0))
    own_pair = jnp.transpose(kv_weight[0], (1, 0, 2))

    share = 2 if parts % 2 == 0 and local_heads % 2 == 0 else 1
    per_part = local_heads // share
    side = lax.rem(part, share)
    far = []
    for index in range(per_part):
        head = side * per_part + index
        first = across(lax.dynamic_index_in_dim(own_query, head, 0, keepdims=True), half_places)
        second = across(lax.dynamic_index_in_dim(own_pair, head, 0, keepdims=True), half_places)
        far.append((first, second, head))
        if share == 2:
            far.append((other_part(first), other_part(second), (1 - side) * per_part + index))

    positions = jnp.arange(tokens, dtype=jnp.int32)[:, None].astype(jnp.float32)
    lanes = jnp.arange(rope_width, dtype=jnp.int32)[None, :]
    angles = positions * frequencies(lanes, rope_width // 2)
    signs = jnp.where(lanes < rope_width // 2, -1.0, 1.0)
    table = jnp.concatenate([jnp.cos(angles), jnp.sin(angles) * signs], axis=1)

    pieces, offsets = [], []
    for distance in range(half_places):
        (mixed,) = attend(
            [same[distance]], [other[distance]], [groups[distance]], core, own_query, own_pair, table, lengths, rope_width
        )
        pieces.append(across(mixed, distance) if distance else mixed)
        offsets.append((place ^ distance) * block_width)
    for query_part, pair_part, head in far:
        mixed_all = attend(same, other, groups, core, query_part, pair_part, table, lengths, rope_width)
        for distance in range(half_places):
            pieces.append(across(mixed_all[distance], distance) if distance else mixed_all[0])
            offsets.append((place ^ distance ^ half_places) * block_width + head * value_width)
    return place_pieces(pieces, offsets, places * block_width)


def solution(mesh):
    return jax.shard_map(
        shards,
        mesh=mesh,
        in_specs=(
            P(("parts", "seq", "head"), None),
            P(),
            P(),
            P("head", None, "seq", None),
            P("head", None, "seq", None),
            P("parts", None),
        ),
        out_specs=P(("parts", "seq"), "head"),
        check_vma=False,
    )
```

```python
from functools import partial
import math

import jax
import jax.numpy as jnp
from jax import lax
from jax.experimental import pallas as pl
from jax.experimental.pallas import tpu as pltpu
from jax.sharding import PartitionSpec as P

epsilon = 1e-06
VMEM_LIMIT = 32 * 1024 * 1024
LIGHT = pl.CostEstimate(flops=1024, bytes_accessed=1024, transcendentals=0)
NT = (((1,), (1,)), ((), ()))
NN = (((1,), (0,)), ((), ()))


def frequencies(lane, half_width):
    steps = lax.rem(lane, half_width).astype(jnp.float32)
    return jnp.exp(steps * (-math.log(10000.0) / half_width))


def begins_of(lengths_ref, group, token_ids):
    begin = jnp.zeros_like(token_ids)
    start = jnp.int32(0)
    for slot in range(lengths_ref.shape[1]):
        begin = jnp.where(token_ids >= start, start, begin)
        start = start + lengths_ref[group, slot]
    return begin


def prepare_kernel(q_width, kv_width, place_ref, lengths_ref, latents_ref, q_gain_ref, kv_gain_ref, out_ref):
    rows = latents_ref.shape[1]
    rope_width = latents_ref.shape[0] - q_width - kv_width
    half_width = rope_width // 2

    def normalized(low, width, gain_ref):
        part = latents_ref[low : low + width, :].astype(jnp.float32)
        scale = lax.rsqrt(jnp.mean(part * part, axis=0, keepdims=True) + epsilon)
        return (jnp.transpose(part * scale) * gain_ref[...]).astype(jnp.bfloat16)

    out_ref[:, :q_width] = normalized(0, q_width, q_gain_ref)
    out_ref[:, q_width : q_width + kv_width] = normalized(q_width, kv_width, kv_gain_ref)
    token_ids = lax.broadcasted_iota(jnp.int32, (1, rows), 1) + place_ref[1] * rows
    position = (token_ids - begins_of(lengths_ref, place_ref[0], token_ids)).astype(jnp.float32)
    angle = position * frequencies(lax.broadcasted_iota(jnp.int32, (half_width, rows), 0), half_width)
    cosine, sine = jnp.cos(angle), jnp.sin(angle)
    rope = latents_ref[q_width + kv_width :, :].astype(jnp.float32)
    first, second = rope[:half_width], rope[half_width:]
    turned = jnp.concatenate([first * cosine - second * sine, second * cosine + first * sine], axis=0)
    spare = out_ref.shape[1] - q_width - kv_width - rope_width
    if spare:
        turned = jnp.concatenate([turned, jnp.zeros((spare, rows), jnp.float32)], axis=0)
    out_ref[:, q_width + kv_width :] = jnp.transpose(turned).astype(jnp.bfloat16)


def prepare(latents, q_gain, kv_gain, lengths, place):
    rows = latents.shape[0]
    width = -(-latents.shape[1] // 128) * 128
    smem = pl.BlockSpec(memory_space=pltpu.SMEM)
    vmem = pl.BlockSpec(memory_space=pltpu.VMEM)
    return pl.pallas_call(
        partial(prepare_kernel, q_gain.shape[0], kv_gain.shape[0]),
        out_shape=jax.ShapeDtypeStruct((rows, width), jnp.bfloat16),
        in_specs=[smem, smem, vmem, vmem, vmem],
        out_specs=vmem,
        compiler_params=pltpu.CompilerParams(vmem_limit_bytes=VMEM_LIMIT),
        cost_estimate=LIGHT,
        name="prepare",
    )(place, lengths, jnp.transpose(latents), q_gain[None, :], kv_gain[None, :])


def pick_kernel(index_ref, source_ref, out_ref):
    out_ref[...] = source_ref[...].reshape(out_ref.shape)


def pick(source, index, block, axis):
    shape = list(source.shape)
    shape[axis] = block
    out_shape = [entry for entry in shape if entry != 1]
    position = lambda step, index_ref: tuple(index_ref[0] if at == axis else 0 for at in range(len(shape)))
    return pl.pallas_call(
        pick_kernel,
        grid_spec=pltpu.PrefetchScalarGridSpec(
            num_scalar_prefetch=1,
            grid=(1,),
            in_specs=[pl.BlockSpec(tuple(shape), position)],
            out_specs=pl.BlockSpec(tuple(out_shape), lambda step, index_ref: (0,) * len(out_shape)),
        ),
        out_shape=jax.ShapeDtypeStruct(tuple(out_shape), source.dtype),
        compiler_params=pltpu.CompilerParams(vmem_limit_bytes=VMEM_LIMIT),
        cost_estimate=LIGHT,
        name="pick",
    )(jnp.reshape(index, (1,)).astype(jnp.int32), source)


def project(tokens_ref, sizes, weight_refs, pair_at):
    heads, q_width, kv_width, nope_width, rope_width, value_width = sizes
    query_width, pair_width = nope_width + rope_width, nope_width + value_width

    def dot(tokens, weight, dims):
        return lax.dot_general(tokens, weight, dims, preferred_element_type=jnp.float32)

    latent = tokens_ref[:, q_width : q_width + kv_width]
    if pair_at is None:
        query_ref, pair_ref = weight_refs
        joint = dot(latent, pair_ref[...], NN)
        pair = [joint[:, head * pair_width : (head + 1) * pair_width] for head in range(heads)]
    else:
        pair = []
        for head in range(heads):
            low = pair_at[head] * pair_width
            pair.append(dot(latent, weight_refs[heads + head][:, low : low + pair_width], NN))

    def query(low, high, chosen):
        parts = [(query_ref.at[head] if pair_at is None else weight_refs[head])[low:high, :] for head in chosen]
        return dot(tokens_ref[:, :q_width], jnp.concatenate(parts, axis=0), NT)

    nope = []
    for head in range(0, heads, 2):
        nope.append(query(0, nope_width, range(head, min(head + 2, heads))))
    group = nope_width // rope_width
    chosen = list(range(heads))
    while len(chosen) % group:
        chosen.append(heads - 1)
    rope = query(nope_width, query_width, chosen)
    return nope, rope, pair


def attend_kernel(sizes, slots, pair_at, place_ref, lengths_ref, table_ref, *refs):
    heads, q_width, kv_width, nope_width, rope_width, value_width = sizes
    weight_count = 2 if pair_at is None else 2 * heads
    weight_refs, refs = refs[:weight_count], refs[weight_count:]
    same_refs, other_refs, out_refs = refs[:slots], refs[slots : 2 * slots], refs[2 * slots : 3 * slots]
    tokens_ref, nope_ref, rope_ref, key_ref, value_ref, shared_ref, turn_ref, bias_ref = refs[3 * slots : 3 * slots + 8]
    result_ref = refs[-1] if slots > 1 else out_refs[0]
    core = place_ref[0]
    rows = same_refs[0].shape[0]
    tokens = 2 * rows
    half_width = rope_width // 2
    group_heads = nope_width // rope_width
    score_scale = (nope_width + rope_width) ** -0.5 * math.log2(math.e)
    slot_count = lengths_ref.shape[1]
    block = tokens // slot_count
    for head in range(heads):
        value_ref[head, :, value_width:] = jnp.ones((tokens, value_width), jnp.bfloat16)
    def one_group(slot, carry):
        group = place_ref[1 + slot]
        for index in range(slots):

            @pl.when(slot == index)
            def _(index=index):
                tokens_ref[pl.ds(pl.multiple_of(core * rows, rows), rows), :] = same_refs[index][...]
                tokens_ref[pl.ds(pl.multiple_of((1 - core) * rows, rows), rows), :] = other_refs[index][...]

        starts, start = [], jnp.int32(0)
        for index in range(slot_count):
            starts.append(start)
            start = start + lengths_ref[group, index]
        for index in range(slot_count):
            begin = jnp.int32(0)
            for entry in starts:
                begin = jnp.where(entry <= index * block, entry, begin)
            position = pl.multiple_of(index * block - begin, block)
            turn_ref[index * block : (index + 1) * block, :] = table_ref[pl.ds(position, block), :]
        row_ids = lax.broadcasted_iota(jnp.int32, (tokens, 1), 0)
        begins = begins_of(lengths_ref, group, row_ids)
        col_ids = lax.broadcasted_iota(jnp.int32, (tokens, tokens), 1)
        bias_ref[...] = jnp.where((col_ids <= row_ids) & (col_ids >= begins), 0.0, -jnp.inf)

        nope, rope, pair = project(tokens_ref, sizes, weight_refs, pair_at)
        for index, part in enumerate(nope):
            low = index * 2 * nope_width
            nope_ref[:, low : low + part.shape[1]] = (part * score_scale).astype(jnp.bfloat16)
        lane = lax.broadcasted_iota(jnp.int32, (tokens, nope_width), 1)
        is_first = lax.rem(lane, rope_width) < half_width
        for low in range(0, rope.shape[1], nope_width):
            part = rope[:, low : low + nope_width]
            swapped = jnp.where(
                is_first, pltpu.roll(part, nope_width - half_width, 1), pltpu.roll(part, half_width, 1)
            )
            turned = part * turn_ref[:, :nope_width] + swapped * turn_ref[:, nope_width:]
            rope_ref[:, low : low + nope_width] = (turned * score_scale).astype(jnp.bfloat16)
        for head in range(heads):
            both = pair[head].astype(jnp.bfloat16)
            key_ref[:, head * nope_width : (head + 1) * nope_width] = both[:, :nope_width]
            value_ref[head, :, :value_width] = both[:, nope_width:]
        shared = tokens_ref[:, q_width + kv_width : q_width + kv_width + rope_width]
        blank = jnp.zeros((tokens, rope_width), jnp.bfloat16)
        for index in range(group_heads):
            shared_ref[index] = jnp.concatenate(
                [shared if index == entry else blank for entry in range(group_heads)], axis=1
            )

        for head in range(heads):
            nope_span = slice(head * nope_width, (head + 1) * nope_width)
            rope_low = head // group_heads * nope_width
            for half in range(2):
                low, high = half * rows, (half + 1) * rows
                queries = jnp.concatenate(
                    [nope_ref[low:high, nope_span], rope_ref[low:high, rope_low : rope_low + nope_width]], axis=1
                )
                keys = jnp.concatenate([key_ref[:high, nope_span], shared_ref[head % group_heads, :high, :]], axis=1)
                scores = lax.dot_general(queries, keys, NT, preferred_element_type=jnp.float32)
                scores = scores + bias_ref[low:high, :high]
                terms = jnp.exp2(scores - jnp.max(scores, axis=1, keepdims=True)).astype(jnp.bfloat16)
                mixed = lax.dot_general(terms, value_ref[head, :high, :], NN, preferred_element_type=jnp.float32)
                result_ref[low:high, head * value_width : (head + 1) * value_width] = (
                    mixed[:, :value_width] / mixed[:, value_width:]
                ).astype(jnp.bfloat16)
        for index in range(slots if slots > 1 else 0):

            @pl.when(slot == index)
            def _(index=index):
                out_refs[index][...] = result_ref[...]

        return carry

    if slots > 1:
        lax.fori_loop(0, slots, one_group, 0)
    else:
        one_group(0, 0)


def attend(same, other, groups, core, weights, sizes, table, lengths, pair_at=None):
    slots = len(same)
    rows, width = same[0].shape
    heads, q_width, kv_width, nope_width, rope_width, value_width = sizes
    smem = pl.BlockSpec(memory_space=pltpu.SMEM)
    vmem = pl.BlockSpec(memory_space=pltpu.VMEM)
    place = jnp.stack([core] + groups).astype(jnp.int32)
    tokens = 2 * rows
    group_heads = nope_width // rope_width
    rope_heads = -(-heads // group_heads) * group_heads
    return pl.pallas_call(
        partial(attend_kernel, sizes, slots, pair_at),
        out_shape=[jax.ShapeDtypeStruct((tokens, heads * value_width), jnp.bfloat16)] * slots,
        in_specs=[smem, smem] + [vmem] * (1 + len(weights) + 2 * slots),
        out_specs=[vmem] * slots,
        scratch_shapes=[
            pltpu.VMEM((tokens, width), jnp.bfloat16),
            pltpu.VMEM((tokens, heads * nope_width), jnp.bfloat16),
            pltpu.VMEM((tokens, rope_heads * rope_width), jnp.bfloat16),
            pltpu.VMEM((tokens, heads * nope_width), jnp.bfloat16),
            pltpu.VMEM((heads, tokens, 2 * value_width), jnp.bfloat16),
            pltpu.VMEM((group_heads, tokens, nope_width), jnp.bfloat16),
            pltpu.VMEM((tokens, 2 * nope_width), jnp.float32),
            pltpu.VMEM((tokens, tokens), jnp.float32),
        ]
        + ([pltpu.VMEM((tokens, heads * value_width), jnp.bfloat16)] if slots > 1 else []),
        compiler_params=pltpu.CompilerParams(vmem_limit_bytes=VMEM_LIMIT),
        cost_estimate=LIGHT,
        name="attend",
    )(place, lengths, table, *weights, *same, *other)


def place_kernel(width, count, offsets_ref, *refs):
    pieces, out_ref, sems = refs[:count], refs[-2], refs[-1]
    copies = []
    for piece in pieces:
        for low in range(0, piece.shape[1], width):
            index = len(copies)
            columns = pl.ds(pl.multiple_of(offsets_ref[index], 128), width)
            copies.append(pltpu.make_async_copy(piece.at[:, low : low + width], out_ref.at[:, columns], sems.at[index]))
            copies[-1].start()
    for copy in copies:
        copy.wait()


def place_pieces(pieces, offsets, width, out_width, held=None):
    count = len(pieces)
    any_space = pl.BlockSpec(memory_space=pl.ANY)
    operands = [jnp.stack(offsets).astype(jnp.int32), *pieces]
    specs = [pl.BlockSpec(memory_space=pltpu.SMEM)] + [pl.BlockSpec(memory_space=pltpu.VMEM)] * count
    aliases = {}
    if held is not None:
        aliases = {len(operands): 0}
        operands.append(held)
        specs.append(any_space)
    return pl.pallas_call(
        partial(place_kernel, width, count),
        out_shape=jax.ShapeDtypeStruct((pieces[0].shape[0], out_width), pieces[0].dtype),
        in_specs=specs,
        out_specs=any_space,
        scratch_shapes=[pltpu.SemaphoreType.DMA((len(offsets),))],
        input_output_aliases=aliases,
        compiler_params=pltpu.CompilerParams(vmem_limit_bytes=VMEM_LIMIT),
        cost_estimate=LIGHT,
        name="place_pieces",
    )(*operands)


def after(value, *earlier):
    return lax.optimization_barrier((value, *earlier))[0]


def shards(latents, q_gain, kv_gain, q_weight, kv_weight, lengths):
    q_width, kv_width = q_gain.shape[0], kv_gain.shape[0]
    rope_width = latents.shape[1] - q_width - kv_width
    places = lax.axis_size("seq")
    parts = lax.axis_size("parts")
    half_places = places // 2
    place = lax.axis_index("seq")
    core = lax.axis_index("head")
    part = lax.axis_index("parts")
    tokens = 2 * latents.shape[0]
    local_heads = q_weight.shape[2]
    pair_width = kv_weight.shape[3]
    nope_width = q_weight.shape[3] - rope_width
    value_width = pair_width - nope_width
    block_width = local_heads * value_width
    sizes = (q_width, kv_width, nope_width, rope_width, value_width)

    def across(value, distance):
        return lax.ppermute(value, "seq", [(s, s ^ distance) for s in range(places)])

    def sibling(value):
        return lax.ppermute(value, "head", [(0, 1), (1, 0)])

    def other_part(value):
        return lax.ppermute(value, "parts", [(p, p ^ 1) for p in range(parts)])

    own_query = jnp.transpose(q_weight[0], (1, 2, 0))
    own_pair = jnp.reshape(kv_weight[0], (kv_width, local_heads * pair_width))
    positions = jnp.arange(tokens, dtype=jnp.int32)[:, None].astype(jnp.float32)
    lanes = jnp.arange(nope_width, dtype=jnp.int32)[None, :]
    angles = positions * frequencies(lanes, rope_width // 2)
    signs = jnp.where(lax.rem(lanes, rope_width) < rope_width // 2, -1.0, 1.0)
    table = jnp.concatenate([jnp.cos(angles), jnp.sin(angles) * signs], axis=1)
    groups = [place ^ distance for distance in range(half_places)]

    share = 2 if parts % 2 == 0 and local_heads % 2 == 0 else 1
    per_part = local_heads // share
    side = lax.rem(part, share)

    latent = prepare(latents, q_gain, kv_gain, lengths, jnp.stack([place, core]).astype(jnp.int32))
    same, other = [latent], [sibling(latent)]
    for distance in range(1, half_places):
        same.append(across(latent, distance) if distance & (distance - 1) == 0 else None)
    sent = [pick(own_query, side * per_part + index, 1, 0) for index in range(per_part)]
    sent.insert(1, pick(own_pair, side, per_part * pair_width, 1))
    far = [across(sent[0], half_places)]

    def near(distance, *earlier):
        (mixed,) = attend(
            [after(same[distance], *earlier)],
            [other[distance]],
            [groups[distance]],
            core,
            [own_query, own_pair],
            (local_heads, *sizes),
            table,
            lengths,
        )
        return mixed

    mixed = near(0)
    arrived = [mixed]
    direct = [entry for entry in same[1:] if entry is not None]
    early = far[0]
    for index in range(1, len(sent)):
        far.append(across(after(sent[index], far[index - 1]), half_places))
    for distance in range(1, half_places):
        if same[distance] is None:
            low_bit = distance & -distance
            same[distance] = across(after(same[distance ^ low_bit], mixed), low_bit)
            other.append(None)
        else:
            other.append(sibling(after(same[distance], mixed, early, *direct)))
    crossed = [other_part(after(far[0], mixed))] if share == 2 else []
    for distance in range(1, half_places):
        if other[distance] is None:
            other[distance] = sibling(after(same[distance], mixed, far[1]))
        mixed = near(distance, mixed)
        arrived.append(across(mixed, distance))
    if share == 2:
        crossed.append(other_part(after(far[1], arrived[half_places // 2])))

    placed = []
    for distance in range(half_places):
        base = (place ^ distance) * block_width
        placed.append((arrived[distance], [base + head * value_width for head in range(local_heads)]))
    previous, waiting = arrived[1:-1], arrived[-1:]
    for index in range(per_part):
        at = 2 * index
        chosen = [(far[at], far[1], side * per_part + index)]
        if share == 2:
            if index:
                crossed.append(other_part(after(far[at], mixed)))
            chosen.append((crossed[at], crossed[1], (1 - side) * per_part + index))
        for entries in [[entry] for entry in chosen] if index + 1 == per_part else [chosen]:
            mixed_all = attend(
                [after(same[0], mixed, *previous)] + same[1:],
                other,
                groups,
                core,
                [entry[0] for entry in entries] + [entry[1] for entry in entries],
                (len(entries), *sizes),
                table,
                lengths,
                [index] * len(entries),
            )
            mixed = mixed_all[0]
            received = [across(mixed_all[distance], distance) for distance in range(1, half_places)]
            previous = waiting + received[:-1]
            waiting = received[-1:]
            for distance, piece in enumerate([mixed] + received):
                base = (place ^ distance ^ half_places) * block_width
                placed.append((piece, [base + head * value_width for first, second, head in entries]))
    held, out_width = None, places * block_width
    late = len(placed) - 2 * half_places
    for batch in (placed[:late], placed[late:]):
        offsets = [offset for piece, starts in batch for offset in starts]
        held = place_pieces([piece for piece, starts in batch], offsets, value_width, out_width, held)
    return held


def solution(mesh):
    return jax.shard_map(
        shards,
        mesh=mesh,
        in_specs=(
            P(("parts", "seq", "head"), None),
            P(),
            P(),
            P("head", None, "seq", None),
            P("head", None, "seq", None),
            P("parts", None),
        ),
        out_specs=P(("parts", "seq"), "head"),
        check_vma=False,
    )
```

```python
from functools import partial
import math

import jax
import jax.numpy as jnp
from jax import lax
from jax.experimental import pallas as pl
from jax.experimental.pallas import tpu as pltpu
from jax.sharding import PartitionSpec as P

epsilon = 1e-06
VMEM_LIMIT = 32 * 1024 * 1024
LIGHT = pl.CostEstimate(flops=1024, bytes_accessed=1024, transcendentals=0)
FAR = -(2.0**100)
NT = (((1,), (1,)), ((), ()))
NN = (((1,), (0,)), ((), ()))


def frequencies(lane, half_width):
    steps = lax.rem(lane, half_width).astype(jnp.float32)
    return jnp.exp(steps * (-math.log(10000.0) / half_width))


def prepare_kernel(q_width, kv_width, slot_count, place_ref, latents_ref, gain_ref, out_ref):
    rows = latents_ref.shape[1]
    rope_width = latents_ref.shape[0] - q_width - kv_width
    half_width = rope_width // 2

    def normalized(low, width):
        part = latents_ref[low : low + width, :].astype(jnp.float32)
        scale = lax.rsqrt(jnp.mean(part * part, axis=0, keepdims=True) + epsilon)
        return (jnp.transpose(part * scale) * gain_ref[:, low : low + width]).astype(jnp.bfloat16)

    out_ref[:, :q_width] = normalized(0, q_width)
    out_ref[:, q_width : q_width + kv_width] = normalized(q_width, kv_width)
    spare = out_ref.shape[1] - q_width - kv_width - rope_width
    token_ids = lax.broadcasted_iota(jnp.int32, (1, rows), 1) + place_ref[1] * rows
    slot_ids = lax.broadcasted_iota(jnp.int32, (spare, rows), 0)
    begin, start, inside = jnp.zeros_like(token_ids), jnp.int32(0), jnp.zeros((spare, rows), jnp.float32)
    for slot in range(slot_count):
        stop = start + place_ref[2 + place_ref[0] * slot_count + slot]
        begin = jnp.where(token_ids >= start, start, begin)
        member = jnp.where((token_ids >= start) & (token_ids < stop), 1.0, 0.0)
        inside = jnp.where(slot_ids == slot, member, inside)
        start = stop
    position = (token_ids - begin).astype(jnp.float32)
    angle = position * frequencies(lax.broadcasted_iota(jnp.int32, (half_width, rows), 0), half_width)
    cosine, sine = jnp.cos(angle), jnp.sin(angle)
    rope = latents_ref[q_width + kv_width :, :].astype(jnp.float32)
    first, second = rope[:half_width], rope[half_width:]
    turned = jnp.concatenate([first * cosine - second * sine, second * cosine + first * sine, inside], axis=0)
    out_ref[:, q_width + kv_width :] = jnp.transpose(turned).astype(jnp.bfloat16)


def prepare(latents, gains, q_width, kv_width, slot_count, place):
    rows = latents.shape[0]
    rope_width = latents.shape[1] - q_width - kv_width
    width = q_width + kv_width + -(-(rope_width + slot_count) // 128) * 128
    vmem = pl.BlockSpec(memory_space=pltpu.VMEM)
    return pl.pallas_call(
        partial(prepare_kernel, q_width, kv_width, slot_count),
        out_shape=jax.ShapeDtypeStruct((rows, width), jnp.bfloat16),
        in_specs=[pl.BlockSpec(memory_space=pltpu.SMEM), vmem, vmem],
        out_specs=vmem,
        compiler_params=pltpu.CompilerParams(vmem_limit_bytes=VMEM_LIMIT),
        cost_estimate=LIGHT,
        name="prepare",
    )(place, jnp.transpose(latents), gains[None, :])


def pick_kernel(index_ref, source_ref, out_ref):
    out_ref[...] = source_ref[...]


def pick(source, index, block, axis):
    shape = list(source.shape)
    shape[axis] = block
    out_shape = shape
    position = lambda step, index_ref: tuple(index_ref[0] if at == axis else 0 for at in range(len(shape)))
    return pl.pallas_call(
        pick_kernel,
        grid_spec=pltpu.PrefetchScalarGridSpec(
            num_scalar_prefetch=1,
            grid=(1,),
            in_specs=[pl.BlockSpec(tuple(shape), position)],
            out_specs=pl.BlockSpec(tuple(out_shape), lambda step, index_ref: (0,) * len(out_shape)),
        ),
        out_shape=jax.ShapeDtypeStruct(tuple(out_shape), source.dtype),
        compiler_params=pltpu.CompilerParams(vmem_limit_bytes=VMEM_LIMIT),
        cost_estimate=LIGHT,
        name="pick",
    )(jnp.reshape(index, (1,)).astype(jnp.int32), source)


def project(tokens_ref, sizes, weight_refs, chosen):
    heads, q_width, kv_width, nope_width, rope_width, value_width = sizes
    query_width, pair_width = nope_width + rope_width, nope_width + value_width

    def dot(tokens, weight, dims):
        return lax.dot_general(tokens, weight, dims, preferred_element_type=jnp.float32)

    latent = tokens_ref[:, q_width : q_width + kv_width]
    query_ref, pair_ref = weight_refs
    columns = [slice(number * pair_width, (number + 1) * pair_width) for number in chosen]
    every = dot(latent, pair_ref[:, columns[0].start : columns[-1].stop], NN)
    pair = [every[:, head * pair_width : (head + 1) * pair_width] for head in range(heads)]

    def query(low, high, picked):
        parts = [query_ref[number if query_ref.shape[0] > 1 else 0, low:high, :] for number in picked]
        return dot(tokens_ref[:, :q_width], jnp.concatenate(parts, axis=0), NT)

    nope = [query(0, nope_width, chosen[head : head + 2]) for head in range(0, heads, 2)]
    picked = list(chosen)
    while len(picked) * rope_width % nope_width:
        picked.append(picked[-1])
    return nope, query(nope_width, query_width, picked), pair


def attend_group(sizes, chosen, tokens_ref, weight_refs, scratch, out_ref):
    heads, q_width, kv_width, nope_width, rope_width, value_width = sizes
    query_ref, key_ref, value_ref, turn_ref, bias_ref = scratch
    tokens = tokens_ref.shape[0]
    rows = bias_ref.shape[0]
    half_width = rope_width // 2
    score_scale = (nope_width + rope_width) ** -0.5 * math.log2(math.e)
    nope, rope, pair = project(tokens_ref, sizes, weight_refs, chosen)
    lane = lax.broadcasted_iota(jnp.int32, (tokens, nope_width), 1)
    is_first = lax.rem(lane, rope_width) < half_width
    is_rope = lane < rope_width
    shared = tokens_ref[:, q_width + kv_width :]
    apart = jnp.where(is_rope, 0.0, (1.0 - shared.astype(jnp.float32)) * FAR)
    for head in range(heads):
        low = head % 2 * nope_width
        part = nope[head // 2][:, low : low + nope_width]
        query_ref[:, 2 * head * nope_width : (2 * head + 1) * nope_width] = (part * score_scale).astype(jnp.bfloat16)
        both = pair[head].astype(jnp.bfloat16)
        key_ref[:, head * nope_width : (head + 1) * nope_width] = both[:, :nope_width]
        value_ref[head, :, :value_width] = both[:, nope_width:]
    group_heads = nope_width // rope_width
    for low in range(0, rope.shape[1], nope_width):
        part = rope[:, low : low + nope_width]
        swapped = jnp.where(is_first, pltpu.roll(part, nope_width - half_width, 1), pltpu.roll(part, half_width, 1))
        turned = (part * turn_ref[:, :nope_width] + swapped * turn_ref[:, nope_width:]) * score_scale
        for index in range(group_heads):
            head = low // rope_width + index
            if head < heads:
                moved = pltpu.roll(turned, nope_width - index * rope_width, 1) if index else turned
                query_ref[:, (2 * head + 1) * nope_width : (2 * head + 2) * nope_width] = jnp.where(
                    is_rope, moved, apart
                ).astype(jnp.bfloat16)
    for head in range(heads):
        for half in range(2):
            low, high = half * rows, (half + 1) * rows
            queries = query_ref[low:high, 2 * head * nope_width : (2 * head + 2) * nope_width]
            keys = jnp.concatenate(
                [key_ref[:high, head * nope_width : (head + 1) * nope_width], tokens_ref[:high, q_width + kv_width :]], axis=1
            )
            scores = lax.dot_general(queries, keys, NT, preferred_element_type=jnp.float32)
            last = scores[:, low:] + bias_ref[...]
            scores = jnp.concatenate([scores[:, :low], last], axis=1) if half else last
            terms = jnp.exp2(scores - jnp.max(scores, axis=1, keepdims=True)).astype(jnp.bfloat16)
            mixed = lax.dot_general(terms, value_ref[head, :high, :], NN, preferred_element_type=jnp.float32)
            out_ref[low:high, head * value_width : (head + 1) * value_width] = (
                mixed[:, :value_width] / mixed[:, value_width:]
            ).astype(jnp.bfloat16)


def set_up(scratch):
    value_ref, bias_ref = scratch[2], scratch[4]
    rows = bias_ref.shape[0]
    heads, tokens, width = value_ref.shape
    row_ids = lax.broadcasted_iota(jnp.int32, (rows, rows), 0)
    col_ids = lax.broadcasted_iota(jnp.int32, (rows, rows), 1)
    bias_ref[...] = jnp.where(col_ids <= row_ids, 0.0, -jnp.inf)
    for head in range(heads):
        value_ref[head, :, width // 2 :] = jnp.ones((tokens, width // 2), jnp.bfloat16)


def set_turn(group, slot_count, place_ref, table_ref, turn_ref):
    block = turn_ref.shape[0] // slot_count
    starts, start = [], jnp.int32(0)
    for index in range(slot_count):
        starts.append(start)
        start = start + place_ref[2 + group * slot_count + index]
    for index in range(slot_count):
        begin = jnp.int32(0)
        for entry in starts:
            begin = jnp.where(entry <= index * block, entry, begin)
        position = pl.multiple_of(index * block - begin, block)
        turn_ref[index * block : (index + 1) * block, :] = table_ref[pl.ds(position, block), :]


def near_kernel(sizes, slot_count, distance, place_ref, table_ref, query_weight_ref, pair_weight_ref, same_ref, other_ref, out_ref, tokens_ref, *scratch):
    core, group = place_ref[1], place_ref[0] ^ distance
    rows = same_ref.shape[0]
    tokens_ref[pl.ds(pl.multiple_of(core * rows, rows), rows), :] = same_ref[...]
    tokens_ref[pl.ds(pl.multiple_of((1 - core) * rows, rows), rows), :] = other_ref[...]
    set_up(scratch)
    set_turn(group, slot_count, place_ref, table_ref, scratch[3])
    attend_group(sizes, list(range(sizes[0])), tokens_ref, (query_weight_ref, pair_weight_ref), scratch, out_ref)


def far_kernel(sizes, slot_count, slots, chosen, place_ref, table_ref, *refs):
    weight_refs, refs = refs[:2], refs[2:]
    token_refs, out_refs, refs = refs[:slots], refs[slots : 2 * slots], refs[2 * slots :]
    held_ref, result_ref, sems = refs[0], refs[1], refs[2]
    scratch = refs[3:]
    set_up(scratch)

    def fetch(slot):
        for index in range(slots):

            @pl.when(slot == index)
            def _(index=index):
                pltpu.make_async_copy(token_refs[index], held_ref.at[index % 2], sems.at[index % 2]).start()

    fetch(0)

    def one_group(slot, carry):
        turn = lax.rem(slot, 2)
        fetch(slot + 1)
        set_turn(place_ref[0] ^ slot, slot_count, place_ref, table_ref, scratch[3])
        pltpu.make_async_copy(token_refs[0], held_ref.at[turn], sems.at[turn]).wait()
        attend_group(sizes, chosen, held_ref.at[turn], weight_refs, scratch, result_ref)
        for index in range(slots):

            @pl.when(slot == index)
            def _(index=index):
                out_refs[index][...] = result_ref[...]

        return carry

    lax.fori_loop(0, slots, one_group, 0)


def scratch_for(sizes, tokens):
    heads, q_width, kv_width, nope_width, rope_width, value_width = sizes
    return [
        pltpu.VMEM((tokens, 2 * heads * nope_width), jnp.bfloat16),
        pltpu.VMEM((tokens, heads * nope_width), jnp.bfloat16),
        pltpu.VMEM((heads, tokens, 2 * value_width), jnp.bfloat16),
        pltpu.VMEM((tokens, 2 * nope_width), jnp.float32),
        pltpu.VMEM((tokens // 2, tokens // 2), jnp.float32),
    ]


def attend_near(sizes, slot_count, distance, place, table, query_weight, pair_weight, same, other):
    rows, width = same.shape
    heads, value_width = sizes[0], sizes[-1]
    vmem = pl.BlockSpec(memory_space=pltpu.VMEM)
    return pl.pallas_call(
        partial(near_kernel, sizes, slot_count, distance),
        out_shape=[
            jax.ShapeDtypeStruct((2 * rows, heads * value_width), jnp.bfloat16),
            jax.ShapeDtypeStruct((2 * rows, width), jnp.bfloat16),
        ],
        in_specs=[pl.BlockSpec(memory_space=pltpu.SMEM)] + [vmem] * 5,
        out_specs=[vmem, vmem],
        scratch_shapes=scratch_for(sizes, 2 * rows),
        compiler_params=pltpu.CompilerParams(vmem_limit_bytes=VMEM_LIMIT),
        cost_estimate=LIGHT,
        name="attend_near",
    )(place, table, query_weight, pair_weight, same, other)


def attend_far(sizes, slot_count, place, table, query_weight, pair_weight, chosen, groups):
    tokens, width = groups[0].shape
    slots, heads, value_width = len(groups), sizes[0], sizes[-1]
    vmem = pl.BlockSpec(memory_space=pltpu.VMEM)
    return pl.pallas_call(
        partial(far_kernel, sizes, slot_count, slots, chosen),
        out_shape=[jax.ShapeDtypeStruct((tokens, heads * value_width), jnp.bfloat16)] * slots,
        in_specs=[pl.BlockSpec(memory_space=pltpu.SMEM)]
        + [vmem] * 3
        + [pl.BlockSpec(memory_space=pl.ANY)] * slots,
        out_specs=[vmem] * slots,
        scratch_shapes=[
            pltpu.VMEM((2, tokens, width), jnp.bfloat16),
            pltpu.VMEM((tokens, heads * value_width), jnp.bfloat16),
            pltpu.SemaphoreType.DMA((2,)),
        ]
        + scratch_for(sizes, tokens),
        compiler_params=pltpu.CompilerParams(vmem_limit_bytes=VMEM_LIMIT),
        cost_estimate=LIGHT,
        name="attend_far",
    )(place, table, query_weight, pair_weight, *groups)


def place_kernel(width, count, offsets_ref, *refs):
    pieces, out_ref, sems = refs[:count], refs[-2], refs[-1]
    copies = []
    for piece in pieces:
        for low in range(0, piece.shape[1], width):
            index = len(copies)
            columns = pl.ds(pl.multiple_of(offsets_ref[index], 128), width)
            copies.append(pltpu.make_async_copy(piece.at[:, low : low + width], out_ref.at[:, columns], sems.at[index]))
            copies[-1].start()
    for copy in copies:
        copy.wait()


def place_pieces(pieces, offsets, width, out_width, held=None):
    count = len(pieces)
    any_space = pl.BlockSpec(memory_space=pl.ANY)
    operands = [jnp.stack(offsets).astype(jnp.int32), *pieces]
    specs = [pl.BlockSpec(memory_space=pltpu.SMEM)] + [pl.BlockSpec(memory_space=pltpu.VMEM)] * count
    aliases = {}
    if held is not None:
        aliases = {len(operands): 0}
        operands.append(held)
        specs.append(any_space)
    return pl.pallas_call(
        partial(place_kernel, width, count),
        out_shape=jax.ShapeDtypeStruct((pieces[0].shape[0], out_width), pieces[0].dtype),
        in_specs=specs,
        out_specs=any_space,
        scratch_shapes=[pltpu.SemaphoreType.DMA((len(offsets),))],
        input_output_aliases=aliases,
        compiler_params=pltpu.CompilerParams(vmem_limit_bytes=VMEM_LIMIT),
        cost_estimate=LIGHT,
        name="place_pieces",
    )(*operands)


def after(value, *earlier):
    return lax.optimization_barrier((value, *earlier))[0]


def shards(latents, q_gain, kv_gain, q_weight, kv_weight, lengths):
    q_width, kv_width = q_gain.shape[0], kv_gain.shape[0]
    rope_width = latents.shape[1] - q_width - kv_width
    places = lax.axis_size("seq")
    parts = lax.axis_size("parts")
    half_places = places // 2
    place = lax.axis_index("seq")
    core = lax.axis_index("head")
    part = lax.axis_index("parts")
    tokens = 2 * latents.shape[0]
    local_heads = q_weight.shape[2]
    pair_width = kv_weight.shape[3]
    nope_width = q_weight.shape[3] - rope_width
    value_width = pair_width - nope_width
    block_width = local_heads * value_width
    sizes = (q_width, kv_width, nope_width, rope_width, value_width)

    def across(value, distance):
        return lax.ppermute(value, "seq", [(s, s ^ distance) for s in range(places)])

    def sibling(value):
        return lax.ppermute(value, "head", [(0, 1), (1, 0)])

    def other_part(value):
        return lax.ppermute(value, "parts", [(p, p ^ 1) for p in range(parts)])

    slot_count = lengths.shape[1]
    gains = jnp.concatenate([q_gain, kv_gain])
    spot = jnp.concatenate([jnp.stack([place, core]).astype(jnp.int32), jnp.reshape(lengths, -1)])
    own_query = jnp.transpose(q_weight[0], (1, 2, 0))
    own_pair = jnp.reshape(kv_weight[0], (kv_width, local_heads * pair_width))
    positions = jnp.arange(tokens, dtype=jnp.int32)[:, None].astype(jnp.float32)
    lanes = jnp.arange(nope_width, dtype=jnp.int32)[None, :]
    angles = positions * frequencies(lanes, rope_width // 2)
    signs = jnp.where(lax.rem(lanes, rope_width) < rope_width // 2, -1.0, 1.0)
    table = jnp.concatenate([jnp.cos(angles), jnp.sin(angles) * signs], axis=1)
    share = 2 if parts % 2 == 0 and local_heads % 2 == 0 else 1
    per_part = local_heads // share
    side = lax.rem(part, share)

    sent_pair = pick(own_pair, side, per_part * pair_width, 1)
    sent_query = pick(own_query, side, per_part, 0)
    latent = prepare(latents, gains, q_width, kv_width, slot_count, spot)
    same, other = [latent], [sibling(latent)]
    for distance in range(1, half_places):
        same.append(across(latent, distance) if distance & (distance - 1) == 0 else None)
    far_pair = across(sent_pair, half_places)
    far_query = across(sent_query, half_places)

    joined = []

    def near(distance, *earlier):
        mixed, tokens_joined = attend_near(
            (local_heads, *sizes),
            slot_count,
            distance,
            spot,
            table,
            own_query,
            own_pair,
            after(same[distance], *earlier),
            other[distance],
        )
        joined.append(tokens_joined)
        return mixed

    mixed = near(0)
    arrived = [mixed]
    direct = [entry for entry in same[1:] if entry is not None]
    for distance in range(1, half_places):
        if same[distance] is None:
            low_bit = distance & -distance
            same[distance] = across(after(same[distance ^ low_bit], mixed), low_bit)
            other.append(None)
        else:
            other.append(sibling(after(same[distance], mixed, far_pair, *direct)))
    crossed_pair = other_part(after(far_pair, mixed)) if share == 2 else None
    for distance in range(1, half_places):
        if other[distance] is None:
            other[distance] = sibling(after(same[distance], mixed, far_query))
        mixed = near(distance, mixed)
        arrived.append(across(mixed, distance))
    placed = []
    for distance in range(half_places):
        base = (place ^ distance) * block_width
        placed.append((arrived[distance], [base + head * value_width for head in range(local_heads)]))

    rounds = [(far_query, far_pair, list(range(per_part)), side * per_part)]
    crossed = []
    if share == 2:
        for index in range(per_part):
            crossed.append(other_part(after(far_query[index : index + 1], *crossed)))
            rounds.append((crossed[index], crossed_pair, [index], (1 - side) * per_part))
    previous, waiting = arrived[1:-1], arrived[-1:]
    for queries, pairs, chosen, first in rounds:
        mixed_all = attend_far(
            (len(chosen), *sizes), slot_count, after(spot, mixed, *previous), table, queries, pairs, chosen, joined
        )
        mixed = mixed_all[0]
        received = [across(mixed_all[distance], distance) for distance in range(1, half_places)]
        previous, waiting = waiting + received[:-1], received[-1:]
        for distance, piece in enumerate([mixed] + received):
            base = (place ^ distance ^ half_places) * block_width
            placed.append((piece, [base + (first + number) * value_width for number in chosen]))
    held, out_width = None, places * block_width
    late = len(placed) - half_places
    for batch in (placed[:late], placed[late:]):
        offsets = [offset for piece, starts in batch for offset in starts]
        held = place_pieces([piece for piece, starts in batch], offsets, value_width, out_width, held)
    return held


def solution(mesh):
    return jax.shard_map(
        shards,
        mesh=mesh,
        in_specs=(
            P(("parts", "seq", "head"), None),
            P(),
            P(),
            P("head", None, "seq", None),
            P("head", None, "seq", None),
            P("parts", None),
        ),
        out_specs=P(("parts", "seq"), "head"),
        check_vma=False,
    )
```

```python
from functools import partial
import math

import jax
import jax.numpy as jnp
from jax import lax
from jax.experimental import pallas as pl
from jax.experimental.pallas import tpu as pltpu
from jax.sharding import PartitionSpec as P

epsilon = 1e-06
VMEM_LIMIT = 32 * 1024 * 1024
LIGHT = pl.CostEstimate(flops=1024, bytes_accessed=1024, transcendentals=0)
FAR = -(2.0**100)
NT = (((1,), (1,)), ((), ()))
NN = (((1,), (0,)), ((), ()))


def frequencies(lane, half_width):
    steps = lax.rem(lane, half_width).astype(jnp.float32)
    return jnp.exp(steps * (-math.log(10000.0) / half_width))


def prepare_kernel(q_width, kv_width, slot_count, place_ref, latents_ref, gain_ref, out_ref):
    rows = latents_ref.shape[1]
    rope_width = latents_ref.shape[0] - q_width - kv_width
    half_width = rope_width // 2

    def normalized(low, width):
        part = latents_ref[low : low + width, :].astype(jnp.float32)
        scale = lax.rsqrt(jnp.mean(part * part, axis=0, keepdims=True) + epsilon)
        return (jnp.transpose(part * scale) * gain_ref[:, low : low + width]).astype(jnp.bfloat16)

    out_ref[:, :q_width] = normalized(0, q_width)
    out_ref[:, q_width : q_width + kv_width] = normalized(q_width, kv_width)
    spare = out_ref.shape[1] - q_width - kv_width - rope_width
    token_ids = lax.broadcasted_iota(jnp.int32, (1, rows), 1) + place_ref[1] * rows
    slot_ids = lax.broadcasted_iota(jnp.int32, (spare, rows), 0)
    begin, start, inside = jnp.zeros_like(token_ids), jnp.int32(0), jnp.zeros((spare, rows), jnp.float32)
    for slot in range(slot_count):
        stop = start + place_ref[2 + place_ref[0] * slot_count + slot]
        begin = jnp.where(token_ids >= start, start, begin)
        member = jnp.where((token_ids >= start) & (token_ids < stop), 1.0, 0.0)
        inside = jnp.where(slot_ids == slot, member, inside)
        start = stop
    position = (token_ids - begin).astype(jnp.float32)
    angle = position * frequencies(lax.broadcasted_iota(jnp.int32, (half_width, rows), 0), half_width)
    cosine, sine = jnp.cos(angle), jnp.sin(angle)
    rope = latents_ref[q_width + kv_width :, :].astype(jnp.float32)
    first, second = rope[:half_width], rope[half_width:]
    turned = jnp.concatenate([first * cosine - second * sine, second * cosine + first * sine, inside], axis=0)
    out_ref[:, q_width + kv_width :] = jnp.transpose(turned).astype(jnp.bfloat16)


def prepare(latents, gains, q_width, kv_width, slot_count, place):
    rows = latents.shape[0]
    rope_width = latents.shape[1] - q_width - kv_width
    width = q_width + kv_width + -(-(rope_width + slot_count) // 128) * 128
    vmem = pl.BlockSpec(memory_space=pltpu.VMEM)
    return pl.pallas_call(
        partial(prepare_kernel, q_width, kv_width, slot_count),
        out_shape=jax.ShapeDtypeStruct((rows, width), jnp.bfloat16),
        in_specs=[pl.BlockSpec(memory_space=pltpu.SMEM), vmem, vmem],
        out_specs=vmem,
        compiler_params=pltpu.CompilerParams(vmem_limit_bytes=VMEM_LIMIT),
        cost_estimate=LIGHT,
        name="prepare",
    )(place, jnp.transpose(latents), gains[None, :])


def pick_kernel(index_ref, source_ref, out_ref):
    out_ref[...] = source_ref[...]


def pick(source, index, block, axis):
    shape = list(source.shape)
    shape[axis] = block
    out_shape = shape
    position = lambda step, index_ref: tuple(index_ref[0] if at == axis else 0 for at in range(len(shape)))
    return pl.pallas_call(
        pick_kernel,
        grid_spec=pltpu.PrefetchScalarGridSpec(
            num_scalar_prefetch=1,
            grid=(1,),
            in_specs=[pl.BlockSpec(tuple(shape), position)],
            out_specs=pl.BlockSpec(tuple(out_shape), lambda step, index_ref: (0,) * len(out_shape)),
        ),
        out_shape=jax.ShapeDtypeStruct(tuple(out_shape), source.dtype),
        compiler_params=pltpu.CompilerParams(vmem_limit_bytes=VMEM_LIMIT),
        cost_estimate=LIGHT,
        name="pick",
    )(jnp.reshape(index, (1,)).astype(jnp.int32), source)


def attend_group(sizes, chosen, tokens_ref, weight_refs, scratch, out_ref):
    heads, q_width, kv_width, nope_width, rope_width, value_width = sizes
    query_width, pair_width = nope_width + rope_width, nope_width + value_width
    query_ref, key_ref, value_ref, turn_ref, bias_ref = scratch
    query_weight_ref, pair_weight_ref = weight_refs
    tokens = tokens_ref.shape[0]
    rows = bias_ref.shape[0]
    half_width = rope_width // 2
    group_heads = nope_width // rope_width
    score_scale = query_width**-0.5 * math.log2(math.e)
    lane = lax.broadcasted_iota(jnp.int32, (tokens, nope_width), 1)
    is_first = lax.rem(lane, rope_width) < half_width
    is_rope = lane < rope_width
    rope_low = q_width + kv_width
    apart = jnp.where(is_rope, 0.0, (1.0 - tokens_ref[:, rope_low:].astype(jnp.float32)) * FAR)

    def dot(left, right, dims):
        return lax.dot_general(left, right, dims, preferred_element_type=jnp.float32)

    def project(some):
        numbers = [chosen[head] for head in some]
        while len(numbers) < group_heads:
            numbers.append(numbers[-1])

        def query(low, high, picked):
            parts = [query_weight_ref[number, low:high, :] for number in picked]
            return dot(tokens_ref[:, :q_width], jnp.concatenate(parts, axis=0), NT)

        rope = query(nope_width, query_width, numbers)
        nope = query(0, nope_width, numbers[: len(some)])
        first, last = numbers[0] * pair_width, (numbers[len(some) - 1] + 1) * pair_width
        pair = dot(tokens_ref[:, q_width:rope_low], pair_weight_ref[:, first:last], NN)
        swapped = jnp.where(is_first, pltpu.roll(rope, nope_width - half_width, 1), pltpu.roll(rope, half_width, 1))
        turned = (rope * turn_ref[:, :nope_width] + swapped * turn_ref[:, nope_width:]) * score_scale
        for index, head in enumerate(some):
            low = 2 * head * nope_width
            part = nope[:, index * nope_width : (index + 1) * nope_width]
            query_ref[:, low : low + nope_width] = (part * score_scale).astype(jnp.bfloat16)
            moved = pltpu.roll(turned, nope_width - index * rope_width, 1) if index else turned
            query_ref[:, low + nope_width : low + 2 * nope_width] = jnp.where(is_rope, moved, apart).astype(jnp.bfloat16)
            both = pair[:, index * pair_width : (index + 1) * pair_width].astype(jnp.bfloat16)
            key_ref[:, head * nope_width : (head + 1) * nope_width] = both[:, :nope_width]
            value_ref[head, :, :value_width] = both[:, nope_width:]

    def score(head, half):
        low, high = half * rows, (half + 1) * rows
        queries = query_ref[low:high, 2 * head * nope_width : (2 * head + 2) * nope_width]
        shared = tokens_ref[:high, rope_low:]
        keys = jnp.concatenate([key_ref[:high, head * nope_width : (head + 1) * nope_width], shared], axis=1)
        return dot(queries, keys, NT)

    def soften(half, scores):
        low = half * rows
        last = scores[:, low:] + bias_ref[...]
        scores = jnp.concatenate([scores[:, :low], last], axis=1) if half else last
        return jnp.exp2(scores - jnp.max(scores, axis=1, keepdims=True)).astype(jnp.bfloat16)

    def mix(head, half, terms):
        low, high = half * rows, (half + 1) * rows
        mixed = dot(terms, value_ref[head, :high, :], NN)
        out_ref[low:high, head * value_width : (head + 1) * value_width] = (
            mixed[:, :value_width] / mixed[:, value_width:]
        ).astype(jnp.bfloat16)

    batches = [list(range(heads))[low : low + group_heads] for low in range(0, heads, group_heads)]
    project(batches[0])
    yield
    terms = None
    for number, batch in enumerate(batches):
        scores = score(batch[0], 0)
        if number + 1 < len(batches):
            project(batches[number + 1])
        else:
            yield
        for head in batch:
            for half in range(2):
                ahead = (head, 1) if half == 0 else (head + 1, 0)
                following = score(*ahead) if ahead[0] in batch else None
                held = soften(half, scores)
                if terms is not None:
                    mix(*terms)
                terms = (head, half, held)
                scores = following
    yield
    mix(*terms)


def attend_groups(works):
    works = list(works)
    for index, work in enumerate(works):
        if index == 0:
            next(work)
        next(work)
        if index + 1 < len(works):
            next(works[index + 1])
        for rest in work:
            pass


def set_up(scratch, first=True):
    value_ref, bias_ref = scratch[2], scratch[4]
    rows = bias_ref.shape[0]
    heads, tokens, width = value_ref.shape
    if first:
        row_ids = lax.broadcasted_iota(jnp.int32, (rows, rows), 0)
        col_ids = lax.broadcasted_iota(jnp.int32, (rows, rows), 1)
        bias_ref[...] = jnp.where(col_ids <= row_ids, 0.0, -jnp.inf)
    for head in range(heads):
        value_ref[head, :, width // 2 :] = jnp.ones((tokens, width // 2), jnp.bfloat16)


def set_turn(group, slot_count, place_ref, table_ref, turn_ref):
    block = turn_ref.shape[0] // slot_count
    starts, start = [], jnp.int32(0)
    for index in range(slot_count):
        starts.append(start)
        start = start + place_ref[2 + group * slot_count + index]
    for index in range(slot_count):
        begin = jnp.int32(0)
        for entry in starts:
            begin = jnp.where(entry <= index * block, entry, begin)
        position = pl.multiple_of(index * block - begin, block)
        turn_ref[index * block : (index + 1) * block, :] = table_ref[pl.ds(position, block), :]


def near_kernel(sizes, slot_count, distance, place_ref, table_ref, query_weight_ref, pair_weight_ref, same_ref, other_ref, out_ref, tokens_ref, *scratch):
    core, group = place_ref[1], place_ref[0] ^ distance
    rows = same_ref.shape[0]
    tokens_ref[pl.ds(pl.multiple_of(core * rows, rows), rows), :] = same_ref[...]
    tokens_ref[pl.ds(pl.multiple_of((1 - core) * rows, rows), rows), :] = other_ref[...]
    set_up(scratch)
    set_turn(group, slot_count, place_ref, table_ref, scratch[3])
    heads = list(range(sizes[0]))
    attend_groups([attend_group(sizes, heads, tokens_ref, (query_weight_ref, pair_weight_ref), scratch, out_ref)])


def far_kernel(sizes, slot_count, distances, chosen, place_ref, table_ref, *refs):
    slots = len(distances)
    weight_refs, refs = refs[:2], refs[2:]
    token_refs, out_refs, refs = refs[:slots], refs[slots : 2 * slots], refs[2 * slots :]
    bias_ref, refs = refs[0], refs[1:]
    works = []
    for slot in range(slots):
        scratch = [*refs[4 * slot : 4 * slot + 4], bias_ref]
        set_up(scratch, slot == 0)
        set_turn(place_ref[0] ^ distances[slot], slot_count, place_ref, table_ref, scratch[3])
        works.append(attend_group(sizes, chosen, token_refs[slot], weight_refs, scratch, out_refs[slot]))
    attend_groups(works)


def scratch_for(sizes, tokens):
    heads, q_width, kv_width, nope_width, rope_width, value_width = sizes
    return [
        pltpu.VMEM((tokens, 2 * heads * nope_width), jnp.bfloat16),
        pltpu.VMEM((tokens, heads * nope_width), jnp.bfloat16),
        pltpu.VMEM((heads, tokens, 2 * value_width), jnp.bfloat16),
        pltpu.VMEM((tokens, 2 * nope_width), jnp.float32),
        pltpu.VMEM((tokens // 2, tokens // 2), jnp.float32),
    ]


def attend_near(sizes, slot_count, distance, place, table, query_weight, pair_weight, same, other):
    rows, width = same.shape
    heads, value_width = sizes[0], sizes[-1]
    vmem = pl.BlockSpec(memory_space=pltpu.VMEM)
    return pl.pallas_call(
        partial(near_kernel, sizes, slot_count, distance),
        out_shape=[
            jax.ShapeDtypeStruct((2 * rows, heads * value_width), jnp.bfloat16),
            jax.ShapeDtypeStruct((2 * rows, width), jnp.bfloat16),
        ],
        in_specs=[pl.BlockSpec(memory_space=pltpu.SMEM)] + [vmem] * 5,
        out_specs=[vmem, vmem],
        scratch_shapes=scratch_for(sizes, 2 * rows),
        compiler_params=pltpu.CompilerParams(vmem_limit_bytes=VMEM_LIMIT),
        cost_estimate=LIGHT,
        name="attend_near",
    )(place, table, query_weight, pair_weight, same, other)


def attend_far(sizes, slot_count, distances, place, table, query_weight, pair_weight, chosen, groups):
    tokens = groups[0].shape[0]
    slots, heads, value_width = len(groups), sizes[0], sizes[-1]
    vmem = pl.BlockSpec(memory_space=pltpu.VMEM)
    own = scratch_for(sizes, tokens)
    return pl.pallas_call(
        partial(far_kernel, sizes, slot_count, distances, chosen),
        out_shape=[jax.ShapeDtypeStruct((tokens, heads * value_width), jnp.bfloat16)] * slots,
        in_specs=[pl.BlockSpec(memory_space=pltpu.SMEM)] + [vmem] * (3 + slots),
        out_specs=[vmem] * slots,
        scratch_shapes=own[4:] + own[:4] * slots,
        compiler_params=pltpu.CompilerParams(vmem_limit_bytes=VMEM_LIMIT),
        cost_estimate=LIGHT,
        name="attend_far",
    )(place, table, query_weight, pair_weight, *groups)


def place_kernel(width, count, offsets_ref, *refs):
    pieces, out_ref, sems = refs[:count], refs[-2], refs[-1]
    copies = []
    for piece in pieces:
        for low in range(0, piece.shape[1], width):
            index = len(copies)
            columns = pl.ds(pl.multiple_of(offsets_ref[index], 128), width)
            copies.append(pltpu.make_async_copy(piece.at[:, low : low + width], out_ref.at[:, columns], sems.at[index]))
            copies[-1].start()
    for copy in copies:
        copy.wait()


def place_pieces(pieces, offsets, width, out_width, held=None):
    count = len(pieces)
    any_space = pl.BlockSpec(memory_space=pl.ANY)
    operands = [jnp.stack(offsets).astype(jnp.int32), *pieces]
    specs = [pl.BlockSpec(memory_space=pltpu.SMEM)] + [pl.BlockSpec(memory_space=pltpu.VMEM)] * count
    aliases = {}
    if held is not None:
        aliases = {len(operands): 0}
        operands.append(held)
        specs.append(any_space)
    return pl.pallas_call(
        partial(place_kernel, width, count),
        out_shape=jax.ShapeDtypeStruct((pieces[0].shape[0], out_width), pieces[0].dtype),
        in_specs=specs,
        out_specs=any_space,
        scratch_shapes=[pltpu.SemaphoreType.DMA((len(offsets),))],
        input_output_aliases=aliases,
        compiler_params=pltpu.CompilerParams(vmem_limit_bytes=VMEM_LIMIT),
        cost_estimate=LIGHT,
        name="place_pieces",
    )(*operands)


def after(value, *earlier):
    return lax.optimization_barrier((value, *earlier))[0]


def shards(latents, q_gain, kv_gain, q_weight, kv_weight, lengths):
    q_width, kv_width = q_gain.shape[0], kv_gain.shape[0]
    rope_width = latents.shape[1] - q_width - kv_width
    places = lax.axis_size("seq")
    parts = lax.axis_size("parts")
    half_places = places // 2
    place = lax.axis_index("seq")
    core = lax.axis_index("head")
    part = lax.axis_index("parts")
    tokens = 2 * latents.shape[0]
    local_heads = q_weight.shape[2]
    pair_width = kv_weight.shape[3]
    nope_width = q_weight.shape[3] - rope_width
    value_width = pair_width - nope_width
    block_width = local_heads * value_width
    sizes = (q_width, kv_width, nope_width, rope_width, value_width)

    def across(value, distance):
        return lax.ppermute(value, "seq", [(s, s ^ distance) for s in range(places)])

    def sibling(value):
        return lax.ppermute(value, "head", [(0, 1), (1, 0)])

    def other_part(value):
        return lax.ppermute(value, "parts", [(p, p ^ 1) for p in range(parts)])

    slot_count = lengths.shape[1]
    gains = jnp.concatenate([q_gain, kv_gain])
    spot = jnp.concatenate([jnp.stack([place, core]).astype(jnp.int32), jnp.reshape(lengths, -1)])
    own_query = jnp.transpose(q_weight[0], (1, 2, 0))
    own_pair = jnp.reshape(kv_weight[0], (kv_width, local_heads * pair_width))
    positions = jnp.arange(tokens, dtype=jnp.int32)[:, None].astype(jnp.float32)
    lanes = jnp.arange(nope_width, dtype=jnp.int32)[None, :]
    angles = positions * frequencies(lanes, rope_width // 2)
    signs = jnp.where(lax.rem(lanes, rope_width) < rope_width // 2, -1.0, 1.0)
    table = jnp.concatenate([jnp.cos(angles), jnp.sin(angles) * signs], axis=1)
    share = 2 if parts % 2 == 0 and local_heads % 2 == 0 else 1
    per_part = local_heads // share
    side = lax.rem(part, share)

    sent_pair = pick(own_pair, side, per_part * pair_width, 1)
    sent_query = pick(own_query, side, per_part, 0)
    latent = prepare(latents, gains, q_width, kv_width, slot_count, spot)
    same, other = [latent], [sibling(latent)]
    for distance in range(1, half_places):
        same.append(across(latent, distance) if distance & (distance - 1) == 0 else None)
    far_pair = across(sent_pair, half_places)
    far_query = across(sent_query, half_places)

    joined = []

    def near(distance, *earlier):
        mixed, tokens_joined = attend_near(
            (local_heads, *sizes),
            slot_count,
            distance,
            spot,
            table,
            own_query,
            own_pair,
            after(same[distance], *earlier),
            other[distance],
        )
        joined.append(tokens_joined)
        return mixed

    mixed = near(0)
    arrived = [mixed]
    direct = [entry for entry in same[1:] if entry is not None]
    for distance in range(1, half_places):
        if same[distance] is None:
            low_bit = distance & -distance
            same[distance] = across(after(same[distance ^ low_bit], mixed), low_bit)
            other.append(None)
        else:
            other.append(sibling(after(same[distance], mixed, far_pair, *direct)))
    crossed_pair = [other_part(after(far_pair, mixed))] if share == 2 else []
    for distance in range(1, half_places):
        if other[distance] is None:
            other[distance] = sibling(after(same[distance], mixed, far_query, *crossed_pair))
        mixed = near(distance, mixed)
        arrived.append(across(mixed, distance))
    placed = []
    for distance in range(half_places):
        base = (place ^ distance) * block_width
        placed.append((arrived[distance], [base + head * value_width for head in range(local_heads)]))

    out_width = places * block_width

    def flush(held):
        offsets = [offset for piece, starts in placed for offset in starts]
        held = place_pieces([piece for piece, starts in placed], offsets, value_width, out_width, held)
        placed.clear()
        return held

    heads = list(range(per_part))
    rounds = [(far_query, far_pair, side * per_part)]
    if share == 2:
        rounds.append((other_part(far_query), crossed_pair[0], (1 - side) * per_part))
    gates, first_sent, late = [], [], []
    later = [arrived[1:-1], arrived[-1:], first_sent, []]
    for number, (queries, pairs, first) in enumerate(rounds):
        for distances in (list(range(1, half_places)), [0]):
            mixed_some = attend_far(
                (per_part, *sizes),
                slot_count,
                distances,
                after(spot, mixed, *gates),
                table,
                queries,
                pairs,
                heads,
                [joined[distance] for distance in distances],
            )
            mixed, gates = mixed_some[0], later.pop(0)
            for distance, piece in zip(distances, mixed_some):
                base = (place ^ distance ^ half_places) * block_width
                received = across(piece, distance) if distance else piece
                if number == 0 and distance:
                    first_sent.append(received)
                (late if number else placed).append((received, [base + (first + head) * value_width for head in heads]))
    held = flush(None)
    placed.extend(late)
    held = flush(held)
    return held


def solution(mesh):
    return jax.shard_map(
        shards,
        mesh=mesh,
        in_specs=(
            P(("parts", "seq", "head"), None),
            P(),
            P(),
            P("head", None, "seq", None),
            P("head", None, "seq", None),
            P("parts", None),
        ),
        out_specs=P(("parts", "seq"), "head"),
        check_vma=False,
    )
```

```python
from functools import partial
import math

import jax
import jax.numpy as jnp
from jax import lax
from jax.experimental import pallas as pl
from jax.experimental.pallas import tpu as pltpu
from jax.sharding import PartitionSpec as P

epsilon = 1e-06
VMEM_LIMIT = 32 * 1024 * 1024
VMEM_MOST = 60 * 1024 * 1024
LIGHT = pl.CostEstimate(flops=1024, bytes_accessed=1024, transcendentals=0)
FAR = -(2.0**100)
SCRATCH = 5
NT = (((1,), (1,)), ((), ()))
NN = (((1,), (0,)), ((), ()))


def frequencies(lane, half_width):
    steps = lax.rem(lane, half_width).astype(jnp.float32)
    return jnp.exp(steps * (-math.log(10000.0) / half_width))


def prepare_kernel(q_width, kv_width, place_ref, *refs):
    sources, out_ref, held, sems = refs[:4], refs[4], refs[5:9], refs[9]
    latents_ref, q_gain_ref, kv_gain_ref, lengths_ref = held
    copies = [pltpu.make_async_copy(*pair, sems.at[index]) for index, pair in enumerate(zip(sources, held))]
    for copy in copies:
        copy.start()
    for copy in copies:
        copy.wait()
    slot_count = lengths_ref.shape[1]
    rows = latents_ref.shape[1]
    rope_width = latents_ref.shape[0] - q_width - kv_width
    half_width = rope_width // 2

    def normalize(low, width, gain_ref):
        part = latents_ref[low : low + width, :].astype(jnp.float32)
        scale = lax.rsqrt(jnp.mean(part * part, axis=0, keepdims=True) + epsilon)
        normed = jnp.transpose(part * scale)
        lanes = gain_ref.shape[1]
        for index in range(gain_ref.shape[0]):
            span = slice(index * lanes, (index + 1) * lanes)
            out_ref[:, low + span.start : low + span.stop] = (normed[:, span] * gain_ref[index : index + 1, :]).astype(
                jnp.bfloat16
            )

    normalize(0, q_width, q_gain_ref)
    normalize(q_width, kv_width, kv_gain_ref)
    spare = out_ref.shape[1] - q_width - kv_width - rope_width
    token_ids = lax.broadcasted_iota(jnp.int32, (1, rows), 1) + place_ref[1] * rows
    slot_ids = lax.broadcasted_iota(jnp.int32, (spare, rows), 0)
    begin, start, inside = jnp.zeros_like(token_ids), jnp.int32(0), jnp.zeros((spare, rows), jnp.float32)
    for slot in range(slot_count):
        stop = start + lengths_ref[place_ref[0], slot]
        begin = jnp.where(token_ids >= start, start, begin)
        member = jnp.where((token_ids >= start) & (token_ids < stop), 1.0, 0.0)
        inside = jnp.where(slot_ids == slot, member, inside)
        start = stop
    position = (token_ids - begin).astype(jnp.float32)
    angle = position * frequencies(lax.broadcasted_iota(jnp.int32, (half_width, rows), 0), half_width)
    cosine, sine = jnp.cos(angle), jnp.sin(angle)
    rope = latents_ref[q_width + kv_width :, :].astype(jnp.float32)
    first, second = rope[:half_width], rope[half_width:]
    turned = jnp.concatenate([first * cosine - second * sine, second * cosine + first * sine, inside], axis=0)
    out_ref[:, q_width + kv_width :] = jnp.transpose(turned).astype(jnp.bfloat16)


def prepare(latents, q_gain, kv_gain, lengths, place):
    rows = latents.shape[0]
    q_width, kv_width = q_gain.shape[0], kv_gain.shape[0]
    rope_width = latents.shape[1] - q_width - kv_width
    width = q_width + kv_width + -(-(rope_width + lengths.shape[1]) // 128) * 128
    sources = [jnp.transpose(latents), jnp.reshape(q_gain, (-1, 128)), jnp.reshape(kv_gain, (-1, 128)), lengths]
    held = [pltpu.VMEM(source.shape, source.dtype) for source in sources[:3]] + [pltpu.SMEM(lengths.shape, lengths.dtype)]
    return pl.pallas_call(
        partial(prepare_kernel, q_width, kv_width),
        out_shape=jax.ShapeDtypeStruct((rows, width), jnp.bfloat16),
        in_specs=[pl.BlockSpec(memory_space=pltpu.SMEM)] + [pl.BlockSpec(memory_space=pl.ANY)] * len(sources),
        out_specs=pl.BlockSpec(memory_space=pltpu.VMEM),
        scratch_shapes=held + [pltpu.SemaphoreType.DMA((len(sources),))],
        compiler_params=pltpu.CompilerParams(vmem_limit_bytes=VMEM_MOST),
        cost_estimate=LIGHT,
        name="prepare",
    )(place, *sources)


def pick_kernel(index_ref, source_ref, out_ref):
    out_ref[...] = source_ref[...]


def pick(source, index, block, axis):
    shape = list(source.shape)
    shape[axis] = block
    out_shape = shape
    position = lambda step, index_ref: tuple(index_ref[0] if at == axis else 0 for at in range(len(shape)))
    return pl.pallas_call(
        pick_kernel,
        grid_spec=pltpu.PrefetchScalarGridSpec(
            num_scalar_prefetch=1,
            grid=(1,),
            in_specs=[pl.BlockSpec(tuple(shape), position)],
            out_specs=pl.BlockSpec(tuple(out_shape), lambda step, index_ref: (0,) * len(out_shape)),
        ),
        out_shape=jax.ShapeDtypeStruct(tuple(out_shape), source.dtype),
        compiler_params=pltpu.CompilerParams(vmem_limit_bytes=VMEM_LIMIT),
        cost_estimate=LIGHT,
        name="pick",
    )(jnp.reshape(index, (1,)).astype(jnp.int32), source)


def attend_group(sizes, chosen, tokens_ref, weight_refs, scratch, out_ref):
    heads, q_width, kv_width, nope_width, rope_width, value_width = sizes
    query_width, pair_width = nope_width + rope_width, nope_width + value_width
    query_ref, key_ref, value_ref, turn_ref, bias_ref = scratch
    query_weight_ref, pair_weight_ref = weight_refs
    tokens = tokens_ref.shape[0]
    rows = bias_ref.shape[0]
    half_width = rope_width // 2
    group_heads = nope_width // rope_width
    score_scale = query_width**-0.5 * math.log2(math.e)
    lane = lax.broadcasted_iota(jnp.int32, (tokens, nope_width), 1)
    is_first = lax.rem(lane, rope_width) < half_width
    is_rope = lane < rope_width
    rope_low = q_width + kv_width
    apart = jnp.where(is_rope, 0.0, (1.0 - tokens_ref[:, rope_low:].astype(jnp.float32)) * FAR)

    def dot(left, right, dims):
        return lax.dot_general(left, right, dims, preferred_element_type=jnp.float32)

    def project(some):
        numbers = [chosen[head] for head in some]
        while len(numbers) < group_heads:
            numbers.append(numbers[-1])

        def query(low, high, picked):
            parts = [query_weight_ref[number if query_weight_ref.shape[0] > 1 else 0, low:high, :] for number in picked]
            return dot(tokens_ref[:, :q_width], jnp.concatenate(parts, axis=0), NT)

        rope = query(nope_width, query_width, numbers)
        nope = query(0, nope_width, numbers[: len(some)])
        first, last = numbers[0] * pair_width, (numbers[len(some) - 1] + 1) * pair_width
        pair = dot(tokens_ref[:, q_width:rope_low], pair_weight_ref[:, first:last], NN)
        swapped = jnp.where(is_first, pltpu.roll(rope, nope_width - half_width, 1), pltpu.roll(rope, half_width, 1))
        turned = (rope * turn_ref[:, :nope_width] + swapped * turn_ref[:, nope_width:]) * score_scale
        for index, head in enumerate(some):
            low = 2 * head * nope_width
            part = nope[:, index * nope_width : (index + 1) * nope_width]
            query_ref[:, low : low + nope_width] = (part * score_scale).astype(jnp.bfloat16)
            moved = pltpu.roll(turned, nope_width - index * rope_width, 1) if index else turned
            query_ref[:, low + nope_width : low + 2 * nope_width] = jnp.where(is_rope, moved, apart).astype(jnp.bfloat16)
            both = pair[:, index * pair_width : (index + 1) * pair_width].astype(jnp.bfloat16)
            key_ref[:, head * nope_width : (head + 1) * nope_width] = both[:, :nope_width]
            value_ref[head, :, :value_width] = both[:, nope_width:]

    def score(head, half):
        low, high = half * rows, (half + 1) * rows
        queries = query_ref[low:high, 2 * head * nope_width : (2 * head + 2) * nope_width]
        shared = tokens_ref[:high, rope_low:]
        keys = jnp.concatenate([key_ref[:high, head * nope_width : (head + 1) * nope_width], shared], axis=1)
        return dot(queries, keys, NT)

    def soften(half, scores):
        low = half * rows
        last = scores[:, low:] + bias_ref[...]
        scores = jnp.concatenate([scores[:, :low], last], axis=1) if half else last
        return jnp.exp2(scores - jnp.max(scores, axis=1, keepdims=True)).astype(jnp.bfloat16)

    def mix(head, half, terms):
        low, high = half * rows, (half + 1) * rows
        mixed = dot(terms, value_ref[head, :high, :], NN)
        out_ref[low:high, head * value_width : (head + 1) * value_width] = (
            mixed[:, :value_width] / mixed[:, value_width:]
        ).astype(jnp.bfloat16)

    batches = [list(range(heads))[low : low + group_heads] for low in range(0, heads, group_heads)]
    project(batches[0])
    yield
    terms = None
    for number, batch in enumerate(batches):
        scores = score(batch[0], 0)
        if number + 1 < len(batches):
            project(batches[number + 1])
        else:
            yield
        for head in batch:
            for half in range(2):
                ahead = (head, 1) if half == 0 else (head + 1, 0)
                following = score(*ahead) if ahead[0] in batch else None
                held = soften(half, scores)
                if terms is not None:
                    mix(*terms)
                terms = (head, half, held)
                scores = following
    yield
    mix(*terms)


def attend_groups(works):
    works = list(works)
    for index, work in enumerate(works):
        if index == 0:
            next(work)
        next(work)
        if index + 1 < len(works):
            next(works[index + 1])
        for rest in work:
            pass


def set_up(scratch, first=True):
    value_ref, bias_ref = scratch[2], scratch[4]
    rows = bias_ref.shape[0]
    heads, tokens, width = value_ref.shape
    if first:
        row_ids = lax.broadcasted_iota(jnp.int32, (rows, rows), 0)
        col_ids = lax.broadcasted_iota(jnp.int32, (rows, rows), 1)
        bias_ref[...] = jnp.where(col_ids <= row_ids, 0.0, -jnp.inf)
    for head in range(heads):
        value_ref[head, :, width // 2 :] = jnp.ones((tokens, width // 2), jnp.bfloat16)


def set_turn(group, slot_count, place_ref, table_ref, turn_ref):
    block = turn_ref.shape[0] // slot_count
    starts, start = [], jnp.int32(0)
    for index in range(slot_count):
        starts.append(start)
        start = start + place_ref[2 + group * slot_count + index]
    for index in range(slot_count):
        begin = jnp.int32(0)
        for entry in starts:
            begin = jnp.where(entry <= index * block, entry, begin)
        position = pl.multiple_of(index * block - begin, block)
        turn_ref[index * block : (index + 1) * block, :] = table_ref[pl.ds(position, block), :]


def near_kernel(sizes, slot_count, distance, own, place_ref, table_ref, query_weight_ref, pair_weight_ref, *refs):
    count = len(refs) - 2 - SCRATCH
    piece_refs, out_ref, tokens_ref, scratch = refs[:count], refs[count], refs[count + 1], refs[count + 2 :]
    core, group = place_ref[1], place_ref[0] ^ distance
    half = tokens_ref.shape[0] // 2
    for owner, some in ((core, piece_refs[:own]), (1 - core, piece_refs[own:])):
        done = 0
        for piece_ref in some:
            rows = piece_ref.shape[0]
            tokens_ref[pl.ds(pl.multiple_of(owner * half + done, rows), rows), :] = piece_ref[...]
            done += rows
    set_up(scratch)
    set_turn(group, slot_count, place_ref, table_ref, scratch[3])
    heads = list(range(sizes[0]))
    attend_groups([attend_group(sizes, heads, tokens_ref, (query_weight_ref, pair_weight_ref), scratch, out_ref)])


def far_kernel(sizes, slot_count, distances, chosen, place_ref, table_ref, *refs):
    slots = len(distances)
    weight_refs, refs = refs[:2], refs[2:]
    token_refs, out_refs, refs = refs[:slots], refs[slots : 2 * slots], refs[2 * slots :]
    bias_ref, refs = refs[0], refs[1:]
    works = []
    for slot in range(slots):
        scratch = [*refs[4 * slot : 4 * slot + 4], bias_ref]
        set_up(scratch, slot == 0)
        set_turn(place_ref[0] ^ distances[slot], slot_count, place_ref, table_ref, scratch[3])
        works.append(attend_group(sizes, chosen, token_refs[slot], weight_refs, scratch, out_refs[slot]))
    attend_groups(works)


def scratch_for(sizes, tokens):
    heads, q_width, kv_width, nope_width, rope_width, value_width = sizes
    return [
        pltpu.VMEM((tokens, 2 * heads * nope_width), jnp.bfloat16),
        pltpu.VMEM((tokens, heads * nope_width), jnp.bfloat16),
        pltpu.VMEM((heads, tokens, 2 * value_width), jnp.bfloat16),
        pltpu.VMEM((tokens, 2 * nope_width), jnp.float32),
        pltpu.VMEM((tokens // 2, tokens // 2), jnp.float32),
    ]


def attend_near(sizes, slot_count, distance, place, table, query_weight, pair_weight, same, other):
    pieces = [*same, *other]
    tokens, width = sum(piece.shape[0] for piece in pieces), pieces[0].shape[1]
    heads, value_width = sizes[0], sizes[-1]
    vmem = pl.BlockSpec(memory_space=pltpu.VMEM)
    return pl.pallas_call(
        partial(near_kernel, sizes, slot_count, distance, len(same)),
        out_shape=[
            jax.ShapeDtypeStruct((tokens, heads * value_width), jnp.bfloat16),
            jax.ShapeDtypeStruct((tokens, width), jnp.bfloat16),
        ],
        in_specs=[pl.BlockSpec(memory_space=pltpu.SMEM)] + [vmem] * (3 + len(pieces)),
        out_specs=[vmem, vmem],
        scratch_shapes=scratch_for(sizes, tokens),
        compiler_params=pltpu.CompilerParams(vmem_limit_bytes=VMEM_LIMIT),
        cost_estimate=LIGHT,
        name="attend_near",
    )(place, table, query_weight, pair_weight, *pieces)


def attend_far(sizes, slot_count, distances, place, table, query_weight, pair_weight, chosen, groups):
    tokens = groups[0].shape[0]
    slots, heads, value_width = len(groups), sizes[0], sizes[-1]
    vmem = pl.BlockSpec(memory_space=pltpu.VMEM)
    own = scratch_for(sizes, tokens)
    return pl.pallas_call(
        partial(far_kernel, sizes, slot_count, distances, chosen),
        out_shape=[jax.ShapeDtypeStruct((tokens, heads * value_width), jnp.bfloat16)] * slots,
        in_specs=[pl.BlockSpec(memory_space=pltpu.SMEM)] + [vmem] * (3 + slots),
        out_specs=[vmem] * slots,
        scratch_shapes=own[4:] + own[:4] * slots,
        compiler_params=pltpu.CompilerParams(vmem_limit_bytes=VMEM_LIMIT),
        cost_estimate=LIGHT,
        name="attend_far",
    )(place, table, query_weight, pair_weight, *groups)


def place_kernel(width, count, offsets_ref, *refs):
    pieces, out_ref, sems = refs[:count], refs[-2], refs[-1]
    copies = []
    for piece in pieces:
        for low in range(0, piece.shape[1], width):
            index = len(copies)
            columns = pl.ds(pl.multiple_of(offsets_ref[index], 128), width)
            copies.append(pltpu.make_async_copy(piece.at[:, low : low + width], out_ref.at[:, columns], sems.at[index]))
            copies[-1].start()
    for copy in copies:
        copy.wait()


def place_pieces(pieces, offsets, width, out_width, held=None):
    count = len(pieces)
    any_space = pl.BlockSpec(memory_space=pl.ANY)
    operands = [jnp.stack(offsets).astype(jnp.int32), *pieces]
    specs = [pl.BlockSpec(memory_space=pltpu.SMEM)] + [pl.BlockSpec(memory_space=pltpu.VMEM)] * count
    aliases = {}
    if held is not None:
        aliases = {len(operands): 0}
        operands.append(held)
        specs.append(any_space)
    return pl.pallas_call(
        partial(place_kernel, width, count),
        out_shape=jax.ShapeDtypeStruct((pieces[0].shape[0], out_width), pieces[0].dtype),
        in_specs=specs,
        out_specs=any_space,
        scratch_shapes=[pltpu.SemaphoreType.DMA((len(offsets),))],
        input_output_aliases=aliases,
        compiler_params=pltpu.CompilerParams(vmem_limit_bytes=VMEM_LIMIT),
        cost_estimate=LIGHT,
        name="place_pieces",
    )(*operands)


def after(value, *earlier):
    return lax.optimization_barrier((value, *earlier))[0]


def shards(latents, q_gain, kv_gain, q_weight, kv_weight, lengths):
    q_width, kv_width = q_gain.shape[0], kv_gain.shape[0]
    rope_width = latents.shape[1] - q_width - kv_width
    places = lax.axis_size("seq")
    parts = lax.axis_size("parts")
    half_places = places // 2
    place = lax.axis_index("seq")
    core = lax.axis_index("head")
    part = lax.axis_index("parts")
    tokens = 2 * latents.shape[0]
    local_heads = q_weight.shape[2]
    pair_width = kv_weight.shape[3]
    nope_width = q_weight.shape[3] - rope_width
    value_width = pair_width - nope_width
    block_width = local_heads * value_width
    sizes = (q_width, kv_width, nope_width, rope_width, value_width)

    def across(value, distance):
        return lax.ppermute(value, "seq", [(s, s ^ distance) for s in range(places)])

    def sibling(value):
        return lax.ppermute(value, "head", [(0, 1), (1, 0)])

    def other_part(value):
        return lax.ppermute(value, "parts", [(p, p ^ 1) for p in range(parts)])

    slot_count = lengths.shape[1]
    spot = jnp.concatenate([jnp.stack([place, core]).astype(jnp.int32), jnp.reshape(lengths, -1)])
    own_query = jnp.transpose(q_weight[0], (1, 2, 0))
    own_pair = jnp.reshape(kv_weight[0], (kv_width, local_heads * pair_width))
    positions = jnp.arange(tokens, dtype=jnp.int32)[:, None].astype(jnp.float32)
    lanes = jnp.arange(nope_width, dtype=jnp.int32)[None, :]
    angles = positions * frequencies(lanes, rope_width // 2)
    signs = jnp.where(lax.rem(lanes, rope_width) < rope_width // 2, -1.0, 1.0)
    table = jnp.concatenate([jnp.cos(angles), jnp.sin(angles) * signs], axis=1)
    share = 2 if parts % 2 == 0 and local_heads % 2 == 0 else 1
    per_part = local_heads // share
    side = lax.rem(part, share)

    sent_pair = pick(own_pair, side, per_part * pair_width, 1)
    sent_query = pick(own_query, side, per_part, 0)
    latent = prepare(latents, q_gain, kv_gain, lengths, jnp.stack([place, core]).astype(jnp.int32))
    same, other = [latent], [[sibling(latent)]]
    for distance in range(1, half_places):
        same.append(across(latent, distance) if distance & (distance - 1) == 0 else None)
    far_pair = across(sent_pair, half_places)
    far_query = across(sent_query, half_places)

    joined = []

    def near(distance, *earlier):
        mixed, tokens_joined = attend_near(
            (local_heads, *sizes),
            slot_count,
            distance,
            after(spot, *earlier),
            table,
            own_query,
            own_pair,
            [same[distance]],
            other[distance],
        )
        joined.append(tokens_joined)
        return mixed

    mixed = near(0)
    arrived = [mixed]
    direct = [entry for entry in same[1:] if entry is not None]
    for distance in range(1, half_places):
        if same[distance] is None:
            low_bit = distance & -distance
            same[distance] = across(after(same[distance ^ low_bit], mixed), low_bit)
            other.append(None)
        else:
            half_rows = same[distance].shape[0] // 2
            piece = after(same[distance], mixed, far_pair, *direct)
            parted = [piece[:half_rows], piece[half_rows:]] if distance == half_places // 2 else [piece]
            other.append([sibling(piece) for piece in parted])
    crossed_pair = [other_part(after(far_pair, mixed))] if share == 2 else []
    for distance in range(1, half_places):
        if other[distance] is None:
            other[distance] = [sibling(after(same[distance], mixed, far_query, *crossed_pair, *arrived[half_places // 2 :]))]
        mixed = near(distance, mixed)
        arrived.append(across(mixed, distance))
    placed = []
    for distance in range(half_places):
        base = (place ^ distance) * block_width
        placed.append((arrived[distance], [base + head * value_width for head in range(local_heads)]))

    out_width = places * block_width

    def flush(held):
        offsets = [offset for piece, starts in placed for offset in starts]
        held = place_pieces([piece for piece, starts in placed], offsets, value_width, out_width, held)
        placed.clear()
        return held

    rounds = [(far_query, far_pair, list(range(per_part)), side * per_part)]
    if share == 2:
        crossed = other_part(far_query[:1])
        for index in range(per_part):
            rounds.append((crossed, crossed_pair[0], [index], (1 - side) * per_part))
    later = [[], arrived[1:-1], arrived[-1:]]
    late = []
    for number, (queries, pairs, heads, first) in enumerate(rounds):
        sent = []
        for distances in (list(range(1, half_places)), [0]):
            mixed_some = attend_far(
                (len(heads), *sizes),
                slot_count,
                distances,
                after(spot, mixed, *later.pop(0)),
                table,
                queries,
                pairs,
                heads,
                [joined[distance] for distance in distances],
            )
            mixed = mixed_some[0]
            for distance, piece in zip(distances, mixed_some):
                base = (place ^ distance ^ half_places) * block_width
                if distance:
                    piece = across(piece, distance)
                    sent.append(piece)
                spans = [base + (first + head) * value_width for head in heads]
                (late if number + 1 == len(rounds) else placed).append((piece, spans))
            if distances[0] and number + 1 < len(rounds) - 1:
                ahead = other_part(after(far_query[number + 1 : number + 2], rounds[number + 1][0], mixed))
                rounds[number + 2] = (ahead, *rounds[number + 2][1:])
        later += [sent, []]
    held = flush(None)
    placed.extend(late)
    held = flush(held)
    return held


def solution(mesh):
    return jax.shard_map(
        shards,
        mesh=mesh,
        in_specs=(
            P(("parts", "seq", "head"), None),
            P(),
            P(),
            P("head", None, "seq", None),
            P("head", None, "seq", None),
            P("parts", None),
        ),
        out_specs=P(("parts", "seq"), "head"),
        check_vma=False,
    )
```

```python
from functools import partial
import math

import jax
import jax.numpy as jnp
from jax import lax
from jax.experimental import pallas as pl
from jax.experimental.pallas import tpu as pltpu
from jax.sharding import PartitionSpec as P

epsilon = 1e-06
VMEM_LIMIT = 32 * 1024 * 1024
VMEM_NEAR = 44 * 1024 * 1024
LIGHT = pl.CostEstimate(flops=1024, bytes_accessed=1024, transcendentals=0)
FAR = -(2.0**100)
FETCHES = 4
NT = (((1,), (1,)), ((), ()))
NN = (((1,), (0,)), ((), ()))


def frequencies(lane, half_width):
    steps = lax.rem(lane, half_width).astype(jnp.float32)
    return jnp.exp(steps * (-math.log(10000.0) / half_width))


def prepare_kernel(q_width, kv_width, slot_count, place_ref, latents_ref, gain_ref, out_ref):
    rows = latents_ref.shape[1]
    rope_width = latents_ref.shape[0] - q_width - kv_width
    half_width = rope_width // 2

    def normalized(low, width):
        part = latents_ref[low : low + width, :].astype(jnp.float32)
        scale = lax.rsqrt(jnp.mean(part * part, axis=0, keepdims=True) + epsilon)
        return (jnp.transpose(part * scale) * gain_ref[:, low : low + width]).astype(jnp.bfloat16)

    out_ref[:, :q_width] = normalized(0, q_width)
    out_ref[:, q_width : q_width + kv_width] = normalized(q_width, kv_width)
    spare = out_ref.shape[1] - q_width - kv_width - rope_width
    token_ids = lax.broadcasted_iota(jnp.int32, (1, rows), 1) + place_ref[1] * rows
    slot_ids = lax.broadcasted_iota(jnp.int32, (spare, rows), 0)
    begin, start, inside = jnp.zeros_like(token_ids), jnp.int32(0), jnp.zeros((spare, rows), jnp.float32)
    for slot in range(slot_count):
        stop = start + place_ref[2 + place_ref[0] * slot_count + slot]
        begin = jnp.where(token_ids >= start, start, begin)
        member = jnp.where((token_ids >= start) & (token_ids < stop), 1.0, 0.0)
        inside = jnp.where(slot_ids == slot, member, inside)
        start = stop
    position = (token_ids - begin).astype(jnp.float32)
    angle = position * frequencies(lax.broadcasted_iota(jnp.int32, (half_width, rows), 0), half_width)
    cosine, sine = jnp.cos(angle), jnp.sin(angle)
    rope = latents_ref[q_width + kv_width :, :].astype(jnp.float32)
    first, second = rope[:half_width], rope[half_width:]
    turned = jnp.concatenate([first * cosine - second * sine, second * cosine + first * sine, inside], axis=0)
    out_ref[:, q_width + kv_width :] = jnp.transpose(turned).astype(jnp.bfloat16)


def prepare(latents, gains, q_width, kv_width, slot_count, place):
    rows = latents.shape[0]
    rope_width = latents.shape[1] - q_width - kv_width
    width = q_width + kv_width + -(-(rope_width + slot_count) // 128) * 128
    vmem = pl.BlockSpec(memory_space=pltpu.VMEM)
    return pl.pallas_call(
        partial(prepare_kernel, q_width, kv_width, slot_count),
        out_shape=jax.ShapeDtypeStruct((rows, width), jnp.bfloat16),
        in_specs=[pl.BlockSpec(memory_space=pltpu.SMEM), vmem, vmem],
        out_specs=vmem,
        compiler_params=pltpu.CompilerParams(vmem_limit_bytes=VMEM_LIMIT),
        cost_estimate=LIGHT,
        name="prepare",
    )(place, jnp.transpose(latents), gains[None, :])


def pack_kernel(head_ref, query_ref, pair_ref, *out_refs):
    query_rows, q_width = query_ref.shape[1:]
    kv_width, pair_width = pair_ref.shape
    slabs = [(out_ref, low) for out_ref in out_refs for low in range(0, out_ref.shape[0] - query_rows + 1, query_rows)]
    for slab in range(q_width // kv_width):
        out_ref, low = slabs[slab]
        out_ref[low : low + query_rows, :] = query_ref[0, :, slab * kv_width : (slab + 1) * kv_width]
    for fold in range(kv_width // pair_width):
        span = slice(fold * pair_width, (fold + 1) * pair_width)
        out_refs[-1][out_refs[-1].shape[0] - pair_width :, span] = pair_ref[span, :]


def pack(head, query_weight, pair_weight, pair_width, parted):
    query_rows, q_width = query_weight.shape[1:]
    kv_width = pair_weight.shape[0]
    slabs = q_width // kv_width
    rows = [query_rows * (slabs - 1), query_rows + pair_width] if parted else [query_rows * slabs + pair_width]
    return pl.pallas_call(
        pack_kernel,
        grid_spec=pltpu.PrefetchScalarGridSpec(
            num_scalar_prefetch=1,
            grid=(1,),
            in_specs=[
                pl.BlockSpec((1, query_rows, q_width), lambda step, head_ref: (head_ref[0], 0, 0)),
                pl.BlockSpec((kv_width, pair_width), lambda step, head_ref: (0, head_ref[0])),
            ],
            out_specs=[pl.BlockSpec((count, kv_width), lambda step, head_ref: (0, 0)) for count in rows],
        ),
        out_shape=[jax.ShapeDtypeStruct((count, kv_width), jnp.bfloat16) for count in rows],
        compiler_params=pltpu.CompilerParams(vmem_limit_bytes=VMEM_LIMIT),
        cost_estimate=LIGHT,
        name="pack",
    )(jnp.reshape(head, (1,)).astype(jnp.int32), query_weight, pair_weight)


def unpack(packed_refs, query_ref, pair_ref):
    query_rows, q_width = query_ref.shape[1:]
    kv_width = pair_ref.shape[0]
    heads = query_ref.shape[0]
    pair_width = pair_ref.shape[1] // heads
    each = len(packed_refs) // heads
    for head in range(heads):
        some = packed_refs[head * each : (head + 1) * each]
        slabs = [(ref, low) for ref in some for low in range(0, ref.shape[0] - query_rows + 1, query_rows)]
        for slab in range(q_width // kv_width):
            ref, low = slabs[slab]
            query_ref[head, :, slab * kv_width : (slab + 1) * kv_width] = ref[low : low + query_rows, :]
        for fold in range(kv_width // pair_width):
            span = slice(fold * pair_width, (fold + 1) * pair_width)
            pair_ref[span, head * pair_width : (head + 1) * pair_width] = some[-1][some[-1].shape[0] - pair_width :, span]


def attend_group(sizes, chosen, tokens_ref, weight_refs, scratch, out_ref, copies):
    heads, q_width, kv_width, nope_width, rope_width, value_width = sizes
    query_width, pair_width = nope_width + rope_width, nope_width + value_width
    query_ref, key_ref, value_ref, turn_ref, bias_ref = scratch
    query_weight_ref, pair_weight_ref = weight_refs
    tokens = tokens_ref.shape[0]
    rows = bias_ref.shape[0]
    half_width = rope_width // 2
    group_heads = nope_width // rope_width
    score_scale = query_width**-0.5 * math.log2(math.e)
    lane = lax.broadcasted_iota(jnp.int32, (tokens, nope_width), 1)
    is_first = lax.rem(lane, rope_width) < half_width
    is_rope = lane < rope_width
    rope_low = q_width + kv_width
    for copy in copies:
        copy.wait()
    apart = jnp.where(is_rope, 0.0, (1.0 - tokens_ref[:, rope_low:].astype(jnp.float32)) * FAR)

    def dot(left, right, dims):
        return lax.dot_general(left, right, dims, preferred_element_type=jnp.float32)

    def project(some):
        numbers = [chosen[head] for head in some]
        while len(numbers) < group_heads:
            numbers.append(numbers[-1])

        def query(low, high, picked):
            parts = [query_weight_ref[number, low:high, :] for number in picked]
            return dot(tokens_ref[:, :q_width], jnp.concatenate(parts, axis=0), NT)

        rope = query(nope_width, query_width, numbers)
        nope = query(0, nope_width, numbers[: len(some)])
        first, last = numbers[0] * pair_width, (numbers[len(some) - 1] + 1) * pair_width
        pair = dot(tokens_ref[:, q_width:rope_low], pair_weight_ref[:, first:last], NN)
        swapped = jnp.where(is_first, pltpu.roll(rope, nope_width - half_width, 1), pltpu.roll(rope, half_width, 1))
        turned = (rope * turn_ref[:, :nope_width] + swapped * turn_ref[:, nope_width:]) * score_scale
        for index, head in enumerate(some):
            low = 2 * head * nope_width
            part = nope[:, index * nope_width : (index + 1) * nope_width]
            query_ref[:, low : low + nope_width] = (part * score_scale).astype(jnp.bfloat16)
            moved = pltpu.roll(turned, nope_width - index * rope_width, 1) if index else turned
            query_ref[:, low + nope_width : low + 2 * nope_width] = jnp.where(is_rope, moved, apart).astype(jnp.bfloat16)
            both = pair[:, index * pair_width : (index + 1) * pair_width].astype(jnp.bfloat16)
            key_ref[:, head * nope_width : (head + 1) * nope_width] = both[:, :nope_width]
            value_ref[head, :, :value_width] = both[:, nope_width:]

    def score(head, half):
        low, high = half * rows, (half + 1) * rows
        queries = query_ref[low:high, 2 * head * nope_width : (2 * head + 2) * nope_width]
        shared = tokens_ref[:high, rope_low:]
        keys = jnp.concatenate([key_ref[:high, head * nope_width : (head + 1) * nope_width], shared], axis=1)
        return dot(queries, keys, NT)

    def soften(half, scores):
        low = half * rows
        last = scores[:, low:] + bias_ref[...]
        scores = jnp.concatenate([scores[:, :low], last], axis=1) if half else last
        return jnp.exp2(scores - jnp.max(scores, axis=1, keepdims=True)).astype(jnp.bfloat16)

    def mix(head, half, terms):
        low, high = half * rows, (half + 1) * rows
        mixed = dot(terms, value_ref[head, :high, :], NN)
        out_ref[low:high, head * value_width : (head + 1) * value_width] = (
            mixed[:, :value_width] / mixed[:, value_width:]
        ).astype(jnp.bfloat16)

    batches = [list(range(heads))[low : low + group_heads] for low in range(0, heads, group_heads)]
    project(batches[0])
    yield
    terms = None
    for number, batch in enumerate(batches):
        scores = score(batch[0], 0)
        if number + 1 < len(batches):
            project(batches[number + 1])
        else:
            yield
        for head in batch:
            for half in range(2):
                ahead = (head, 1) if half == 0 else (head + 1, 0)
                following = score(*ahead) if ahead[0] in batch else None
                held = soften(half, scores)
                if terms is not None:
                    mix(*terms)
                terms = (head, half, held)
                scores = following
    yield
    mix(*terms)


def attend_groups(works):
    works = list(works)
    for index, work in enumerate(works):
        if index == 0:
            next(work)
        next(work)
        if index + 1 < len(works):
            next(works[index + 1])
        for rest in work:
            pass


def set_up(scratch, first=True):
    value_ref, bias_ref = scratch[2], scratch[4]
    rows = bias_ref.shape[0]
    heads, tokens, width = value_ref.shape
    if first:
        row_ids = lax.broadcasted_iota(jnp.int32, (rows, rows), 0)
        col_ids = lax.broadcasted_iota(jnp.int32, (rows, rows), 1)
        bias_ref[...] = jnp.where(col_ids <= row_ids, 0.0, -jnp.inf)
    for head in range(heads):
        value_ref[head, :, width // 2 :] = jnp.ones((tokens, width // 2), jnp.bfloat16)


def set_turn(group, slot_count, place_ref, table_ref, turn_ref):
    block = turn_ref.shape[0] // slot_count
    starts, start = [], jnp.int32(0)
    for index in range(slot_count):
        starts.append(start)
        start = start + place_ref[2 + group * slot_count + index]
    for index in range(slot_count):
        begin = jnp.int32(0)
        for entry in starts:
            begin = jnp.where(entry <= index * block, entry, begin)
        position = pl.multiple_of(index * block - begin, block)
        turn_ref[index * block : (index + 1) * block, :] = table_ref[pl.ds(position, block), :]


def near_kernel(sizes, slot_count, distances, place_ref, table_ref, query_weight_ref, pair_weight_ref, groups_ref, *refs):
    slots = len(distances)
    out_refs, token_refs, sems, bias_ref = refs[:slots], refs[slots : 2 * slots], refs[2 * slots], refs[2 * slots + 1]
    refs = refs[2 * slots + 2 :]
    copies = []
    for slot, distance in enumerate(distances):
        source = groups_ref.at[lax.rem(place_ref[0] ^ distance, groups_ref.shape[0])]
        step = source.shape[0] // FETCHES
        copies.append([])
        for index in range(FETCHES):
            rows = pl.ds(index * step, step)
            copies[slot].append(pltpu.make_async_copy(source.at[rows], token_refs[slot].at[rows], sems.at[slot, index]))
            copies[slot][index].start()
    heads = list(range(sizes[0]))
    works = []
    for slot, distance in enumerate(distances):
        scratch = [*refs[4 * slot : 4 * slot + 4], bias_ref]
        set_up(scratch, slot == 0)
        set_turn(place_ref[0] ^ distance, slot_count, place_ref, table_ref, scratch[3])
        weights = (query_weight_ref, pair_weight_ref)
        works.append(attend_group(sizes, heads, token_refs[slot], weights, scratch, out_refs[slot], copies[slot]))
    attend_groups(works)


def far_kernel(sizes, slot_count, distances, count, place_ref, table_ref, *refs):
    slots, heads = len(distances), sizes[0]
    packed_refs, refs = refs[:count], refs[count:]
    token_refs, out_refs, refs = refs[:slots], refs[slots : 2 * slots], refs[2 * slots :]
    query_weight_ref, pair_weight_ref, bias_ref, refs = refs[0], refs[1], refs[2], refs[3:]
    unpack(packed_refs, query_weight_ref, pair_weight_ref)
    works = []
    for slot in range(slots):
        scratch = [*refs[4 * slot : 4 * slot + 4], bias_ref]
        set_up(scratch, slot == 0)
        set_turn(place_ref[0] ^ distances[slot], slot_count, place_ref, table_ref, scratch[3])
        weights = (query_weight_ref, pair_weight_ref)
        works.append(attend_group(sizes, list(range(heads)), token_refs[slot], weights, scratch, out_refs[slot], []))
    attend_groups(works)


def scratch_for(sizes, tokens):
    heads, q_width, kv_width, nope_width, rope_width, value_width = sizes
    return [
        pltpu.VMEM((tokens, 2 * heads * nope_width), jnp.bfloat16),
        pltpu.VMEM((tokens, heads * nope_width), jnp.bfloat16),
        pltpu.VMEM((heads, tokens, 2 * value_width), jnp.bfloat16),
        pltpu.VMEM((tokens, 2 * nope_width), jnp.float32),
        pltpu.VMEM((tokens // 2, tokens // 2), jnp.float32),
    ]


def attend_near(sizes, slot_count, distances, place, table, query_weight, pair_weight, groups):
    tokens, width = groups.shape[1:]
    slots, heads, value_width = len(distances), sizes[0], sizes[-1]
    vmem = pl.BlockSpec(memory_space=pltpu.VMEM)
    own = scratch_for(sizes, tokens)
    results = pl.pallas_call(
        partial(near_kernel, sizes, slot_count, distances),
        out_shape=[jax.ShapeDtypeStruct((tokens, heads * value_width), jnp.bfloat16)] * slots
        + [jax.ShapeDtypeStruct((tokens, width), jnp.bfloat16)] * slots,
        in_specs=[pl.BlockSpec(memory_space=pltpu.SMEM)] + [vmem] * 3 + [pl.BlockSpec(memory_space=pltpu.HBM)],
        out_specs=[vmem] * (2 * slots),
        scratch_shapes=[pltpu.SemaphoreType.DMA((slots, FETCHES))] + own[4:] + own[:4] * slots,
        compiler_params=pltpu.CompilerParams(vmem_limit_bytes=VMEM_NEAR),
        cost_estimate=LIGHT,
        name="attend_near",
    )(place, table, query_weight, pair_weight, groups)
    return results[:slots], results[slots:]


def attend_far(sizes, slot_count, distances, place, table, packed, groups):
    tokens = groups[0].shape[0]
    slots = len(groups)
    heads, q_width, kv_width, nope_width, rope_width, value_width = sizes
    vmem = pl.BlockSpec(memory_space=pltpu.VMEM)
    own = scratch_for(sizes, tokens)
    return pl.pallas_call(
        partial(far_kernel, sizes, slot_count, distances, len(packed)),
        out_shape=[jax.ShapeDtypeStruct((tokens, heads * value_width), jnp.bfloat16)] * slots,
        in_specs=[pl.BlockSpec(memory_space=pltpu.SMEM)] + [vmem] * (1 + len(packed) + slots),
        out_specs=[vmem] * slots,
        scratch_shapes=[
            pltpu.VMEM((heads, nope_width + rope_width, q_width), jnp.bfloat16),
            pltpu.VMEM((kv_width, heads * (nope_width + value_width)), jnp.bfloat16),
        ]
        + own[4:]
        + own[:4] * slots,
        compiler_params=pltpu.CompilerParams(vmem_limit_bytes=VMEM_LIMIT),
        cost_estimate=LIGHT,
        name="attend_far",
    )(place, table, *packed, *groups)


def place_kernel(width, count, offsets_ref, *refs):
    pieces, out_ref, sems = refs[:count], refs[-2], refs[-1]
    copies = []
    for piece in pieces:
        for low in range(0, piece.shape[1], width):
            index = len(copies)
            columns = pl.ds(pl.multiple_of(offsets_ref[index], 128), width)
            copies.append(pltpu.make_async_copy(piece.at[:, low : low + width], out_ref.at[:, columns], sems.at[index]))
            copies[-1].start()
    for copy in copies:
        copy.wait()


def place_pieces(pieces, offsets, width, out_width, held=None):
    count = len(pieces)
    any_space = pl.BlockSpec(memory_space=pl.ANY)
    operands = [jnp.stack(offsets).astype(jnp.int32), *pieces]
    specs = [pl.BlockSpec(memory_space=pltpu.SMEM)] + [pl.BlockSpec(memory_space=pltpu.VMEM)] * count
    aliases = {}
    if held is not None:
        aliases = {len(operands): 0}
        operands.append(held)
        specs.append(any_space)
    return pl.pallas_call(
        partial(place_kernel, width, count),
        out_shape=jax.ShapeDtypeStruct((pieces[0].shape[0], out_width), pieces[0].dtype),
        in_specs=specs,
        out_specs=any_space,
        scratch_shapes=[pltpu.SemaphoreType.DMA((len(offsets),))],
        input_output_aliases=aliases,
        compiler_params=pltpu.CompilerParams(vmem_limit_bytes=VMEM_LIMIT),
        cost_estimate=LIGHT,
        name="place_pieces",
    )(*operands)


def after(value, *earlier):
    return lax.optimization_barrier((value, *earlier))[0]


def shards(latents, q_gain, kv_gain, q_weight, kv_weight, lengths):
    q_width, kv_width = q_gain.shape[0], kv_gain.shape[0]
    rope_width = latents.shape[1] - q_width - kv_width
    half_places = lax.axis_size("quad")
    places = 2 * half_places
    parts = lax.axis_size("parts")
    place = lax.axis_index("half") * half_places + lax.axis_index("quad")
    core = lax.axis_index("head")
    part = lax.axis_index("parts")
    tokens = 2 * latents.shape[0]
    local_heads = q_weight.shape[2]
    pair_width = kv_weight.shape[3]
    nope_width = q_weight.shape[3] - rope_width
    value_width = pair_width - nope_width
    block_width = local_heads * value_width
    sizes = (q_width, kv_width, nope_width, rope_width, value_width)

    def across(value, distance):
        return lax.ppermute(value, "quad", [(s, s ^ distance) for s in range(half_places)])

    def opposite(value):
        return lax.ppermute(value, "half", [(0, 1), (1, 0)])

    def other_part(value):
        return lax.ppermute(value, "parts", [(p, p ^ 1) for p in range(parts)])

    slot_count = lengths.shape[1]
    gains = jnp.concatenate([q_gain, kv_gain])
    spot = jnp.concatenate([jnp.stack([place, core]).astype(jnp.int32), jnp.reshape(lengths, -1)])
    own_query = jnp.transpose(q_weight[0], (1, 2, 0))
    own_pair = jnp.reshape(kv_weight[0], (kv_width, local_heads * pair_width))
    positions = jnp.arange(tokens, dtype=jnp.int32)[:, None].astype(jnp.float32)
    lanes = jnp.arange(nope_width, dtype=jnp.int32)[None, :]
    angles = positions * frequencies(lanes, rope_width // 2)
    signs = jnp.where(lax.rem(lanes, rope_width) < rope_width // 2, -1.0, 1.0)
    table = jnp.concatenate([jnp.cos(angles), jnp.sin(angles) * signs], axis=1)
    share = 2 if parts % 2 == 0 and local_heads % 2 == 0 else 1
    per_part = local_heads // share
    side = lax.rem(part, share)

    latent = prepare(latents, gains, q_width, kv_width, slot_count, spot)
    sent = [pack(side * per_part + index, own_query, own_pair, pair_width, index > 0) for index in range(per_part)]
    groups = lax.all_gather(latent, ("quad", "head"), axis=0, tiled=True).reshape(half_places, tokens, latent.shape[1])
    far = [[opposite(piece) for piece in pieces] for pieces in sent]

    placed, joined, arrived = [], {}, {}
    orders = [[*range(half_places // 2, half_places), *range(1, half_places // 2)], [0]]
    mixed = None
    for distances in orders:
        results, fetched = attend_near(
            (local_heads, *sizes),
            slot_count,
            distances,
            spot if mixed is None else after(spot, mixed),
            table,
            own_query,
            own_pair,
            groups,
        )
        mixed = results[0]
        for distance, result, rows in zip(distances, results, fetched):
            joined[distance] = rows
            arrived[distance] = across(result, distance) if distance else result
            base = (place ^ distance) * block_width
            placed.append((arrived[distance], [base + head * value_width for head in range(local_heads)]))

    out_width = places * block_width

    def flush(held):
        offsets = [offset for piece, starts in placed for offset in starts]
        held = place_pieces([piece for piece, starts in placed], offsets, value_width, out_width, held)
        placed.clear()
        return held

    crossed = []
    for index, pieces in enumerate(far if share == 2 else []):
        crossed.append([other_part(after(piece, mixed) if index else piece) for piece in pieces])
    rounds = []
    for index in range(per_part):
        weights, numbers = [*far[index]], [side * per_part + index]
        if share == 2:
            weights.extend(crossed[index])
            numbers.append((1 - side) * per_part + index)
        rounds.append((weights, numbers))
    late, sent_before = [], []
    for number, (weights, numbers) in enumerate(rounds):
        last = number + 1 == len(rounds)
        sent_now = []
        for distances in (list(range(1, half_places)), [0]):
            gates = [arrived[distance] for distance in range(1, half_places - 1)] if last else []
            if distances == [0] and last:
                gates = [arrived[half_places - 1], *sent_before]
            mixed_some = attend_far(
                (len(numbers), *sizes),
                slot_count,
                distances,
                after(spot, mixed, *gates),
                table,
                weights,
                [joined[distance] for distance in distances],
            )
            mixed = mixed_some[0]
            for distance, piece in zip(distances, mixed_some):
                base = (place ^ distance ^ half_places) * block_width
                if distance:
                    piece = across(piece, distance)
                    sent_now.append(piece)
                (late if last else placed).append((piece, [base + head * value_width for head in numbers]))
        sent_before = sent_now
    held = flush(None)
    placed.extend(late)
    held = flush(held)
    return held


def solution(mesh):
    parts, places, cores = (mesh.shape[name] for name in ("parts", "seq", "head"))
    devices = mesh.devices.reshape(parts, 2, places // 2, cores)
    return jax.shard_map(
        shards,
        mesh=jax.sharding.Mesh(devices, ("parts", "half", "quad", "head")),
        in_specs=(
            P(("parts", "half", "quad", "head"), None),
            P(),
            P(),
            P("head", None, ("half", "quad"), None),
            P("head", None, ("half", "quad"), None),
            P("parts", None),
        ),
        out_specs=P(("parts", "half", "quad"), "head"),
        check_vma=False,
    )
```

```python
from functools import partial
import math

import jax
import jax.numpy as jnp
from jax import lax
from jax.experimental import pallas as pl
from jax.experimental.pallas import tpu as pltpu
from jax.sharding import PartitionSpec as P

epsilon = 1e-06
VMEM_LIMIT = 32 * 1024 * 1024
LIGHT = pl.CostEstimate(flops=1024, bytes_accessed=1024, transcendentals=0)
FAR = -(2.0**100)
NT = (((1,), (1,)), ((), ()))
NN = (((1,), (0,)), ((), ()))


def frequencies(lane, half_width):
    steps = lax.rem(lane, half_width).astype(jnp.float32)
    return jnp.exp(steps * (-math.log(10000.0) / half_width))


def prepare_kernel(q_width, kv_width, slot_count, place_ref, latents_ref, gain_ref, out_ref):
    rows = latents_ref.shape[1]
    rope_width = latents_ref.shape[0] - q_width - kv_width
    half_width = rope_width // 2

    def normalized(low, width):
        part = latents_ref[low : low + width, :].astype(jnp.float32)
        scale = lax.rsqrt(jnp.mean(part * part, axis=0, keepdims=True) + epsilon)
        return (jnp.transpose(part * scale) * gain_ref[:, low : low + width]).astype(jnp.bfloat16)

    out_ref[:, :q_width] = normalized(0, q_width)
    out_ref[:, q_width : q_width + kv_width] = normalized(q_width, kv_width)
    spare = out_ref.shape[1] - q_width - kv_width - rope_width
    token_ids = lax.broadcasted_iota(jnp.int32, (1, rows), 1) + place_ref[1] * rows
    slot_ids = lax.broadcasted_iota(jnp.int32, (spare, rows), 0)
    begin, start, inside = jnp.zeros_like(token_ids), jnp.int32(0), jnp.zeros((spare, rows), jnp.float32)
    for slot in range(slot_count):
        stop = start + place_ref[2 + place_ref[0] * slot_count + slot]
        begin = jnp.where(token_ids >= start, start, begin)
        member = jnp.where((token_ids >= start) & (token_ids < stop), 1.0, 0.0)
        inside = jnp.where(slot_ids == slot, member, inside)
        start = stop
    position = (token_ids - begin).astype(jnp.float32)
    angle = position * frequencies(lax.broadcasted_iota(jnp.int32, (half_width, rows), 0), half_width)
    cosine, sine = jnp.cos(angle), jnp.sin(angle)
    rope = latents_ref[q_width + kv_width :, :].astype(jnp.float32)
    first, second = rope[:half_width], rope[half_width:]
    turned = jnp.concatenate([first * cosine - second * sine, second * cosine + first * sine, inside], axis=0)
    out_ref[:, q_width + kv_width :] = jnp.transpose(turned).astype(jnp.bfloat16)


def prepare(latents, gains, q_width, kv_width, slot_count, place):
    rows = latents.shape[0]
    rope_width = latents.shape[1] - q_width - kv_width
    width = q_width + kv_width + -(-(rope_width + slot_count) // 128) * 128
    vmem = pl.BlockSpec(memory_space=pltpu.VMEM)
    return pl.pallas_call(
        partial(prepare_kernel, q_width, kv_width, slot_count),
        out_shape=jax.ShapeDtypeStruct((rows, width), jnp.bfloat16),
        in_specs=[pl.BlockSpec(memory_space=pltpu.SMEM), vmem, vmem],
        out_specs=vmem,
        compiler_params=pltpu.CompilerParams(vmem_limit_bytes=VMEM_LIMIT),
        cost_estimate=LIGHT,
        name="prepare",
    )(place, jnp.transpose(latents), gains[None, :])


def pick_kernel(index_ref, source_ref, out_ref):
    out_ref[...] = source_ref[...]


def pick(source, index, block, axis):
    shape = list(source.shape)
    shape[axis] = block
    out_shape = shape
    position = lambda step, index_ref: tuple(index_ref[0] if at == axis else 0 for at in range(len(shape)))
    return pl.pallas_call(
        pick_kernel,
        grid_spec=pltpu.PrefetchScalarGridSpec(
            num_scalar_prefetch=1,
            grid=(1,),
            in_specs=[pl.BlockSpec(tuple(shape), position)],
            out_specs=pl.BlockSpec(tuple(out_shape), lambda step, index_ref: (0,) * len(out_shape)),
        ),
        out_shape=jax.ShapeDtypeStruct(tuple(out_shape), source.dtype),
        compiler_params=pltpu.CompilerParams(vmem_limit_bytes=VMEM_LIMIT),
        cost_estimate=LIGHT,
        name="pick",
    )(jnp.reshape(index, (1,)).astype(jnp.int32), source)


def attend_group(sizes, chosen, tokens_ref, weight_refs, scratch, out_ref):
    heads, q_width, kv_width, nope_width, rope_width, value_width = sizes
    query_width, pair_width = nope_width + rope_width, nope_width + value_width
    query_ref, key_ref, value_ref, turn_ref, bias_ref = scratch
    query_weight_ref, pair_weight_ref = weight_refs
    tokens = tokens_ref.shape[0]
    rows = bias_ref.shape[0]
    half_width = rope_width // 2
    group_heads = nope_width // rope_width
    score_scale = query_width**-0.5 * math.log2(math.e)
    lane = lax.broadcasted_iota(jnp.int32, (tokens, nope_width), 1)
    is_first = lax.rem(lane, rope_width) < half_width
    is_rope = lane < rope_width
    rope_low = q_width + kv_width
    apart = jnp.where(is_rope, 0.0, (1.0 - tokens_ref[:, rope_low:].astype(jnp.float32)) * FAR)

    def dot(left, right, dims):
        return lax.dot_general(left, right, dims, preferred_element_type=jnp.float32)

    def project(some):
        numbers = [chosen[head] for head in some]
        while len(numbers) < group_heads:
            numbers.append(numbers[-1])

        def query(low, high, picked):
            parts = [query_weight_ref[number, low:high, :] for number in picked]
            return dot(tokens_ref[:, :q_width], jnp.concatenate(parts, axis=0), NT)

        rope = query(nope_width, query_width, numbers)
        nope = query(0, nope_width, numbers[: len(some)])
        first, last = numbers[0] * pair_width, (numbers[len(some) - 1] + 1) * pair_width
        pair = dot(tokens_ref[:, q_width:rope_low], pair_weight_ref[:, first:last], NN)
        swapped = jnp.where(is_first, pltpu.roll(rope, nope_width - half_width, 1), pltpu.roll(rope, half_width, 1))
        turned = (rope * turn_ref[:, :nope_width] + swapped * turn_ref[:, nope_width:]) * score_scale
        for index, head in enumerate(some):
            low = 2 * head * nope_width
            part = nope[:, index * nope_width : (index + 1) * nope_width]
            query_ref[:, low : low + nope_width] = (part * score_scale).astype(jnp.bfloat16)
            moved = pltpu.roll(turned, nope_width - index * rope_width, 1) if index else turned
            query_ref[:, low + nope_width : low + 2 * nope_width] = jnp.where(is_rope, moved, apart).astype(jnp.bfloat16)
            both = pair[:, index * pair_width : (index + 1) * pair_width].astype(jnp.bfloat16)
            key_ref[:, head * nope_width : (head + 1) * nope_width] = both[:, :nope_width]
            value_ref[head, :, :value_width] = both[:, nope_width:]

    def score(head, half):
        low, high = half * rows, (half + 1) * rows
        queries = query_ref[low:high, 2 * head * nope_width : (2 * head + 2) * nope_width]
        shared = tokens_ref[:high, rope_low:]
        keys = jnp.concatenate([key_ref[:high, head * nope_width : (head + 1) * nope_width], shared], axis=1)
        return dot(queries, keys, NT)

    def soften(half, scores):
        low = half * rows
        last = scores[:, low:] + bias_ref[...]
        scores = jnp.concatenate([scores[:, :low], last], axis=1) if half else last
        return jnp.exp2(scores - jnp.max(scores, axis=1, keepdims=True)).astype(jnp.bfloat16)

    def mix(head, half, terms):
        low, high = half * rows, (half + 1) * rows
        mixed = dot(terms, value_ref[head, :high, :], NN)
        out_ref[low:high, head * value_width : (head + 1) * value_width] = (
            mixed[:, :value_width] / mixed[:, value_width:]
        ).astype(jnp.bfloat16)

    batches = [list(range(heads))[low : low + group_heads] for low in range(0, heads, group_heads)]
    project(batches[0])
    yield
    terms = None
    for number, batch in enumerate(batches):
        scores = score(batch[0], 0)
        if number + 1 < len(batches):
            project(batches[number + 1])
        else:
            yield
        for head in batch:
            for half in range(2):
                ahead = (head, 1) if half == 0 else (head + 1, 0)
                following = score(*ahead) if ahead[0] in batch else None
                held = soften(half, scores)
                if terms is not None:
                    mix(*terms)
                terms = (head, half, held)
                scores = following
    yield
    mix(*terms)


def attend_groups(works):
    works = list(works)
    for index, work in enumerate(works):
        if index == 0:
            next(work)
        next(work)
        if index + 1 < len(works):
            next(works[index + 1])
        for rest in work:
            pass


def set_up(scratch, first=True):
    value_ref, bias_ref = scratch[2], scratch[4]
    rows = bias_ref.shape[0]
    heads, tokens, width = value_ref.shape
    if first:
        row_ids = lax.broadcasted_iota(jnp.int32, (rows, rows), 0)
        col_ids = lax.broadcasted_iota(jnp.int32, (rows, rows), 1)
        bias_ref[...] = jnp.where(col_ids <= row_ids, 0.0, -jnp.inf)
    for head in range(heads):
        value_ref[head, :, width // 2 :] = jnp.ones((tokens, width // 2), jnp.bfloat16)


def set_turn(group, slot_count, place_ref, table_ref, turn_ref):
    block = turn_ref.shape[0] // slot_count
    starts, start = [], jnp.int32(0)
    for index in range(slot_count):
        starts.append(start)
        start = start + place_ref[2 + group * slot_count + index]
    for index in range(slot_count):
        begin = jnp.int32(0)
        for entry in starts:
            begin = jnp.where(entry <= index * block, entry, begin)
        position = pl.multiple_of(index * block - begin, block)
        turn_ref[index * block : (index + 1) * block, :] = table_ref[pl.ds(position, block), :]


def near_kernel(sizes, slot_count, distance, place_ref, table_ref, query_weight_ref, pair_weight_ref, same_ref, other_ref, out_ref, tokens_ref, *scratch):
    core, group = place_ref[1], place_ref[0] ^ distance
    rows = same_ref.shape[0]
    tokens_ref[pl.ds(pl.multiple_of(core * rows, rows), rows), :] = same_ref[...]
    tokens_ref[pl.ds(pl.multiple_of((1 - core) * rows, rows), rows), :] = other_ref[...]
    set_up(scratch)
    set_turn(group, slot_count, place_ref, table_ref, scratch[3])
    heads = list(range(sizes[0]))
    attend_groups([attend_group(sizes, heads, tokens_ref, (query_weight_ref, pair_weight_ref), scratch, out_ref)])


def far_kernel(sizes, slot_count, distances, chosen, place_ref, table_ref, *refs):
    slots = len(distances)
    weight_refs, refs = refs[:2], refs[2:]
    token_refs, out_refs, refs = refs[:slots], refs[slots : 2 * slots], refs[2 * slots :]
    bias_ref, refs = refs[0], refs[1:]
    works = []
    for slot in range(slots):
        scratch = [*refs[4 * slot : 4 * slot + 4], bias_ref]
        set_up(scratch, slot == 0)
        set_turn(place_ref[0] ^ distances[slot], slot_count, place_ref, table_ref, scratch[3])
        works.append(attend_group(sizes, chosen, token_refs[slot], weight_refs, scratch, out_refs[slot]))
    attend_groups(works)


def scratch_for(sizes, tokens):
    heads, q_width, kv_width, nope_width, rope_width, value_width = sizes
    return [
        pltpu.VMEM((tokens, 2 * heads * nope_width), jnp.bfloat16),
        pltpu.VMEM((tokens, heads * nope_width), jnp.bfloat16),
        pltpu.VMEM((heads, tokens, 2 * value_width), jnp.bfloat16),
        pltpu.VMEM((tokens, 2 * nope_width), jnp.float32),
        pltpu.VMEM((tokens // 2, tokens // 2), jnp.float32),
    ]


def attend_near(sizes, slot_count, distance, place, table, query_weight, pair_weight, same, other):
    rows, width = same.shape
    heads, value_width = sizes[0], sizes[-1]
    vmem = pl.BlockSpec(memory_space=pltpu.VMEM)
    return pl.pallas_call(
        partial(near_kernel, sizes, slot_count, distance),
        out_shape=[
            jax.ShapeDtypeStruct((2 * rows, heads * value_width), jnp.bfloat16),
            jax.ShapeDtypeStruct((2 * rows, width), jnp.bfloat16),
        ],
        in_specs=[pl.BlockSpec(memory_space=pltpu.SMEM)] + [vmem] * 5,
        out_specs=[vmem, vmem],
        scratch_shapes=scratch_for(sizes, 2 * rows),
        compiler_params=pltpu.CompilerParams(vmem_limit_bytes=VMEM_LIMIT),
        cost_estimate=LIGHT,
        name="attend_near",
    )(place, table, query_weight, pair_weight, same, other)


def attend_far(sizes, slot_count, distances, place, table, query_weight, pair_weight, chosen, groups):
    tokens = groups[0].shape[0]
    slots, heads, value_width = len(groups), sizes[0], sizes[-1]
    vmem = pl.BlockSpec(memory_space=pltpu.VMEM)
    own = scratch_for(sizes, tokens)
    return pl.pallas_call(
        partial(far_kernel, sizes, slot_count, distances, chosen),
        out_shape=[jax.ShapeDtypeStruct((tokens, heads * value_width), jnp.bfloat16)] * slots,
        in_specs=[pl.BlockSpec(memory_space=pltpu.SMEM)] + [vmem] * (3 + slots),
        out_specs=[vmem] * slots,
        scratch_shapes=own[4:] + own[:4] * slots,
        compiler_params=pltpu.CompilerParams(vmem_limit_bytes=VMEM_LIMIT),
        cost_estimate=LIGHT,
        name="attend_far",
    )(place, table, query_weight, pair_weight, *groups)


def place_kernel(width, count, offsets_ref, *refs):
    pieces, out_ref, sems = refs[:count], refs[-2], refs[-1]
    copies = []
    for piece in pieces:
        for low in range(0, piece.shape[1], width):
            index = len(copies)
            columns = pl.ds(pl.multiple_of(offsets_ref[index], 128), width)
            copies.append(pltpu.make_async_copy(piece.at[:, low : low + width], out_ref.at[:, columns], sems.at[index]))
            copies[-1].start()
    for copy in copies:
        copy.wait()


def place_pieces(pieces, offsets, width, out_width, held=None):
    count = len(pieces)
    any_space = pl.BlockSpec(memory_space=pl.ANY)
    operands = [jnp.stack(offsets).astype(jnp.int32), *pieces]
    specs = [pl.BlockSpec(memory_space=pltpu.SMEM)] + [pl.BlockSpec(memory_space=pltpu.VMEM)] * count
    aliases = {}
    if held is not None:
        aliases = {len(operands): 0}
        operands.append(held)
        specs.append(any_space)
    return pl.pallas_call(
        partial(place_kernel, width, count),
        out_shape=jax.ShapeDtypeStruct((pieces[0].shape[0], out_width), pieces[0].dtype),
        in_specs=specs,
        out_specs=any_space,
        scratch_shapes=[pltpu.SemaphoreType.DMA((len(offsets),))],
        input_output_aliases=aliases,
        compiler_params=pltpu.CompilerParams(vmem_limit_bytes=VMEM_LIMIT),
        cost_estimate=LIGHT,
        name="place_pieces",
    )(*operands)


def after(value, *earlier):
    return lax.optimization_barrier((value, *earlier))[0]


def shards(latents, q_gain, kv_gain, q_weight, kv_weight, lengths):
    q_width, kv_width = q_gain.shape[0], kv_gain.shape[0]
    rope_width = latents.shape[1] - q_width - kv_width
    places = lax.axis_size("seq")
    parts = lax.axis_size("parts")
    half_places = places // 2
    place = lax.axis_index("seq")
    core = lax.axis_index("head")
    part = lax.axis_index("parts")
    tokens = 2 * latents.shape[0]
    local_heads = q_weight.shape[2]
    pair_width = kv_weight.shape[3]
    nope_width = q_weight.shape[3] - rope_width
    value_width = pair_width - nope_width
    block_width = local_heads * value_width
    sizes = (q_width, kv_width, nope_width, rope_width, value_width)

    def across(value, distance):
        return lax.ppermute(value, "seq", [(s, s ^ distance) for s in range(places)])

    def sibling(value):
        return lax.ppermute(value, "head", [(0, 1), (1, 0)])

    def other_part(value):
        return lax.ppermute(value, "parts", [(p, p ^ 1) for p in range(parts)])

    slot_count = lengths.shape[1]
    gains = jnp.concatenate([q_gain, kv_gain])
    spot = jnp.concatenate([jnp.stack([place, core]).astype(jnp.int32), jnp.reshape(lengths, -1)])
    own_query = jnp.transpose(q_weight[0], (1, 2, 0))
    own_pair = jnp.reshape(kv_weight[0], (kv_width, local_heads * pair_width))
    positions = jnp.arange(tokens, dtype=jnp.int32)[:, None].astype(jnp.float32)
    lanes = jnp.arange(nope_width, dtype=jnp.int32)[None, :]
    angles = positions * frequencies(lanes, rope_width // 2)
    signs = jnp.where(lax.rem(lanes, rope_width) < rope_width // 2, -1.0, 1.0)
    table = jnp.concatenate([jnp.cos(angles), jnp.sin(angles) * signs], axis=1)
    share = 2 if parts % 2 == 0 and local_heads % 2 == 0 else 1
    per_part = local_heads // share
    side = lax.rem(part, share)

    sent_pair = pick(own_pair, side, per_part * pair_width, 1)
    sent_query = pick(own_query, side, per_part, 0)
    latent = prepare(latents, gains, q_width, kv_width, slot_count, spot)
    same, other = [latent], [sibling(latent)]
    for distance in range(1, half_places):
        same.append(across(latent, distance) if distance & (distance - 1) == 0 else None)
    far_query = across(sent_query, half_places)
    far_pair = across(after(sent_pair, far_query), half_places)

    joined = []

    def near(distance, *earlier):
        mixed, tokens_joined = attend_near(
            (local_heads, *sizes),
            slot_count,
            distance,
            spot,
            table,
            own_query,
            own_pair,
            after(same[distance], *earlier),
            other[distance],
        )
        joined.append(tokens_joined)
        return mixed

    mixed = near(0)
    arrived = [mixed]
    direct = [entry for entry in same[1:] if entry is not None]
    for distance in range(1, half_places):
        if same[distance] is None:
            low_bit = distance & -distance
            same[distance] = across(after(same[distance ^ low_bit], mixed), low_bit)
            other.append(None)
        else:
            other.append(sibling(after(same[distance], mixed, far_query, *direct)))
    crossed_query = [other_part(after(far_query, mixed))] if share == 2 else []
    for distance in range(1, half_places):
        if other[distance] is None:
            other[distance] = sibling(after(same[distance], mixed, far_pair, *crossed_query))
        mixed = near(distance, mixed)
        arrived.append(across(mixed, distance))
    placed = []
    for distance in range(half_places):
        base = (place ^ distance) * block_width
        placed.append((arrived[distance], [base + head * value_width for head in range(local_heads)]))

    out_width = places * block_width

    def flush(held):
        offsets = [offset for piece, starts in placed for offset in starts]
        held = place_pieces([piece for piece, starts in placed], offsets, value_width, out_width, held)
        placed.clear()
        return held

    heads = list(range(per_part))
    rounds = [(far_query, far_pair, side * per_part)]
    if share == 2:
        rounds.append((crossed_query[0], other_part(far_pair), (1 - side) * per_part))
    gates, first_sent, late = [], [], []
    later = [arrived[1:-1], arrived[-1:], first_sent, []]
    for number, (queries, pairs, first) in enumerate(rounds):
        for distances in (list(range(1, half_places)), [0]):
            mixed_some = attend_far(
                (per_part, *sizes),
                slot_count,
                distances,
                after(spot, mixed, *gates),
                table,
                queries,
                pairs,
                heads,
                [joined[distance] for distance in distances],
            )
            mixed, gates = mixed_some[0], later.pop(0)
            for distance, piece in zip(distances, mixed_some):
                base = (place ^ distance ^ half_places) * block_width
                received = across(piece, distance) if distance else piece
                if number == 0 and distance:
                    first_sent.append(received)
                (late if number else placed).append((received, [base + (first + head) * value_width for head in heads]))
    held = flush(None)
    placed.extend(late)
    held = flush(held)
    return held


def solution(mesh):
    return jax.shard_map(
        shards,
        mesh=mesh,
        in_specs=(
            P(("parts", "seq", "head"), None),
            P(),
            P(),
            P("head", None, "seq", None),
            P("head", None, "seq", None),
            P("parts", None),
        ),
        out_specs=P(("parts", "seq"), "head"),
        check_vma=False,
    )
```

```python
from functools import partial
import math

import jax
import jax.numpy as jnp
from jax import lax
from jax.experimental import pallas as pl
from jax.experimental.pallas import tpu as pltpu
from jax.sharding import PartitionSpec as P

epsilon = 1e-06
VMEM_LIMIT = 32 * 1024 * 1024
LIGHT = pl.CostEstimate(flops=1024, bytes_accessed=1024, transcendentals=0)
FAR = -(2.0**100)
NT = (((1,), (1,)), ((), ()))
NN = (((1,), (0,)), ((), ()))


def frequencies(lane, half_width):
    steps = lax.rem(lane, half_width).astype(jnp.float32)
    return jnp.exp(steps * (-math.log(10000.0) / half_width))


def prepare_kernel(q_width, kv_width, slot_count, place_ref, latents_ref, gain_ref, out_ref):
    rows = latents_ref.shape[1]
    rope_width = latents_ref.shape[0] - q_width - kv_width
    half_width = rope_width // 2

    def normalized(low, width):
        part = latents_ref[low : low + width, :].astype(jnp.float32)
        scale = lax.rsqrt(jnp.mean(part * part, axis=0, keepdims=True) + epsilon)
        return (jnp.transpose(part * scale) * gain_ref[:, low : low + width]).astype(jnp.bfloat16)

    out_ref[:, :q_width] = normalized(0, q_width)
    out_ref[:, q_width : q_width + kv_width] = normalized(q_width, kv_width)
    spare = out_ref.shape[1] - q_width - kv_width - rope_width
    token_ids = lax.broadcasted_iota(jnp.int32, (1, rows), 1) + place_ref[1] * rows
    slot_ids = lax.broadcasted_iota(jnp.int32, (spare, rows), 0)
    begin, start, inside = jnp.zeros_like(token_ids), jnp.int32(0), jnp.zeros((spare, rows), jnp.float32)
    for slot in range(slot_count):
        stop = start + place_ref[2 + place_ref[0] * slot_count + slot]
        begin = jnp.where(token_ids >= start, start, begin)
        member = jnp.where((token_ids >= start) & (token_ids < stop), 1.0, 0.0)
        inside = jnp.where(slot_ids == slot, member, inside)
        start = stop
    position = (token_ids - begin).astype(jnp.float32)
    angle = position * frequencies(lax.broadcasted_iota(jnp.int32, (half_width, rows), 0), half_width)
    cosine, sine = jnp.cos(angle), jnp.sin(angle)
    rope = latents_ref[q_width + kv_width :, :].astype(jnp.float32)
    first, second = rope[:half_width], rope[half_width:]
    turned = jnp.concatenate([first * cosine - second * sine, second * cosine + first * sine, inside], axis=0)
    out_ref[:, q_width + kv_width :] = jnp.transpose(turned).astype(jnp.bfloat16)


def prepare(latents, gains, q_width, kv_width, slot_count, place):
    rows = latents.shape[0]
    rope_width = latents.shape[1] - q_width - kv_width
    width = q_width + kv_width + -(-(rope_width + slot_count) // 128) * 128
    vmem = pl.BlockSpec(memory_space=pltpu.VMEM)
    return pl.pallas_call(
        partial(prepare_kernel, q_width, kv_width, slot_count),
        out_shape=jax.ShapeDtypeStruct((rows, width), jnp.bfloat16),
        in_specs=[pl.BlockSpec(memory_space=pltpu.SMEM), vmem, vmem],
        out_specs=vmem,
        compiler_params=pltpu.CompilerParams(vmem_limit_bytes=VMEM_LIMIT),
        cost_estimate=LIGHT,
        name="prepare",
    )(place, jnp.transpose(latents), gains[None, :])


def pick_kernel(index_ref, source_ref, out_ref):
    out_ref[...] = source_ref[...]


def pick(source, index, block, axis):
    shape = list(source.shape)
    shape[axis] = block
    out_shape = shape
    position = lambda step, index_ref: tuple(index_ref[0] if at == axis else 0 for at in range(len(shape)))
    return pl.pallas_call(
        pick_kernel,
        grid_spec=pltpu.PrefetchScalarGridSpec(
            num_scalar_prefetch=1,
            grid=(1,),
            in_specs=[pl.BlockSpec(tuple(shape), position)],
            out_specs=pl.BlockSpec(tuple(out_shape), lambda step, index_ref: (0,) * len(out_shape)),
        ),
        out_shape=jax.ShapeDtypeStruct(tuple(out_shape), source.dtype),
        compiler_params=pltpu.CompilerParams(vmem_limit_bytes=VMEM_LIMIT),
        cost_estimate=LIGHT,
        name="pick",
    )(jnp.reshape(index, (1,)).astype(jnp.int32), source)


def attend_group(sizes, chosen, tokens_ref, scratch, out_refs):
    heads, q_width, kv_width, nope_width, rope_width, value_width = sizes
    query_width, pair_width = nope_width + rope_width, nope_width + value_width
    query_ref, key_ref, value_ref, turn_ref, bias_ref = scratch
    out_heads = heads // len(out_refs)
    tokens = tokens_ref.shape[0]
    rows = bias_ref.shape[0]
    half_width = rope_width // 2
    group_heads = nope_width // rope_width
    score_scale = query_width**-0.5 * math.log2(math.e)
    lane = lax.broadcasted_iota(jnp.int32, (tokens, nope_width), 1)
    is_first = lax.rem(lane, rope_width) < half_width
    is_rope = lane < rope_width
    rope_low = q_width + kv_width
    apart = jnp.where(is_rope, 0.0, (1.0 - tokens_ref[:, rope_low:].astype(jnp.float32)) * FAR)

    def dot(left, right, dims):
        return lax.dot_general(left, right, dims, preferred_element_type=jnp.float32)

    def project(some):
        picked = [chosen[head] for head in some]
        while len(picked) < group_heads:
            picked.append(picked[-1])

        def query(low, high, picked):
            parts = [query_weight_ref[number, low:high, :] for query_weight_ref, _, number in picked]
            return dot(tokens_ref[:, :q_width], jnp.concatenate(parts, axis=0), NT)

        rope = query(nope_width, query_width, picked)
        nope = query(0, nope_width, picked[: len(some)])
        latent = tokens_ref[:, q_width:rope_low]
        pairs = [weight_ref[:, number * pair_width : (number + 1) * pair_width] for _, weight_ref, number in picked]
        pair = dot(latent, jnp.concatenate(pairs[: len(some)], axis=1), NN)
        swapped = jnp.where(is_first, pltpu.roll(rope, nope_width - half_width, 1), pltpu.roll(rope, half_width, 1))
        turned = (rope * turn_ref[:, :nope_width] + swapped * turn_ref[:, nope_width:]) * score_scale
        for index, head in enumerate(some):
            low = 2 * head * nope_width
            part = nope[:, index * nope_width : (index + 1) * nope_width]
            query_ref[:, low : low + nope_width] = (part * score_scale).astype(jnp.bfloat16)
            moved = pltpu.roll(turned, nope_width - index * rope_width, 1) if index else turned
            query_ref[:, low + nope_width : low + 2 * nope_width] = jnp.where(is_rope, moved, apart).astype(jnp.bfloat16)
            both = pair[:, index * pair_width : (index + 1) * pair_width].astype(jnp.bfloat16)
            key_ref[:, head * nope_width : (head + 1) * nope_width] = both[:, :nope_width]
            value_ref[head, :, :value_width] = both[:, nope_width:]

    def score(head, half):
        low, high = half * rows, (half + 1) * rows
        queries = query_ref[low:high, 2 * head * nope_width : (2 * head + 2) * nope_width]
        shared = tokens_ref[:high, rope_low:]
        keys = jnp.concatenate([key_ref[:high, head * nope_width : (head + 1) * nope_width], shared], axis=1)
        return dot(queries, keys, NT)

    def soften(half, scores):
        low = half * rows
        last = scores[:, low:] + bias_ref[...]
        scores = jnp.concatenate([scores[:, :low], last], axis=1) if half else last
        return jnp.exp2(scores - jnp.max(scores, axis=1, keepdims=True)).astype(jnp.bfloat16)

    def mix(head, half, terms):
        low, high = half * rows, (half + 1) * rows
        mixed = dot(terms, value_ref[head, :high, :], NN)
        column = head % out_heads * value_width
        out_refs[head // out_heads][low:high, column : column + value_width] = (
            mixed[:, :value_width] / mixed[:, value_width:]
        ).astype(jnp.bfloat16)

    batches = [list(range(heads))[low : low + group_heads] for low in range(0, heads, group_heads)]
    project(batches[0])
    yield
    terms = None
    for number, batch in enumerate(batches):
        scores = score(batch[0], 0)
        if number + 1 < len(batches):
            project(batches[number + 1])
        else:
            yield
        for head in batch:
            for half in range(2):
                ahead = (head, 1) if half == 0 else (head + 1, 0)
                following = score(*ahead) if ahead[0] in batch else None
                held = soften(half, scores)
                if terms is not None:
                    mix(*terms)
                terms = (head, half, held)
                scores = following
    yield
    mix(*terms)


def attend_groups(works):
    works = list(works)
    for index, work in enumerate(works):
        if index == 0:
            next(work)
        next(work)
        if index + 1 < len(works):
            next(works[index + 1])
        for rest in work:
            pass


def set_up(scratch, first=True):
    value_ref, bias_ref = scratch[2], scratch[4]
    rows = bias_ref.shape[0]
    heads, tokens, width = value_ref.shape
    if first:
        row_ids = lax.broadcasted_iota(jnp.int32, (rows, rows), 0)
        col_ids = lax.broadcasted_iota(jnp.int32, (rows, rows), 1)
        bias_ref[...] = jnp.where(col_ids <= row_ids, 0.0, -jnp.inf)
    for head in range(heads):
        value_ref[head, :, width // 2 :] = jnp.ones((tokens, width // 2), jnp.bfloat16)


def set_turn(group, slot_count, place_ref, table_ref, turn_ref):
    block = turn_ref.shape[0] // slot_count
    starts, start = [], jnp.int32(0)
    for index in range(slot_count):
        starts.append(start)
        start = start + place_ref[2 + group * slot_count + index]
    for index in range(slot_count):
        begin = jnp.int32(0)
        for entry in starts:
            begin = jnp.where(entry <= index * block, entry, begin)
        position = pl.multiple_of(index * block - begin, block)
        turn_ref[index * block : (index + 1) * block, :] = table_ref[pl.ds(position, block), :]


def near_kernel(sizes, slot_count, distance, place_ref, table_ref, query_weight_ref, pair_weight_ref, same_ref, other_ref, out_ref, tokens_ref, *scratch):
    core, group = place_ref[1], place_ref[0] ^ distance
    rows = same_ref.shape[0]
    tokens_ref[pl.ds(pl.multiple_of(core * rows, rows), rows), :] = same_ref[...]
    tokens_ref[pl.ds(pl.multiple_of((1 - core) * rows, rows), rows), :] = other_ref[...]
    set_up(scratch)
    set_turn(group, slot_count, place_ref, table_ref, scratch[3])
    chosen = [(query_weight_ref, pair_weight_ref, head) for head in range(sizes[0])]
    attend_groups([attend_group(sizes, chosen, tokens_ref, scratch, [out_ref])])


def far_kernel(sizes, slot_count, distances, parts, arrays, place_ref, table_ref, *refs):
    slots = len(distances)
    query_refs, pair_refs, refs = refs[:arrays], refs[arrays : 2 * arrays], refs[2 * arrays :]
    token_refs, out_refs, refs = refs[:slots], refs[slots : slots + sum(parts)], refs[slots + sum(parts) :]
    bias_ref, refs = refs[0], refs[1:]
    chosen = [(*both, number) for both in zip(query_refs, pair_refs) for number in range(both[0].shape[0])]
    works, first = [], 0
    for slot in range(slots):
        scratch = [*refs[4 * slot : 4 * slot + 4], bias_ref]
        set_up(scratch, slot == 0)
        set_turn(place_ref[0] ^ distances[slot], slot_count, place_ref, table_ref, scratch[3])
        works.append(attend_group(sizes, chosen, token_refs[slot], scratch, out_refs[first : first + parts[slot]]))
        first += parts[slot]
    attend_groups(works)


def scratch_for(sizes, tokens):
    heads, q_width, kv_width, nope_width, rope_width, value_width = sizes
    return [
        pltpu.VMEM((tokens, 2 * heads * nope_width), jnp.bfloat16),
        pltpu.VMEM((tokens, heads * nope_width), jnp.bfloat16),
        pltpu.VMEM((heads, tokens, 2 * value_width), jnp.bfloat16),
        pltpu.VMEM((tokens, 2 * nope_width), jnp.float32),
        pltpu.VMEM((tokens // 2, tokens // 2), jnp.float32),
    ]


def attend_near(sizes, slot_count, distance, place, table, query_weight, pair_weight, same, other):
    rows, width = same.shape
    heads, value_width = sizes[0], sizes[-1]
    vmem = pl.BlockSpec(memory_space=pltpu.VMEM)
    return pl.pallas_call(
        partial(near_kernel, sizes, slot_count, distance),
        out_shape=[
            jax.ShapeDtypeStruct((2 * rows, heads * value_width), jnp.bfloat16),
            jax.ShapeDtypeStruct((2 * rows, width), jnp.bfloat16),
        ],
        in_specs=[pl.BlockSpec(memory_space=pltpu.SMEM)] + [vmem] * 5,
        out_specs=[vmem, vmem],
        scratch_shapes=scratch_for(sizes, 2 * rows),
        compiler_params=pltpu.CompilerParams(vmem_limit_bytes=VMEM_LIMIT),
        cost_estimate=LIGHT,
        name="attend_near",
    )(place, table, query_weight, pair_weight, same, other)


def attend_far(sizes, slot_count, distances, parts, place, table, queries, pairs, groups):
    tokens = groups[0].shape[0]
    slots, heads, value_width = len(groups), sizes[0], sizes[-1]
    vmem = pl.BlockSpec(memory_space=pltpu.VMEM)
    own = scratch_for(sizes, tokens)
    shapes = [jax.ShapeDtypeStruct((tokens, heads // part * value_width), jnp.bfloat16) for part in parts for _ in range(part)]
    results = pl.pallas_call(
        partial(far_kernel, sizes, slot_count, distances, parts, len(queries)),
        out_shape=shapes,
        in_specs=[pl.BlockSpec(memory_space=pltpu.SMEM)] + [vmem] * (1 + 2 * len(queries) + slots),
        out_specs=[vmem] * len(shapes),
        scratch_shapes=own[4:] + own[:4] * slots,
        compiler_params=pltpu.CompilerParams(vmem_limit_bytes=VMEM_LIMIT),
        cost_estimate=LIGHT,
        name="attend_far",
    )(place, table, *queries, *pairs, *groups)
    return [results[sum(parts[:slot]) : sum(parts[: slot + 1])] for slot in range(slots)]


def place_kernel(width, count, offsets_ref, *refs):
    pieces, out_ref, sems = refs[:count], refs[-2], refs[-1]
    copies = []
    for piece in pieces:
        for low in range(0, piece.shape[1], width):
            index = len(copies)
            columns = pl.ds(pl.multiple_of(offsets_ref[index], 128), width)
            copies.append(pltpu.make_async_copy(piece.at[:, low : low + width], out_ref.at[:, columns], sems.at[index]))
            copies[-1].start()
    for copy in copies:
        copy.wait()


def place_pieces(pieces, offsets, width, out_width, held=None):
    count = len(pieces)
    any_space = pl.BlockSpec(memory_space=pl.ANY)
    operands = [jnp.stack(offsets).astype(jnp.int32), *pieces]
    specs = [pl.BlockSpec(memory_space=pltpu.SMEM)] + [pl.BlockSpec(memory_space=pltpu.VMEM)] * count
    aliases = {}
    if held is not None:
        aliases = {len(operands): 0}
        operands.append(held)
        specs.append(any_space)
    return pl.pallas_call(
        partial(place_kernel, width, count),
        out_shape=jax.ShapeDtypeStruct((pieces[0].shape[0], out_width), pieces[0].dtype),
        in_specs=specs,
        out_specs=any_space,
        scratch_shapes=[pltpu.SemaphoreType.DMA((len(offsets),))],
        input_output_aliases=aliases,
        compiler_params=pltpu.CompilerParams(vmem_limit_bytes=VMEM_LIMIT),
        cost_estimate=LIGHT,
        name="place_pieces",
    )(*operands)


def after(value, *earlier):
    return lax.optimization_barrier((value, *earlier))[0]


def shards(latents, q_gain, kv_gain, q_weight, kv_weight, lengths):
    q_width, kv_width = q_gain.shape[0], kv_gain.shape[0]
    rope_width = latents.shape[1] - q_width - kv_width
    places = lax.axis_size("seq")
    parts = lax.axis_size("parts")
    half_places = places // 2
    place = lax.axis_index("seq")
    core = lax.axis_index("head")
    part = lax.axis_index("parts")
    tokens = 2 * latents.shape[0]
    local_heads = q_weight.shape[2]
    pair_width = kv_weight.shape[3]
    nope_width = q_weight.shape[3] - rope_width
    value_width = pair_width - nope_width
    block_width = local_heads * value_width
    sizes = (q_width, kv_width, nope_width, rope_width, value_width)

    def across(value, distance):
        return lax.ppermute(value, "seq", [(s, s ^ distance) for s in range(places)])

    def sibling(value):
        return lax.ppermute(value, "head", [(0, 1), (1, 0)])

    def other_part(value):
        return lax.ppermute(value, "parts", [(p, p ^ 1) for p in range(parts)])

    slot_count = lengths.shape[1]
    gains = jnp.concatenate([q_gain, kv_gain])
    spot = jnp.concatenate([jnp.stack([place, core]).astype(jnp.int32), jnp.reshape(lengths, -1)])
    own_query = jnp.transpose(q_weight[0], (1, 2, 0))
    own_pair = jnp.reshape(kv_weight[0], (kv_width, local_heads * pair_width))
    positions = jnp.arange(tokens, dtype=jnp.int32)[:, None].astype(jnp.float32)
    lanes = jnp.arange(nope_width, dtype=jnp.int32)[None, :]
    angles = positions * frequencies(lanes, rope_width // 2)
    signs = jnp.where(lax.rem(lanes, rope_width) < rope_width // 2, -1.0, 1.0)
    table = jnp.concatenate([jnp.cos(angles), jnp.sin(angles) * signs], axis=1)
    share = 2 if parts % 2 == 0 and local_heads % 2 == 0 else 1
    per_part = local_heads // share
    side = lax.rem(part, share)

    sent_pair = pick(own_pair, side, per_part * pair_width, 1)
    sent_query = pick(own_query, side, per_part, 0)
    latent = prepare(latents, gains, q_width, kv_width, slot_count, spot)
    same, other = [latent], [sibling(latent)]
    for distance in range(1, half_places):
        same.append(across(latent, distance) if distance & (distance - 1) == 0 else None)
    far_query = across(sent_query, half_places)
    far_pair = across(after(sent_pair, far_query), half_places)

    joined = []

    def near(distance, *earlier):
        mixed, tokens_joined = attend_near(
            (local_heads, *sizes),
            slot_count,
            distance,
            spot,
            table,
            own_query,
            own_pair,
            after(same[distance], *earlier),
            other[distance],
        )
        joined.append(tokens_joined)
        return mixed

    mixed = near(0)
    arrived = [mixed]
    direct = [entry for entry in same[1:] if entry is not None]
    for distance in range(1, half_places):
        if same[distance] is None:
            low_bit = distance & -distance
            same[distance] = across(after(same[distance ^ low_bit], mixed), low_bit)
            other.append(None)
        else:
            other.append(sibling(after(same[distance], mixed, far_query, *direct)))
    crossed_query = [other_part(after(far_query, mixed))] if share == 2 else []
    for distance in range(1, half_places):
        if other[distance] is None:
            other[distance] = sibling(after(same[distance], mixed, far_pair, *crossed_query))
        mixed = near(distance, mixed)
        arrived.append(across(mixed, distance))
    placed = []
    for distance in range(half_places):
        base = (place ^ distance) * block_width
        placed.append((arrived[distance], [base + head * value_width for head in range(local_heads)]))

    out_width = places * block_width

    def flush(held):
        offsets = [offset for piece, starts in placed for offset in starts]
        held = place_pieces([piece for piece, starts in placed], offsets, value_width, out_width, held)
        placed.clear()
        return held

    queries, pairs = [far_query], [far_pair]
    numbers = [side * per_part + index for index in range(per_part)]
    if share == 2:
        queries.append(crossed_query[0])
        pairs.append(other_part(far_pair))
        numbers += [(1 - side) * per_part + index for index in range(per_part)]
    late, gates = [], []
    for distances in (list(range(half_places // 2, half_places)), list(range(1, half_places // 2)) + [0]):
        parts_of = [share if 0 < distance < half_places // 2 else 1 for distance in distances]
        mixed_some = attend_far(
            (len(numbers), *sizes),
            slot_count,
            distances,
            parts_of,
            after(spot, mixed, *gates),
            table,
            queries,
            pairs,
            [joined[distance] for distance in distances],
        )
        mixed, gates = mixed_some[0][0], arrived[1:]
        for distance, pieces in zip(distances, mixed_some):
            base = (place ^ distance ^ half_places) * block_width
            each = len(numbers) // len(pieces)
            for index, piece in enumerate(pieces):
                spans = [base + number * value_width for number in numbers[index * each : (index + 1) * each]]
                late.append((across(piece, distance) if distance else piece, spans))
    held = flush(None)
    placed.extend(late)
    held = flush(held)
    return held


def solution(mesh):
    return jax.shard_map(
        shards,
        mesh=mesh,
        in_specs=(
            P(("parts", "seq", "head"), None),
            P(),
            P(),
            P("head", None, "seq", None),
            P("head", None, "seq", None),
            P("parts", None),
        ),
        out_specs=P(("parts", "seq"), "head"),
        check_vma=False,
    )
```

```python
from functools import partial
import math

import jax
import jax.numpy as jnp
from jax import lax
from jax.experimental import pallas as pl
from jax.experimental.pallas import tpu as pltpu
from jax.sharding import PartitionSpec as P

epsilon = 1e-06
VMEM_LIMIT = 32 * 1024 * 1024
LIGHT = pl.CostEstimate(flops=1024, bytes_accessed=1024, transcendentals=0)
FAR = -(2.0**100)
NT = (((1,), (1,)), ((), ()))
NN = (((1,), (0,)), ((), ()))


def frequencies(lane, half_width):
    steps = lax.rem(lane, half_width).astype(jnp.float32)
    return jnp.exp(steps * (-math.log(10000.0) / half_width))


def swapped_bits(slot):
    return (slot & ~3) | (slot & 1) << 1 | (slot & 2) >> 1


def distance_of(slot, core, half_places):
    if half_places < 4:
        return slot
    return jnp.where(core == 0, slot, swapped_bits(slot))


def prepare_kernel(q_width, kv_width, slot_count, place_ref, latents_ref, gain_ref, out_ref):
    rows = latents_ref.shape[1]
    rope_width = latents_ref.shape[0] - q_width - kv_width
    half_width = rope_width // 2

    def normalized(low, width):
        part = latents_ref[low : low + width, :].astype(jnp.float32)
        scale = lax.rsqrt(jnp.mean(part * part, axis=0, keepdims=True) + epsilon)
        return (jnp.transpose(part * scale) * gain_ref[:, low : low + width]).astype(jnp.bfloat16)

    out_ref[:, :q_width] = normalized(0, q_width)
    out_ref[:, q_width : q_width + kv_width] = normalized(q_width, kv_width)
    spare = out_ref.shape[1] - q_width - kv_width - rope_width
    token_ids = lax.broadcasted_iota(jnp.int32, (1, rows), 1) + place_ref[1] * rows
    slot_ids = lax.broadcasted_iota(jnp.int32, (spare, rows), 0)
    begin, start, inside = jnp.zeros_like(token_ids), jnp.int32(0), jnp.zeros((spare, rows), jnp.float32)
    for slot in range(slot_count):
        stop = start + place_ref[2 + place_ref[0] * slot_count + slot]
        begin = jnp.where(token_ids >= start, start, begin)
        member = jnp.where((token_ids >= start) & (token_ids < stop), 1.0, 0.0)
        inside = jnp.where(slot_ids == slot, member, inside)
        start = stop
    position = (token_ids - begin).astype(jnp.float32)
    angle = position * frequencies(lax.broadcasted_iota(jnp.int32, (half_width, rows), 0), half_width)
    cosine, sine = jnp.cos(angle), jnp.sin(angle)
    rope = latents_ref[q_width + kv_width :, :].astype(jnp.float32)
    first, second = rope[:half_width], rope[half_width:]
    turned = jnp.concatenate([first * cosine - second * sine, second * cosine + first * sine, inside], axis=0)
    out_ref[:, q_width + kv_width :] = jnp.transpose(turned).astype(jnp.bfloat16)


def prepare(latents, gains, q_width, kv_width, slot_count, place):
    rows = latents.shape[0]
    rope_width = latents.shape[1] - q_width - kv_width
    width = q_width + kv_width + -(-(rope_width + slot_count) // 128) * 128
    vmem = pl.BlockSpec(memory_space=pltpu.VMEM)
    return pl.pallas_call(
        partial(prepare_kernel, q_width, kv_width, slot_count),
        out_shape=jax.ShapeDtypeStruct((rows, width), jnp.bfloat16),
        in_specs=[pl.BlockSpec(memory_space=pltpu.SMEM), vmem, vmem],
        out_specs=vmem,
        compiler_params=pltpu.CompilerParams(vmem_limit_bytes=VMEM_LIMIT),
        cost_estimate=LIGHT,
        name="prepare",
    )(place, jnp.transpose(latents), gains[None, :])


def pick_kernel(index_ref, source_ref, out_ref):
    out_ref[...] = source_ref[...]


def pick(source, index, block, axis):
    shape = list(source.shape)
    shape[axis] = block
    out_shape = shape
    position = lambda step, index_ref: tuple(index_ref[0] if at == axis else 0 for at in range(len(shape)))
    return pl.pallas_call(
        pick_kernel,
        grid_spec=pltpu.PrefetchScalarGridSpec(
            num_scalar_prefetch=1,
            grid=(1,),
            in_specs=[pl.BlockSpec(tuple(shape), position)],
            out_specs=pl.BlockSpec(tuple(out_shape), lambda step, index_ref: (0,) * len(out_shape)),
        ),
        out_shape=jax.ShapeDtypeStruct(tuple(out_shape), source.dtype),
        compiler_params=pltpu.CompilerParams(vmem_limit_bytes=VMEM_LIMIT),
        cost_estimate=LIGHT,
        name="pick",
    )(jnp.reshape(index, (1,)).astype(jnp.int32), source)


def attend_group(sizes, chosen, tokens_ref, scratch, out_refs):
    heads, q_width, kv_width, nope_width, rope_width, value_width = sizes
    query_width, pair_width = nope_width + rope_width, nope_width + value_width
    query_ref, key_ref, value_ref, turn_ref, bias_ref = scratch
    out_heads = heads // len(out_refs)
    tokens = tokens_ref.shape[0]
    rows = bias_ref.shape[0]
    half_width = rope_width // 2
    group_heads = nope_width // rope_width
    score_scale = query_width**-0.5 * math.log2(math.e)
    lane = lax.broadcasted_iota(jnp.int32, (tokens, nope_width), 1)
    is_first = lax.rem(lane, rope_width) < half_width
    is_rope = lane < rope_width
    rope_low = q_width + kv_width
    apart = jnp.where(is_rope, 0.0, (1.0 - tokens_ref[:, rope_low:].astype(jnp.float32)) * FAR)

    def dot(left, right, dims):
        return lax.dot_general(left, right, dims, preferred_element_type=jnp.float32)

    def project(some):
        picked = [chosen[head] for head in some]
        while len(picked) < group_heads:
            picked.append(picked[-1])

        def query(low, high, picked):
            parts = [query_weight_ref[number, low:high, :] for query_weight_ref, _, number in picked]
            return dot(tokens_ref[:, :q_width], jnp.concatenate(parts, axis=0), NT)

        rope = query(nope_width, query_width, picked)
        nope = query(0, nope_width, picked[: len(some)])
        latent = tokens_ref[:, q_width:rope_low]
        pairs = [weight_ref[:, number * pair_width : (number + 1) * pair_width] for _, weight_ref, number in picked]
        pair = dot(latent, jnp.concatenate(pairs[: len(some)], axis=1), NN)
        swapped = jnp.where(is_first, pltpu.roll(rope, nope_width - half_width, 1), pltpu.roll(rope, half_width, 1))
        turned = (rope * turn_ref[:, :nope_width] + swapped * turn_ref[:, nope_width:]) * score_scale
        for index, head in enumerate(some):
            low = 2 * head * nope_width
            part = nope[:, index * nope_width : (index + 1) * nope_width]
            query_ref[:, low : low + nope_width] = (part * score_scale).astype(jnp.bfloat16)
            moved = pltpu.roll(turned, nope_width - index * rope_width, 1) if index else turned
            query_ref[:, low + nope_width : low + 2 * nope_width] = jnp.where(is_rope, moved, apart).astype(jnp.bfloat16)
            both = pair[:, index * pair_width : (index + 1) * pair_width].astype(jnp.bfloat16)
            key_ref[:, head * nope_width : (head + 1) * nope_width] = both[:, :nope_width]
            value_ref[head, :, :value_width] = both[:, nope_width:]

    def score(head, half):
        low, high = half * rows, (half + 1) * rows
        queries = query_ref[low:high, 2 * head * nope_width : (2 * head + 2) * nope_width]
        shared = tokens_ref[:high, rope_low:]
        keys = jnp.concatenate([key_ref[:high, head * nope_width : (head + 1) * nope_width], shared], axis=1)
        return dot(queries, keys, NT)

    def soften(half, scores):
        low = half * rows
        last = scores[:, low:] + bias_ref[...]
        scores = jnp.concatenate([scores[:, :low], last], axis=1) if half else last
        return jnp.exp2(scores - jnp.max(scores, axis=1, keepdims=True)).astype(jnp.bfloat16)

    def mix(head, half, terms):
        low, high = half * rows, (half + 1) * rows
        mixed = dot(terms, value_ref[head, :high, :], NN)
        column = head % out_heads * value_width
        out_refs[head // out_heads][low:high, column : column + value_width] = (
            mixed[:, :value_width] / mixed[:, value_width:]
        ).astype(jnp.bfloat16)

    batches = [list(range(heads))[low : low + group_heads] for low in range(0, heads, group_heads)]
    project(batches[0])
    yield
    terms = None
    for number, batch in enumerate(batches):
        scores = score(batch[0], 0)
        if number + 1 < len(batches):
            project(batches[number + 1])
        else:
            yield
        for head in batch:
            for half in range(2):
                ahead = (head, 1) if half == 0 else (head + 1, 0)
                following = score(*ahead) if ahead[0] in batch else None
                held = soften(half, scores)
                if terms is not None:
                    mix(*terms)
                terms = (head, half, held)
                scores = following
    yield
    mix(*terms)


def attend_groups(works):
    works = list(works)
    for index, work in enumerate(works):
        if index == 0:
            next(work)
        next(work)
        if index + 1 < len(works):
            next(works[index + 1])
        for rest in work:
            pass


def set_up(scratch, first=True):
    value_ref, bias_ref = scratch[2], scratch[4]
    rows = bias_ref.shape[0]
    heads, tokens, width = value_ref.shape
    if first:
        row_ids = lax.broadcasted_iota(jnp.int32, (rows, rows), 0)
        col_ids = lax.broadcasted_iota(jnp.int32, (rows, rows), 1)
        bias_ref[...] = jnp.where(col_ids <= row_ids, 0.0, -jnp.inf)
    for head in range(heads):
        value_ref[head, :, width // 2 :] = jnp.ones((tokens, width // 2), jnp.bfloat16)


def set_turn(group, slot_count, place_ref, table_ref, turn_ref):
    block = turn_ref.shape[0] // slot_count
    starts, start = [], jnp.int32(0)
    for index in range(slot_count):
        starts.append(start)
        start = start + place_ref[2 + group * slot_count + index]
    for index in range(slot_count):
        begin = jnp.int32(0)
        for entry in starts:
            begin = jnp.where(entry <= index * block, entry, begin)
        position = pl.multiple_of(index * block - begin, block)
        turn_ref[index * block : (index + 1) * block, :] = table_ref[pl.ds(position, block), :]


def near_kernel(sizes, slot_count, slot, half_places, place_ref, table_ref, query_weight_ref, pair_weight_ref, same_ref, other_ref, out_ref, tokens_ref, *scratch):
    core = place_ref[1]
    group = place_ref[0] ^ distance_of(slot, core, half_places)
    rows = same_ref.shape[0]
    tokens_ref[pl.ds(pl.multiple_of(core * rows, rows), rows), :] = same_ref[...]
    tokens_ref[pl.ds(pl.multiple_of((1 - core) * rows, rows), rows), :] = other_ref[...]
    set_up(scratch)
    set_turn(group, slot_count, place_ref, table_ref, scratch[3])
    chosen = [(query_weight_ref, pair_weight_ref, head) for head in range(sizes[0])]
    attend_groups([attend_group(sizes, chosen, tokens_ref, scratch, [out_ref])])


def far_kernel(sizes, slot_count, numbers, half_places, parts, arrays, place_ref, table_ref, *refs):
    slots = len(numbers)
    query_refs, pair_refs, refs = refs[:arrays], refs[arrays : 2 * arrays], refs[2 * arrays :]
    token_refs, out_refs, refs = refs[:slots], refs[slots : slots + sum(parts)], refs[slots + sum(parts) :]
    bias_ref, refs = refs[0], refs[1:]
    chosen = [(*both, number) for both in zip(query_refs, pair_refs) for number in range(both[0].shape[0])]
    works, first = [], 0
    for slot in range(slots):
        scratch = [*refs[4 * slot : 4 * slot + 4], bias_ref]
        set_up(scratch, slot == 0)
        group = place_ref[0] ^ distance_of(numbers[slot], place_ref[1], half_places)
        set_turn(group, slot_count, place_ref, table_ref, scratch[3])
        works.append(attend_group(sizes, chosen, token_refs[slot], scratch, out_refs[first : first + parts[slot]]))
        first += parts[slot]
    attend_groups(works)


def scratch_for(sizes, tokens):
    heads, q_width, kv_width, nope_width, rope_width, value_width = sizes
    return [
        pltpu.VMEM((tokens, 2 * heads * nope_width), jnp.bfloat16),
        pltpu.VMEM((tokens, heads * nope_width), jnp.bfloat16),
        pltpu.VMEM((heads, tokens, 2 * value_width), jnp.bfloat16),
        pltpu.VMEM((tokens, 2 * nope_width), jnp.float32),
        pltpu.VMEM((tokens // 2, tokens // 2), jnp.float32),
    ]


def attend_near(sizes, slot_count, slot, half_places, place, table, query_weight, pair_weight, same, other):
    rows, width = same.shape
    heads, value_width = sizes[0], sizes[-1]
    vmem = pl.BlockSpec(memory_space=pltpu.VMEM)
    return pl.pallas_call(
        partial(near_kernel, sizes, slot_count, slot, half_places),
        out_shape=[
            jax.ShapeDtypeStruct((2 * rows, heads * value_width), jnp.bfloat16),
            jax.ShapeDtypeStruct((2 * rows, width), jnp.bfloat16),
        ],
        in_specs=[pl.BlockSpec(memory_space=pltpu.SMEM)] + [vmem] * 5,
        out_specs=[vmem, vmem],
        scratch_shapes=scratch_for(sizes, 2 * rows),
        compiler_params=pltpu.CompilerParams(vmem_limit_bytes=VMEM_LIMIT),
        cost_estimate=LIGHT,
        name="attend_near",
    )(place, table, query_weight, pair_weight, same, other)


def attend_far(sizes, slot_count, numbers, half_places, parts, place, table, queries, pairs, groups):
    tokens = groups[0].shape[0]
    slots, heads, value_width = len(groups), sizes[0], sizes[-1]
    vmem = pl.BlockSpec(memory_space=pltpu.VMEM)
    own = scratch_for(sizes, tokens)
    shapes = [jax.ShapeDtypeStruct((tokens, heads // part * value_width), jnp.bfloat16) for part in parts for _ in range(part)]
    results = pl.pallas_call(
        partial(far_kernel, sizes, slot_count, numbers, half_places, parts, len(queries)),
        out_shape=shapes,
        in_specs=[pl.BlockSpec(memory_space=pltpu.SMEM)] + [vmem] * (1 + 2 * len(queries) + slots),
        out_specs=[vmem] * len(shapes),
        scratch_shapes=own[4:] + own[:4] * slots,
        compiler_params=pltpu.CompilerParams(vmem_limit_bytes=VMEM_LIMIT),
        cost_estimate=LIGHT,
        name="attend_far",
    )(place, table, *queries, *pairs, *groups)
    return [results[sum(parts[:slot]) : sum(parts[: slot + 1])] for slot in range(slots)]


def place_kernel(width, count, offsets_ref, *refs):
    pieces, out_ref, sems = refs[:count], refs[-2], refs[-1]
    copies = []
    for piece in pieces:
        for low in range(0, piece.shape[1], width):
            index = len(copies)
            columns = pl.ds(pl.multiple_of(offsets_ref[index], 128), width)
            copies.append(pltpu.make_async_copy(piece.at[:, low : low + width], out_ref.at[:, columns], sems.at[index]))
            copies[-1].start()
    for copy in copies:
        copy.wait()


def place_pieces(pieces, offsets, width, out_width, held=None):
    count = len(pieces)
    any_space = pl.BlockSpec(memory_space=pl.ANY)
    operands = [jnp.stack(offsets).astype(jnp.int32), *pieces]
    specs = [pl.BlockSpec(memory_space=pltpu.SMEM)] + [pl.BlockSpec(memory_space=pltpu.VMEM)] * count
    aliases = {}
    if held is not None:
        aliases = {len(operands): 0}
        operands.append(held)
        specs.append(any_space)
    return pl.pallas_call(
        partial(place_kernel, width, count),
        out_shape=jax.ShapeDtypeStruct((pieces[0].shape[0], out_width), pieces[0].dtype),
        in_specs=specs,
        out_specs=any_space,
        scratch_shapes=[pltpu.SemaphoreType.DMA((len(offsets),))],
        input_output_aliases=aliases,
        compiler_params=pltpu.CompilerParams(vmem_limit_bytes=VMEM_LIMIT),
        cost_estimate=LIGHT,
        name="place_pieces",
    )(*operands)


def after(value, *earlier):
    return lax.optimization_barrier((value, *earlier))[0]


def shards(latents, q_gain, kv_gain, q_weight, kv_weight, lengths):
    q_width, kv_width = q_gain.shape[0], kv_gain.shape[0]
    rope_width = latents.shape[1] - q_width - kv_width
    places = lax.axis_size("seq")
    parts = lax.axis_size("parts")
    half_places = places // 2
    place = lax.axis_index("seq")
    core = lax.axis_index("head")
    part = lax.axis_index("parts")
    tokens = 2 * latents.shape[0]
    local_heads = q_weight.shape[2]
    pair_width = kv_weight.shape[3]
    nope_width = q_weight.shape[3] - rope_width
    value_width = pair_width - nope_width
    block_width = local_heads * value_width
    sizes = (q_width, kv_width, nope_width, rope_width, value_width)

    def away(slot):
        return place ^ distance_of(slot, core, half_places)

    def opposite(value):
        return lax.ppermute(value, "seq", [(s, s ^ half_places) for s in range(places)])

    def across(value, slot):
        other_slot = slot if half_places < 4 else swapped_bits(slot)
        pairs = [(2 * s + c, 2 * (s ^ distance) + c) for s in range(places) for c, distance in enumerate((slot, other_slot))]
        return lax.ppermute(value, ("seq", "head"), pairs)

    def sibling(value):
        return lax.ppermute(value, "head", [(0, 1), (1, 0)])

    def other_part(value):
        return lax.ppermute(value, "parts", [(p, p ^ 1) for p in range(parts)])

    slot_count = lengths.shape[1]
    gains = jnp.concatenate([q_gain, kv_gain])
    spot = jnp.concatenate([jnp.stack([place, core]).astype(jnp.int32), jnp.reshape(lengths, -1)])
    own_query = jnp.transpose(q_weight[0], (1, 2, 0))
    own_pair = jnp.reshape(kv_weight[0], (kv_width, local_heads * pair_width))
    positions = jnp.arange(tokens, dtype=jnp.int32)[:, None].astype(jnp.float32)
    lanes = jnp.arange(nope_width, dtype=jnp.int32)[None, :]
    angles = positions * frequencies(lanes, rope_width // 2)
    signs = jnp.where(lax.rem(lanes, rope_width) < rope_width // 2, -1.0, 1.0)
    table = jnp.concatenate([jnp.cos(angles), jnp.sin(angles) * signs], axis=1)
    share = 2 if parts % 2 == 0 and local_heads % 2 == 0 else 1
    per_part = local_heads // share
    side = lax.rem(part, share)

    sent_pair = pick(own_pair, side, per_part * pair_width, 1)
    sent_query = pick(own_query, side, per_part, 0)
    latent = prepare(latents, gains, q_width, kv_width, slot_count, spot)
    same, other = [latent], [sibling(latent)]
    for distance in range(1, half_places):
        same.append(across(latent, distance) if distance & (distance - 1) == 0 else None)
    far_query = opposite(sent_query)
    far_pair = opposite(after(sent_pair, far_query))

    joined = []

    def near(distance, *earlier):
        mixed, tokens_joined = attend_near(
            (local_heads, *sizes),
            slot_count,
            distance,
            half_places,
            spot,
            table,
            own_query,
            own_pair,
            after(same[distance], *earlier),
            other[distance],
        )
        joined.append(tokens_joined)
        return mixed

    mixed = near(0)
    arrived = [mixed]
    direct = [entry for entry in same[1:] if entry is not None]
    partner = [slot if half_places < 4 else swapped_bits(slot) for slot in range(half_places)]
    for distance in range(1, half_places):
        if same[distance] is None:
            low_bit = distance & -distance
            same[distance] = across(after(same[distance ^ low_bit], mixed), low_bit)
    for distance in range(1, half_places):
        if distance & (distance - 1) == 0:
            other.append(sibling(after(same[partner[distance]], mixed, far_query, *direct)))
        else:
            other.append(None)
    crossed_query = [other_part(after(far_query, mixed))] if share == 2 else []
    for distance in range(1, half_places):
        if other[distance] is None:
            other[distance] = sibling(after(same[partner[distance]], mixed, far_pair, *crossed_query))
        mixed = near(distance, mixed)
        arrived.append(across(mixed, distance))
    placed = []
    for distance in range(half_places):
        base = away(distance) * block_width
        placed.append((arrived[distance], [base + head * value_width for head in range(local_heads)]))

    out_width = places * block_width

    def flush(held):
        offsets = [offset for piece, starts in placed for offset in starts]
        held = place_pieces([piece for piece, starts in placed], offsets, value_width, out_width, held)
        placed.clear()
        return held

    queries, pairs = [far_query], [far_pair]
    numbers = [side * per_part + index for index in range(per_part)]
    if share == 2:
        queries.append(crossed_query[0])
        pairs.append(other_part(far_pair))
        numbers += [(1 - side) * per_part + index for index in range(per_part)]
    late, gates = [], []
    for distances in (list(range(half_places // 2, half_places)), list(range(1, half_places // 2)) + [0]):
        parts_of = [share if 0 < distance < half_places // 2 else 1 for distance in distances]
        mixed_some = attend_far(
            (len(numbers), *sizes),
            slot_count,
            distances,
            half_places,
            parts_of,
            after(spot, mixed, *gates),
            table,
            queries,
            pairs,
            [joined[distance] for distance in distances],
        )
        mixed, gates = mixed_some[0][0], arrived[1:]
        for distance, pieces in zip(distances, mixed_some):
            base = (away(distance) ^ half_places) * block_width
            each = len(numbers) // len(pieces)
            for index, piece in enumerate(pieces):
                spans = [base + number * value_width for number in numbers[index * each : (index + 1) * each]]
                late.append((across(piece, distance) if distance else piece, spans))
    held = flush(None)
    placed.extend(late)
    held = flush(held)
    return held


def solution(mesh):
    return jax.shard_map(
        shards,
        mesh=mesh,
        in_specs=(
            P(("parts", "seq", "head"), None),
            P(),
            P(),
            P("head", None, "seq", None),
            P("head", None, "seq", None),
            P("parts", None),
        ),
        out_specs=P(("parts", "seq"), "head"),
        check_vma=False,
    )
```

```python
from functools import partial
import math

import jax
import jax.numpy as jnp
from jax import lax
from jax.experimental import pallas as pl
from jax.experimental.pallas import tpu as pltpu
from jax.sharding import PartitionSpec as P

epsilon = 1e-06
VMEM_LIMIT = 32 * 1024 * 1024
LIGHT = pl.CostEstimate(flops=1024, bytes_accessed=1024, transcendentals=0)
FAR = -(2.0**100)
NT = (((1,), (1,)), ((), ()))
NN = (((1,), (0,)), ((), ()))


def frequencies(lane, half_width):
    steps = lax.rem(lane, half_width).astype(jnp.float32)
    return jnp.exp(steps * (-math.log(10000.0) / half_width))


def swapped_bits(slot):
    return (slot & ~3) | (slot & 1) << 1 | (slot & 2) >> 1


def distance_of(slot, core, half_places):
    if half_places < 4:
        return slot
    return jnp.where(core == 0, slot, swapped_bits(slot))


def prepare_kernel(q_width, kv_width, slot_count, place_ref, latents_ref, gain_ref, out_ref):
    rows = latents_ref.shape[1]
    rope_width = latents_ref.shape[0] - q_width - kv_width
    half_width = rope_width // 2

    def normalized(low, width):
        part = latents_ref[low : low + width, :].astype(jnp.float32)
        scale = lax.rsqrt(jnp.mean(part * part, axis=0, keepdims=True) + epsilon)
        return (jnp.transpose(part * scale) * gain_ref[:, low : low + width]).astype(jnp.bfloat16)

    out_ref[:, :q_width] = normalized(0, q_width)
    out_ref[:, q_width : q_width + kv_width] = normalized(q_width, kv_width)
    spare = out_ref.shape[1] - q_width - kv_width - rope_width
    token_ids = lax.broadcasted_iota(jnp.int32, (1, rows), 1) + place_ref[1] * rows
    slot_ids = lax.broadcasted_iota(jnp.int32, (spare, rows), 0)
    begin, start, inside = jnp.zeros_like(token_ids), jnp.int32(0), jnp.zeros((spare, rows), jnp.float32)
    for slot in range(slot_count):
        stop = start + place_ref[2 + place_ref[0] * slot_count + slot]
        begin = jnp.where(token_ids >= start, start, begin)
        member = jnp.where((token_ids >= start) & (token_ids < stop), 1.0, 0.0)
        inside = jnp.where(slot_ids == slot, member, inside)
        start = stop
    position = (token_ids - begin).astype(jnp.float32)
    angle = position * frequencies(lax.broadcasted_iota(jnp.int32, (half_width, rows), 0), half_width)
    cosine, sine = jnp.cos(angle), jnp.sin(angle)
    rope = latents_ref[q_width + kv_width :, :].astype(jnp.float32)
    first, second = rope[:half_width], rope[half_width:]
    turned = jnp.concatenate([first * cosine - second * sine, second * cosine + first * sine, inside], axis=0)
    out_ref[:, q_width + kv_width :] = jnp.transpose(turned).astype(jnp.bfloat16)


def prepare(latents, gains, q_width, kv_width, slot_count, place):
    rows = latents.shape[0]
    rope_width = latents.shape[1] - q_width - kv_width
    width = q_width + kv_width + -(-(rope_width + slot_count) // 128) * 128
    vmem = pl.BlockSpec(memory_space=pltpu.VMEM)
    return pl.pallas_call(
        partial(prepare_kernel, q_width, kv_width, slot_count),
        out_shape=jax.ShapeDtypeStruct((rows, width), jnp.bfloat16),
        in_specs=[pl.BlockSpec(memory_space=pltpu.SMEM), vmem, vmem],
        out_specs=vmem,
        compiler_params=pltpu.CompilerParams(vmem_limit_bytes=VMEM_LIMIT),
        cost_estimate=LIGHT,
        name="prepare",
    )(place, jnp.transpose(latents), gains[None, :])


def pick_kernel(index_ref, source_ref, out_ref):
    out_ref[...] = source_ref[...]


def pick(source, index, block, axis):
    shape = list(source.shape)
    shape[axis] = block
    out_shape = shape
    position = lambda step, index_ref: tuple(index_ref[0] if at == axis else 0 for at in range(len(shape)))
    return pl.pallas_call(
        pick_kernel,
        grid_spec=pltpu.PrefetchScalarGridSpec(
            num_scalar_prefetch=1,
            grid=(1,),
            in_specs=[pl.BlockSpec(tuple(shape), position)],
            out_specs=pl.BlockSpec(tuple(out_shape), lambda step, index_ref: (0,) * len(out_shape)),
        ),
        out_shape=jax.ShapeDtypeStruct(tuple(out_shape), source.dtype),
        compiler_params=pltpu.CompilerParams(vmem_limit_bytes=VMEM_LIMIT),
        cost_estimate=LIGHT,
        name="pick",
    )(jnp.reshape(index, (1,)).astype(jnp.int32), source)


def attend_group(sizes, chosen, tokens_ref, scratch, out_refs):
    heads, q_width, kv_width, nope_width, rope_width, value_width = sizes
    query_width, pair_width = nope_width + rope_width, nope_width + value_width
    query_ref, key_ref, value_ref, turn_ref, bias_ref = scratch
    out_heads = heads // len(out_refs)
    tokens = tokens_ref.shape[0]
    rows = bias_ref.shape[0]
    half_width = rope_width // 2
    group_heads = nope_width // rope_width
    score_scale = query_width**-0.5 * math.log2(math.e)
    lane = lax.broadcasted_iota(jnp.int32, (tokens, nope_width), 1)
    is_first = lax.rem(lane, rope_width) < half_width
    is_rope = lane < rope_width
    rope_low = q_width + kv_width
    apart = jnp.where(is_rope, 0.0, (1.0 - tokens_ref[:, rope_low:].astype(jnp.float32)) * FAR)

    def dot(left, right, dims):
        return lax.dot_general(left, right, dims, preferred_element_type=jnp.float32)

    def project(some):
        picked = [chosen[head] for head in some]
        while len(picked) < group_heads:
            picked.append(picked[-1])

        def query(low, high, picked):
            parts = [query_weight_ref[number, low:high, :] for query_weight_ref, _, number in picked]
            return dot(tokens_ref[:, :q_width], jnp.concatenate(parts, axis=0), NT)

        rope = query(nope_width, query_width, picked)
        nope = query(0, nope_width, picked[: len(some)])
        latent = tokens_ref[:, q_width:rope_low]
        pairs = [weight_ref[:, number * pair_width : (number + 1) * pair_width] for _, weight_ref, number in picked]
        pair = dot(latent, jnp.concatenate(pairs[: len(some)], axis=1), NN)
        swapped = jnp.where(is_first, pltpu.roll(rope, nope_width - half_width, 1), pltpu.roll(rope, half_width, 1))
        turned = (rope * turn_ref[:, :nope_width] + swapped * turn_ref[:, nope_width:]) * score_scale
        for index, head in enumerate(some):
            low = 2 * head * nope_width
            part = nope[:, index * nope_width : (index + 1) * nope_width]
            query_ref[:, low : low + nope_width] = (part * score_scale).astype(jnp.bfloat16)
            moved = pltpu.roll(turned, nope_width - index * rope_width, 1) if index else turned
            query_ref[:, low + nope_width : low + 2 * nope_width] = jnp.where(is_rope, moved, apart).astype(jnp.bfloat16)
            both = pair[:, index * pair_width : (index + 1) * pair_width].astype(jnp.bfloat16)
            key_ref[:, head * nope_width : (head + 1) * nope_width] = both[:, :nope_width]
            value_ref[head, :, :value_width] = both[:, nope_width:]

    def score(head, half):
        low, high = half * rows, (half + 1) * rows
        queries = query_ref[low:high, 2 * head * nope_width : (2 * head + 2) * nope_width]
        shared = tokens_ref[:high, rope_low:]
        keys = jnp.concatenate([key_ref[:high, head * nope_width : (head + 1) * nope_width], shared], axis=1)
        return dot(queries, keys, NT)

    def soften(half, scores):
        low = half * rows
        last = scores[:, low:] + bias_ref[...]
        scores = jnp.concatenate([scores[:, :low], last], axis=1) if half else last
        return jnp.exp2(scores - jnp.max(scores, axis=1, keepdims=True)).astype(jnp.bfloat16)

    def mix(head, half, terms):
        low, high = half * rows, (half + 1) * rows
        mixed = dot(terms, value_ref[head, :high, :], NN)
        column = head % out_heads * value_width
        out_refs[head // out_heads][low:high, column : column + value_width] = (
            mixed[:, :value_width] / mixed[:, value_width:]
        ).astype(jnp.bfloat16)

    batches = [list(range(heads))[low : low + group_heads] for low in range(0, heads, group_heads)]
    project(batches[0])
    yield
    terms = None
    for number, batch in enumerate(batches):
        scores = score(batch[0], 0)
        if number + 1 < len(batches):
            project(batches[number + 1])
        else:
            yield
        for head in batch:
            for half in range(2):
                ahead = (head, 1) if half == 0 else (head + 1, 0)
                following = score(*ahead) if ahead[0] in batch else None
                held = soften(half, scores)
                if terms is not None:
                    mix(*terms)
                terms = (head, half, held)
                scores = following
    yield
    mix(*terms)


def attend_groups(works):
    works = list(works)
    for index, work in enumerate(works):
        if index == 0:
            next(work)
        next(work)
        if index + 1 < len(works):
            next(works[index + 1])
        for rest in work:
            pass


def set_up(scratch, first=True):
    value_ref, bias_ref = scratch[2], scratch[4]
    rows = bias_ref.shape[0]
    heads, tokens, width = value_ref.shape
    if first:
        row_ids = lax.broadcasted_iota(jnp.int32, (rows, rows), 0)
        col_ids = lax.broadcasted_iota(jnp.int32, (rows, rows), 1)
        bias_ref[...] = jnp.where(col_ids <= row_ids, 0.0, -jnp.inf)
    for head in range(heads):
        value_ref[head, :, width // 2 :] = jnp.ones((tokens, width // 2), jnp.bfloat16)


def set_turn(group, slot_count, place_ref, table_ref, turn_ref):
    block = turn_ref.shape[0] // slot_count
    starts, start = [], jnp.int32(0)
    for index in range(slot_count):
        starts.append(start)
        start = start + place_ref[2 + group * slot_count + index]
    for index in range(slot_count):
        begin = jnp.int32(0)
        for entry in starts:
            begin = jnp.where(entry <= index * block, entry, begin)
        position = pl.multiple_of(index * block - begin, block)
        turn_ref[index * block : (index + 1) * block, :] = table_ref[pl.ds(position, block), :]


def near_kernel(sizes, slot_count, slot, half_places, place_ref, table_ref, query_weight_ref, pair_weight_ref, same_ref, other_ref, out_ref, tokens_ref, *scratch):
    core = place_ref[1]
    group = place_ref[0] ^ distance_of(slot, core, half_places)
    rows = same_ref.shape[0]
    tokens_ref[pl.ds(pl.multiple_of(core * rows, rows), rows), :] = same_ref[...]
    tokens_ref[pl.ds(pl.multiple_of((1 - core) * rows, rows), rows), :] = other_ref[...]
    set_up(scratch)
    set_turn(group, slot_count, place_ref, table_ref, scratch[3])
    chosen = [(query_weight_ref, pair_weight_ref, head) for head in range(sizes[0])]
    attend_groups([attend_group(sizes, chosen, tokens_ref, scratch, [out_ref])])


def far_kernel(sizes, slot_count, numbers, half_places, parts, arrays, place_ref, table_ref, *refs):
    slots = len(numbers)
    query_refs, pair_refs, refs = refs[:arrays], refs[arrays : 2 * arrays], refs[2 * arrays :]
    token_refs, out_refs, refs = refs[:slots], refs[slots : slots + sum(parts)], refs[slots + sum(parts) :]
    bias_ref, refs = refs[0], refs[1:]
    chosen = [(*both, number) for both in zip(query_refs, pair_refs) for number in range(both[0].shape[0])]
    works, first = [], 0
    for slot in range(slots):
        scratch = [*refs[4 * slot : 4 * slot + 4], bias_ref]
        set_up(scratch, slot == 0)
        group = place_ref[0] ^ distance_of(numbers[slot], place_ref[1], half_places)
        set_turn(group, slot_count, place_ref, table_ref, scratch[3])
        works.append(attend_group(sizes, chosen, token_refs[slot], scratch, out_refs[first : first + parts[slot]]))
        first += parts[slot]
    attend_groups(works)


def scratch_for(sizes, tokens):
    heads, q_width, kv_width, nope_width, rope_width, value_width = sizes
    return [
        pltpu.VMEM((tokens, 2 * heads * nope_width), jnp.bfloat16),
        pltpu.VMEM((tokens, heads * nope_width), jnp.bfloat16),
        pltpu.VMEM((heads, tokens, 2 * value_width), jnp.bfloat16),
        pltpu.VMEM((tokens, 2 * nope_width), jnp.float32),
        pltpu.VMEM((tokens // 2, tokens // 2), jnp.float32),
    ]


def attend_near(sizes, slot_count, slot, half_places, place, table, query_weight, pair_weight, same, other):
    rows, width = same.shape
    heads, value_width = sizes[0], sizes[-1]
    vmem = pl.BlockSpec(memory_space=pltpu.VMEM)
    return pl.pallas_call(
        partial(near_kernel, sizes, slot_count, slot, half_places),
        out_shape=[
            jax.ShapeDtypeStruct((2 * rows, heads * value_width), jnp.bfloat16),
            jax.ShapeDtypeStruct((2 * rows, width), jnp.bfloat16),
        ],
        in_specs=[pl.BlockSpec(memory_space=pltpu.SMEM)] + [vmem] * 5,
        out_specs=[vmem, vmem],
        scratch_shapes=scratch_for(sizes, 2 * rows),
        compiler_params=pltpu.CompilerParams(vmem_limit_bytes=VMEM_LIMIT),
        cost_estimate=LIGHT,
        name="attend_near",
    )(place, table, query_weight, pair_weight, same, other)


def attend_far(sizes, slot_count, numbers, half_places, parts, place, table, queries, pairs, groups):
    tokens = groups[0].shape[0]
    slots, heads, value_width = len(groups), sizes[0], sizes[-1]
    vmem = pl.BlockSpec(memory_space=pltpu.VMEM)
    own = scratch_for(sizes, tokens)
    shapes = [jax.ShapeDtypeStruct((tokens, heads // part * value_width), jnp.bfloat16) for part in parts for _ in range(part)]
    results = pl.pallas_call(
        partial(far_kernel, sizes, slot_count, numbers, half_places, parts, len(queries)),
        out_shape=shapes,
        in_specs=[pl.BlockSpec(memory_space=pltpu.SMEM)] + [vmem] * (1 + 2 * len(queries) + slots),
        out_specs=[vmem] * len(shapes),
        scratch_shapes=own[4:] + own[:4] * slots,
        compiler_params=pltpu.CompilerParams(vmem_limit_bytes=VMEM_LIMIT),
        cost_estimate=LIGHT,
        name="attend_far",
    )(place, table, *queries, *pairs, *groups)
    return [results[sum(parts[:slot]) : sum(parts[: slot + 1])] for slot in range(slots)]


def place_kernel(width, count, offsets_ref, *refs):
    pieces, out_ref, sems = refs[:count], refs[-2], refs[-1]
    copies = []
    for piece in pieces:
        for low in range(0, piece.shape[1], width):
            index = len(copies)
            columns = pl.ds(pl.multiple_of(offsets_ref[index], 128), width)
            copies.append(pltpu.make_async_copy(piece.at[:, low : low + width], out_ref.at[:, columns], sems.at[index]))
            copies[-1].start()
    for copy in copies:
        copy.wait()


def place_pieces(pieces, offsets, width, out_width, held=None):
    count = len(pieces)
    any_space = pl.BlockSpec(memory_space=pl.ANY)
    operands = [jnp.stack(offsets).astype(jnp.int32), *pieces]
    specs = [pl.BlockSpec(memory_space=pltpu.SMEM)] + [pl.BlockSpec(memory_space=pltpu.VMEM)] * count
    aliases = {}
    if held is not None:
        aliases = {len(operands): 0}
        operands.append(held)
        specs.append(any_space)
    return pl.pallas_call(
        partial(place_kernel, width, count),
        out_shape=jax.ShapeDtypeStruct((pieces[0].shape[0], out_width), pieces[0].dtype),
        in_specs=specs,
        out_specs=any_space,
        scratch_shapes=[pltpu.SemaphoreType.DMA((len(offsets),))],
        input_output_aliases=aliases,
        compiler_params=pltpu.CompilerParams(vmem_limit_bytes=VMEM_LIMIT),
        cost_estimate=LIGHT,
        name="place_pieces",
    )(*operands)


def after(value, *earlier):
    return lax.optimization_barrier((value, *earlier))[0]


def shards(latents, q_gain, kv_gain, q_weight, kv_weight, lengths):
    q_width, kv_width = q_gain.shape[0], kv_gain.shape[0]
    rope_width = latents.shape[1] - q_width - kv_width
    places = lax.axis_size("seq")
    parts = lax.axis_size("parts")
    half_places = places // 2
    place = lax.axis_index("seq")
    core = lax.axis_index("head")
    part = lax.axis_index("parts")
    tokens = 2 * latents.shape[0]
    local_heads = q_weight.shape[2]
    pair_width = kv_weight.shape[3]
    nope_width = q_weight.shape[3] - rope_width
    value_width = pair_width - nope_width
    block_width = local_heads * value_width
    sizes = (q_width, kv_width, nope_width, rope_width, value_width)

    def away(slot):
        return place ^ distance_of(slot, core, half_places)

    def opposite(value):
        return lax.ppermute(value, "seq", [(s, s ^ half_places) for s in range(places)])

    def across(value, slot):
        other_slot = slot if half_places < 4 else swapped_bits(slot)
        pairs = [(2 * s + c, 2 * (s ^ distance) + c) for s in range(places) for c, distance in enumerate((slot, other_slot))]
        return lax.ppermute(value, ("seq", "head"), pairs)

    def sibling(value):
        return lax.ppermute(value, "head", [(0, 1), (1, 0)])

    def other_part(value):
        return lax.ppermute(value, "parts", [(p, p ^ 1) for p in range(parts)])

    slot_count = lengths.shape[1]
    gains = jnp.concatenate([q_gain, kv_gain])
    spot = jnp.concatenate([jnp.stack([place, core]).astype(jnp.int32), jnp.reshape(lengths, -1)])
    own_query = jnp.transpose(q_weight[0], (1, 2, 0))
    own_pair = jnp.reshape(kv_weight[0], (kv_width, local_heads * pair_width))
    positions = jnp.arange(tokens, dtype=jnp.int32)[:, None].astype(jnp.float32)
    lanes = jnp.arange(nope_width, dtype=jnp.int32)[None, :]
    angles = positions * frequencies(lanes, rope_width // 2)
    signs = jnp.where(lax.rem(lanes, rope_width) < rope_width // 2, -1.0, 1.0)
    table = jnp.concatenate([jnp.cos(angles), jnp.sin(angles) * signs], axis=1)
    share = 2 if parts % 2 == 0 and local_heads % 2 == 0 else 1
    per_part = local_heads // share
    side = lax.rem(part, share)

    sent_pair = pick(own_pair, side, per_part * pair_width, 1)
    sent_query = pick(own_query, side, per_part, 0)
    latent = prepare(latents, gains, q_width, kv_width, slot_count, spot)
    same, other = [latent], [sibling(latent)]
    for distance in range(1, half_places):
        same.append(across(latent, distance) if distance & (distance - 1) == 0 else None)
    far_query = opposite(sent_query)
    far_pair = opposite(after(sent_pair, far_query))

    joined = []

    def near(distance, *earlier):
        mixed, tokens_joined = attend_near(
            (local_heads, *sizes),
            slot_count,
            distance,
            half_places,
            spot,
            table,
            own_query,
            own_pair,
            after(same[distance], *earlier),
            other[distance],
        )
        joined.append(tokens_joined)
        return mixed

    mixed = near(0)
    arrived = [mixed]
    direct = [entry for entry in same[1:] if entry is not None]
    partner = [slot if half_places < 4 else swapped_bits(slot) for slot in range(half_places)]
    for distance in range(1, half_places):
        if same[distance] is None:
            low_bit = distance & -distance
            same[distance] = across(after(same[distance ^ low_bit], mixed), low_bit)
    for distance in range(1, half_places):
        if distance & (distance - 1) == 0:
            other.append(sibling(after(same[partner[distance]], mixed, *direct)))
        else:
            other.append(None)
    for distance in range(1, half_places):
        if other[distance] is None:
            other[distance] = sibling(after(same[partner[distance]], mixed, far_query))
        mixed = near(distance, mixed)
        arrived.append(across(mixed, distance))
    placed = []
    for distance in range(half_places):
        base = away(distance) * block_width
        placed.append((arrived[distance], [base + head * value_width for head in range(local_heads)]))

    out_width = places * block_width

    def flush(held):
        offsets = [offset for piece, starts in placed for offset in starts]
        held = place_pieces([piece for piece, starts in placed], offsets, value_width, out_width, held)
        placed.clear()
        return held

    straight = (far_query, far_pair, [side * per_part + index for index in range(per_part)])
    sets = [straight]
    if share == 2:
        crossed_query, crossed_pair = other_part(far_query), other_part(after(far_pair, mixed))
        sets.append((crossed_query, crossed_pair, [(1 - side) * per_part + index for index in range(per_part)]))
    neighbours, middle = list(range(1, half_places)), half_places // 2
    calls = [(sets[:1], neighbours, 1, arrived[1:])]
    if share == 2:
        calls.append((sets[1:], list(range(middle, half_places)), 1, []))
        calls.append((sets[1:], list(range(1, middle)), per_part, []))
    calls.append((sets, [0], 1, []))
    late, sent = [], []
    for chosen, slots, parts_of, gates in calls:
        numbers = [number for _, _, some in chosen for number in some]
        mixed_some = attend_far(
            (len(numbers), *sizes),
            slot_count,
            slots,
            half_places,
            [parts_of] * len(slots),
            after(spot, mixed, *gates, *(sent if slots == [0] else [])),
            table,
            [query for query, _, _ in chosen],
            [pair for _, pair, _ in chosen],
            [joined[slot] for slot in slots],
        )
        mixed = mixed_some[0][0]
        for slot, pieces in zip(slots, mixed_some):
            base = (away(slot) ^ half_places) * block_width
            each = len(numbers) // len(pieces)
            for index, piece in enumerate(pieces):
                spans = [base + number * value_width for number in numbers[index * each : (index + 1) * each]]
                if slot:
                    piece = across(piece, slot)
                    if slots == neighbours:
                        sent.append(piece)
                (placed if slots == neighbours else late).append((piece, spans))
    held = flush(None)
    placed.extend(late)
    held = flush(held)
    return held


def solution(mesh):
    return jax.shard_map(
        shards,
        mesh=mesh,
        in_specs=(
            P(("parts", "seq", "head"), None),
            P(),
            P(),
            P("head", None, "seq", None),
            P("head", None, "seq", None),
            P("parts", None),
        ),
        out_specs=P(("parts", "seq"), "head"),
        check_vma=False,
    )
```

```python
from functools import partial
import math

import jax
import jax.numpy as jnp
from jax import lax
from jax.experimental import pallas as pl
from jax.experimental.pallas import tpu as pltpu
from jax.sharding import PartitionSpec as P

epsilon = 1e-06
VMEM_LIMIT = 20 * 1024 * 1024
LIGHT = pl.CostEstimate(flops=1024, bytes_accessed=1024, transcendentals=0)
FAR = -(2.0**100)
NT = (((1,), (1,)), ((), ()))
NN = (((1,), (0,)), ((), ()))


def frequencies(lane, half_width):
    steps = lax.rem(lane, half_width).astype(jnp.float32)
    return jnp.exp(steps * (-math.log(10000.0) / half_width))


def swapped_bits(slot):
    return (slot & ~3) | (slot & 1) << 1 | (slot & 2) >> 1


def distance_of(slot, core, half_places):
    if half_places < 4:
        return slot
    return jnp.where(core == 0, slot, swapped_bits(slot))


def prepare_kernel(q_width, kv_width, slot_count, place_ref, latents_ref, gain_ref, out_ref):
    rows = latents_ref.shape[1]
    rope_width = latents_ref.shape[0] - q_width - kv_width
    half_width = rope_width // 2

    def normalized(low, width):
        part = latents_ref[low : low + width, :].astype(jnp.float32)
        scale = lax.rsqrt(jnp.mean(part * part, axis=0, keepdims=True) + epsilon)
        return (jnp.transpose(part * scale) * gain_ref[:, low : low + width]).astype(jnp.bfloat16)

    out_ref[:, :q_width] = normalized(0, q_width)
    out_ref[:, q_width : q_width + kv_width] = normalized(q_width, kv_width)
    spare = out_ref.shape[1] - q_width - kv_width - rope_width
    token_ids = lax.broadcasted_iota(jnp.int32, (1, rows), 1) + place_ref[1] * rows
    slot_ids = lax.broadcasted_iota(jnp.int32, (spare, rows), 0)
    begin, start, inside = jnp.zeros_like(token_ids), jnp.int32(0), jnp.zeros((spare, rows), jnp.float32)
    for slot in range(slot_count):
        stop = start + place_ref[2 + place_ref[0] * slot_count + slot]
        begin = jnp.where(token_ids >= start, start, begin)
        member = jnp.where((token_ids >= start) & (token_ids < stop), 1.0, 0.0)
        inside = jnp.where(slot_ids == slot, member, inside)
        start = stop
    position = (token_ids - begin).astype(jnp.float32)
    angle = position * frequencies(lax.broadcasted_iota(jnp.int32, (half_width, rows), 0), half_width)
    cosine, sine = jnp.cos(angle), jnp.sin(angle)
    rope = latents_ref[q_width + kv_width :, :].astype(jnp.float32)
    first, second = rope[:half_width], rope[half_width:]
    turned = jnp.concatenate([first * cosine - second * sine, second * cosine + first * sine, inside], axis=0)
    out_ref[:, q_width + kv_width :] = jnp.transpose(turned).astype(jnp.bfloat16)


def prepare(latents, gains, q_width, kv_width, slot_count, place):
    rows = latents.shape[0]
    rope_width = latents.shape[1] - q_width - kv_width
    width = q_width + kv_width + -(-(rope_width + slot_count) // 128) * 128
    vmem = pl.BlockSpec(memory_space=pltpu.VMEM)
    return pl.pallas_call(
        partial(prepare_kernel, q_width, kv_width, slot_count),
        out_shape=jax.ShapeDtypeStruct((rows, width), jnp.bfloat16),
        in_specs=[pl.BlockSpec(memory_space=pltpu.SMEM), vmem, vmem],
        out_specs=vmem,
        compiler_params=pltpu.CompilerParams(vmem_limit_bytes=VMEM_LIMIT),
        cost_estimate=LIGHT,
        name="prepare",
    )(place, jnp.transpose(latents), gains[None, :])


def pick_kernel(index_ref, source_ref, out_ref):
    out_ref[...] = source_ref[...]


def pick(source, index, block, axis):
    shape = list(source.shape)
    shape[axis] = block
    out_shape = shape
    position = lambda step, index_ref: tuple(index_ref[0] if at == axis else 0 for at in range(len(shape)))
    return pl.pallas_call(
        pick_kernel,
        grid_spec=pltpu.PrefetchScalarGridSpec(
            num_scalar_prefetch=1,
            grid=(1,),
            in_specs=[pl.BlockSpec(tuple(shape), position)],
            out_specs=pl.BlockSpec(tuple(out_shape), lambda step, index_ref: (0,) * len(out_shape)),
        ),
        out_shape=jax.ShapeDtypeStruct(tuple(out_shape), source.dtype),
        compiler_params=pltpu.CompilerParams(vmem_limit_bytes=VMEM_LIMIT),
        cost_estimate=LIGHT,
        name="pick",
    )(jnp.reshape(index, (1,)).astype(jnp.int32), source)


def attend_group(sizes, chosen, tokens_ref, scratch, out_refs):
    heads, q_width, kv_width, nope_width, rope_width, value_width = sizes
    query_width, pair_width = nope_width + rope_width, nope_width + value_width
    query_ref, key_ref, value_ref, turn_ref, bias_ref = scratch
    out_heads = heads // len(out_refs)
    tokens = tokens_ref.shape[0]
    rows = bias_ref.shape[0]
    half_width = rope_width // 2
    group_heads = nope_width // rope_width
    score_scale = query_width**-0.5 * math.log2(math.e)
    lane = lax.broadcasted_iota(jnp.int32, (tokens, nope_width), 1)
    is_first = lax.rem(lane, rope_width) < half_width
    is_rope = lane < rope_width
    rope_low = q_width + kv_width
    apart = jnp.where(is_rope, 0.0, (1.0 - tokens_ref[:, rope_low:].astype(jnp.float32)) * FAR)

    def dot(left, right, dims):
        return lax.dot_general(left, right, dims, preferred_element_type=jnp.float32)

    def project(some):
        picked = [chosen[head] for head in some]
        while len(picked) < group_heads:
            picked.append(picked[-1])

        def query(low, high, picked):
            parts = [query_weight_ref[number, low:high, :] for query_weight_ref, _, number in picked]
            return dot(tokens_ref[:, :q_width], jnp.concatenate(parts, axis=0), NT)

        rope = query(nope_width, query_width, picked)
        nope = query(0, nope_width, picked[: len(some)])
        latent = tokens_ref[:, q_width:rope_low]
        pairs = [weight_ref[:, number * pair_width : (number + 1) * pair_width] for _, weight_ref, number in picked]
        pair = dot(latent, jnp.concatenate(pairs[: len(some)], axis=1), NN)
        swapped = jnp.where(is_first, pltpu.roll(rope, nope_width - half_width, 1), pltpu.roll(rope, half_width, 1))
        turned = (rope * turn_ref[:, :nope_width] + swapped * turn_ref[:, nope_width:]) * score_scale
        for index, head in enumerate(some):
            low = 2 * head * nope_width
            part = nope[:, index * nope_width : (index + 1) * nope_width]
            query_ref[:, low : low + nope_width] = (part * score_scale).astype(jnp.bfloat16)
            moved = pltpu.roll(turned, nope_width - index * rope_width, 1) if index else turned
            query_ref[:, low + nope_width : low + 2 * nope_width] = jnp.where(is_rope, moved, apart).astype(jnp.bfloat16)
            both = pair[:, index * pair_width : (index + 1) * pair_width].astype(jnp.bfloat16)
            key_ref[:, head * nope_width : (head + 1) * nope_width] = both[:, :nope_width]
            value_ref[head, :, :value_width] = both[:, nope_width:]

    def score(head, half):
        low, high = half * rows, (half + 1) * rows
        queries = query_ref[low:high, 2 * head * nope_width : (2 * head + 2) * nope_width]
        shared = tokens_ref[:high, rope_low:]
        keys = jnp.concatenate([key_ref[:high, head * nope_width : (head + 1) * nope_width], shared], axis=1)
        return dot(queries, keys, NT)

    def soften(half, scores):
        low = half * rows
        last = scores[:, low:] + bias_ref[...]
        scores = jnp.concatenate([scores[:, :low], last], axis=1) if half else last
        return jnp.exp2(scores - jnp.max(scores, axis=1, keepdims=True)).astype(jnp.bfloat16)

    def mix(head, half, terms):
        low, high = half * rows, (half + 1) * rows
        mixed = dot(terms, value_ref[head, :high, :], NN)
        column = head % out_heads * value_width
        out_refs[head // out_heads][low:high, column : column + value_width] = (
            mixed[:, :value_width] / mixed[:, value_width:]
        ).astype(jnp.bfloat16)

    batches = [list(range(heads))[low : low + group_heads] for low in range(0, heads, group_heads)]
    project(batches[0])
    yield
    terms = None
    for number, batch in enumerate(batches):
        scores = score(batch[0], 0)
        if number + 1 < len(batches):
            project(batches[number + 1])
        else:
            yield
        for head in batch:
            for half in range(2):
                ahead = (head, 1) if half == 0 else (head + 1, 0)
                following = score(*ahead) if ahead[0] in batch else None
                held = soften(half, scores)
                if terms is not None:
                    mix(*terms)
                terms = (head, half, held)
                scores = following
    yield
    mix(*terms)


def attend_groups(works):
    works = list(works)
    for index, work in enumerate(works):
        if index == 0:
            next(work)
        next(work)
        if index + 1 < len(works):
            next(works[index + 1])
        for rest in work:
            pass


def set_up(scratch, first=True):
    value_ref, bias_ref = scratch[2], scratch[4]
    rows = bias_ref.shape[0]
    heads, tokens, width = value_ref.shape
    if first:
        row_ids = lax.broadcasted_iota(jnp.int32, (rows, rows), 0)
        col_ids = lax.broadcasted_iota(jnp.int32, (rows, rows), 1)
        bias_ref[...] = jnp.where(col_ids <= row_ids, 0.0, -jnp.inf)
    for head in range(heads):
        value_ref[head, :, width // 2 :] = jnp.ones((tokens, width // 2), jnp.bfloat16)


def set_turn(group, slot_count, place_ref, table_ref, turn_ref):
    block = turn_ref.shape[0] // slot_count
    starts, start = [], jnp.int32(0)
    for index in range(slot_count):
        starts.append(start)
        start = start + place_ref[2 + group * slot_count + index]
    for index in range(slot_count):
        begin = jnp.int32(0)
        for entry in starts:
            begin = jnp.where(entry <= index * block, entry, begin)
        position = pl.multiple_of(index * block - begin, block)
        turn_ref[index * block : (index + 1) * block, :] = table_ref[pl.ds(position, block), :]


def near_kernel(sizes, slot_count, slot, half_places, place_ref, table_ref, query_weight_ref, pair_weight_ref, same_ref, other_ref, out_ref, tokens_ref, *scratch):
    core = place_ref[1]
    group = place_ref[0] ^ distance_of(slot, core, half_places)
    rows = same_ref.shape[0]
    tokens_ref[pl.ds(pl.multiple_of(core * rows, rows), rows), :] = same_ref[...]
    tokens_ref[pl.ds(pl.multiple_of((1 - core) * rows, rows), rows), :] = other_ref[...]
    set_up(scratch)
    set_turn(group, slot_count, place_ref, table_ref, scratch[3])
    chosen = [(query_weight_ref, pair_weight_ref, head) for head in range(sizes[0])]
    attend_groups([attend_group(sizes, chosen, tokens_ref, scratch, [out_ref])])


def far_kernel(sizes, slot_count, numbers, half_places, parts, arrays, place_ref, table_ref, *refs):
    slots = len(numbers)
    query_refs, pair_refs, refs = refs[:arrays], refs[arrays : 2 * arrays], refs[2 * arrays :]
    token_refs, out_refs, refs = refs[:slots], refs[slots : slots + sum(parts)], refs[slots + sum(parts) :]
    bias_ref, refs = refs[0], refs[1:]
    chosen = [(*both, number) for both in zip(query_refs, pair_refs) for number in range(both[0].shape[0])]
    works, first = [], 0
    for slot in range(slots):
        scratch = [*refs[4 * slot : 4 * slot + 4], bias_ref]
        set_up(scratch, slot == 0)
        group = place_ref[0] ^ distance_of(numbers[slot], place_ref[1], half_places)
        set_turn(group, slot_count, place_ref, table_ref, scratch[3])
        works.append(attend_group(sizes, chosen, token_refs[slot], scratch, out_refs[first : first + parts[slot]]))
        first += parts[slot]
    attend_groups(works)


def scratch_for(sizes, tokens):
    heads, q_width, kv_width, nope_width, rope_width, value_width = sizes
    return [
        pltpu.VMEM((tokens, 2 * heads * nope_width), jnp.bfloat16),
        pltpu.VMEM((tokens, heads * nope_width), jnp.bfloat16),
        pltpu.VMEM((heads, tokens, 2 * value_width), jnp.bfloat16),
        pltpu.VMEM((tokens, 2 * nope_width), jnp.float32),
        pltpu.VMEM((tokens // 2, tokens // 2), jnp.float32),
    ]


def attend_near(sizes, slot_count, slot, half_places, place, table, query_weight, pair_weight, same, other):
    rows, width = same.shape
    heads, value_width = sizes[0], sizes[-1]
    vmem = pl.BlockSpec(memory_space=pltpu.VMEM)
    return pl.pallas_call(
        partial(near_kernel, sizes, slot_count, slot, half_places),
        out_shape=[
            jax.ShapeDtypeStruct((2 * rows, heads * value_width), jnp.bfloat16),
            jax.ShapeDtypeStruct((2 * rows, width), jnp.bfloat16),
        ],
        in_specs=[pl.BlockSpec(memory_space=pltpu.SMEM)] + [vmem] * 5,
        out_specs=[vmem, vmem],
        scratch_shapes=scratch_for(sizes, 2 * rows),
        compiler_params=pltpu.CompilerParams(vmem_limit_bytes=VMEM_LIMIT),
        cost_estimate=LIGHT,
        name="attend_near",
    )(place, table, query_weight, pair_weight, same, other)


def attend_far(sizes, slot_count, numbers, half_places, parts, place, table, queries, pairs, groups):
    tokens = groups[0].shape[0]
    slots, heads, value_width = len(groups), sizes[0], sizes[-1]
    vmem = pl.BlockSpec(memory_space=pltpu.VMEM)
    own = scratch_for(sizes, tokens)
    shapes = [jax.ShapeDtypeStruct((tokens, heads // part * value_width), jnp.bfloat16) for part in parts for _ in range(part)]
    results = pl.pallas_call(
        partial(far_kernel, sizes, slot_count, numbers, half_places, parts, len(queries)),
        out_shape=shapes,
        in_specs=[pl.BlockSpec(memory_space=pltpu.SMEM)] + [vmem] * (1 + 2 * len(queries) + slots),
        out_specs=[vmem] * len(shapes),
        scratch_shapes=own[4:] + own[:4] * slots,
        compiler_params=pltpu.CompilerParams(vmem_limit_bytes=VMEM_LIMIT),
        cost_estimate=LIGHT,
        name="attend_far",
    )(place, table, *queries, *pairs, *groups)
    return [results[sum(parts[:slot]) : sum(parts[: slot + 1])] for slot in range(slots)]


def place_kernel(width, count, offsets_ref, *refs):
    pieces, out_ref, sems = refs[:count], refs[-2], refs[-1]
    copies = []
    for piece in pieces:
        for low in range(0, piece.shape[1], width):
            index = len(copies)
            columns = pl.ds(pl.multiple_of(offsets_ref[index], 128), width)
            copies.append(pltpu.make_async_copy(piece.at[:, low : low + width], out_ref.at[:, columns], sems.at[index]))
            copies[-1].start()
    for copy in copies:
        copy.wait()


def place_pieces(pieces, offsets, width, out_width, held=None):
    count = len(pieces)
    any_space = pl.BlockSpec(memory_space=pl.ANY)
    operands = [jnp.stack(offsets).astype(jnp.int32), *pieces]
    specs = [pl.BlockSpec(memory_space=pltpu.SMEM)] + [pl.BlockSpec(memory_space=pltpu.VMEM)] * count
    aliases = {}
    if held is not None:
        aliases = {len(operands): 0}
        operands.append(held)
        specs.append(any_space)
    return pl.pallas_call(
        partial(place_kernel, width, count),
        out_shape=jax.ShapeDtypeStruct((pieces[0].shape[0], out_width), pieces[0].dtype),
        in_specs=specs,
        out_specs=any_space,
        scratch_shapes=[pltpu.SemaphoreType.DMA((len(offsets),))],
        input_output_aliases=aliases,
        compiler_params=pltpu.CompilerParams(vmem_limit_bytes=VMEM_LIMIT),
        cost_estimate=LIGHT,
        name="place_pieces",
    )(*operands)


def after(value, *earlier):
    return lax.optimization_barrier((value, *earlier))[0]


def shards(latents, q_gain, kv_gain, q_weight, kv_weight, lengths):
    q_width, kv_width = q_gain.shape[0], kv_gain.shape[0]
    rope_width = latents.shape[1] - q_width - kv_width
    places = lax.axis_size("seq")
    parts = lax.axis_size("parts")
    half_places = places // 2
    place = lax.axis_index("seq")
    core = lax.axis_index("head")
    part = lax.axis_index("parts")
    tokens = 2 * latents.shape[0]
    local_heads = q_weight.shape[2]
    pair_width = kv_weight.shape[3]
    nope_width = q_weight.shape[3] - rope_width
    value_width = pair_width - nope_width
    block_width = local_heads * value_width
    sizes = (q_width, kv_width, nope_width, rope_width, value_width)

    def away(slot):
        return place ^ distance_of(slot, core, half_places)

    def opposite(value):
        return lax.ppermute(value, "seq", [(s, s ^ half_places) for s in range(places)])

    def across(value, slot):
        other_slot = slot if half_places < 4 else swapped_bits(slot)
        pairs = [(2 * s + c, 2 * (s ^ distance) + c) for s in range(places) for c, distance in enumerate((slot, other_slot))]
        return lax.ppermute(value, ("seq", "head"), pairs)

    def sibling(value):
        return lax.ppermute(value, "head", [(0, 1), (1, 0)])

    def other_part(value):
        return lax.ppermute(value, "parts", [(p, p ^ 1) for p in range(parts)])

    slot_count = lengths.shape[1]
    gains = jnp.concatenate([q_gain, kv_gain])
    spot = jnp.concatenate([jnp.stack([place, core]).astype(jnp.int32), jnp.reshape(lengths, -1)])
    own_query = jnp.transpose(q_weight[0], (1, 2, 0))
    own_pair = jnp.reshape(kv_weight[0], (kv_width, local_heads * pair_width))
    positions = jnp.arange(tokens, dtype=jnp.int32)[:, None].astype(jnp.float32)
    lanes = jnp.arange(nope_width, dtype=jnp.int32)[None, :]
    angles = positions * frequencies(lanes, rope_width // 2)
    signs = jnp.where(lax.rem(lanes, rope_width) < rope_width // 2, -1.0, 1.0)
    table = jnp.concatenate([jnp.cos(angles), jnp.sin(angles) * signs], axis=1)
    share = 2 if parts % 2 == 0 and local_heads % 2 == 0 else 1
    per_part = local_heads // share
    side = lax.rem(part, share)

    sent_pair = pick(own_pair, side, per_part * pair_width, 1)
    sent_query = pick(own_query, side, per_part, 0)
    latent = prepare(latents, gains, q_width, kv_width, slot_count, spot)
    same, other = [latent], [sibling(latent)]
    for distance in range(1, half_places):
        same.append(across(latent, distance) if distance & (distance - 1) == 0 else None)
    far_query = opposite(sent_query)
    far_pair = opposite(after(sent_pair, far_query))

    joined = []

    def near(distance, *earlier):
        mixed, tokens_joined = attend_near(
            (local_heads, *sizes),
            slot_count,
            distance,
            half_places,
            spot,
            table,
            own_query,
            own_pair,
            after(same[distance], *earlier),
            other[distance],
        )
        joined.append(tokens_joined)
        return mixed

    mixed = near(0)
    arrived = [mixed]
    direct = [entry for entry in same[1:] if entry is not None]
    partner = [slot if half_places < 4 else swapped_bits(slot) for slot in range(half_places)]
    for distance in range(1, half_places):
        if same[distance] is None:
            low_bit = distance & -distance
            same[distance] = across(after(same[distance ^ low_bit], mixed), low_bit)
    for distance in range(1, half_places):
        if distance & (distance - 1) == 0:
            other.append(sibling(after(same[partner[distance]], mixed, far_query, *direct)))
        else:
            other.append(None)
    crossed_query = [other_part(after(far_query, mixed))] if share == 2 else []
    for distance in range(1, half_places):
        if other[distance] is None:
            other[distance] = sibling(after(same[partner[distance]], mixed, far_pair, *crossed_query))
        mixed = near(distance, mixed)
        arrived.append(across(mixed, distance))
    placed = []
    for distance in range(half_places):
        base = away(distance) * block_width
        placed.append((arrived[distance], [base + head * value_width for head in range(local_heads)]))

    out_width = places * block_width

    def flush(held):
        offsets = [offset for piece, starts in placed for offset in starts]
        held = place_pieces([piece for piece, starts in placed], offsets, value_width, out_width, held)
        placed.clear()
        return held

    straight = (far_query, far_pair, [side * per_part + index for index in range(per_part)])
    sets = [straight]
    if share == 2:
        sets.append((crossed_query[0], other_part(far_pair), [(1 - side) * per_part + index for index in range(per_part)]))
    neighbours, middle = list(range(1, half_places)), half_places // 2
    calls = [(sets[:1], neighbours, 1, [])]
    if share == 2:
        calls.append((sets[1:], list(range(middle, half_places)), 1, []))
        calls.append((sets[1:], list(range(1, middle)), per_part, []))
    calls.append((sets, [0], 1, arrived[1:]))
    late, sent = [], []
    for chosen, slots, parts_of, gates in calls:
        numbers = [number for _, _, some in chosen for number in some]
        mixed_some = attend_far(
            (len(numbers), *sizes),
            slot_count,
            slots,
            half_places,
            [parts_of] * len(slots),
            after(spot, mixed, *gates, *(sent if slots == [0] else [])),
            table,
            [query for query, _, _ in chosen],
            [pair for _, pair, _ in chosen],
            [joined[slot] for slot in slots],
        )
        mixed = mixed_some[0][0]
        for slot, pieces in zip(slots, mixed_some):
            base = (away(slot) ^ half_places) * block_width
            each = len(numbers) // len(pieces)
            for index, piece in enumerate(pieces):
                spans = [base + number * value_width for number in numbers[index * each : (index + 1) * each]]
                if slot:
                    piece = across(piece, slot)
                    if slots == neighbours:
                        sent.append(piece)
                (placed if slots == neighbours else late).append((piece, spans))
    held = flush(None)
    placed.extend(late)
    held = flush(held)
    return held


def solution(mesh):
    return jax.shard_map(
        shards,
        mesh=mesh,
        in_specs=(
            P(("parts", "seq", "head"), None),
            P(),
            P(),
            P("head", None, "seq", None),
            P("head", None, "seq", None),
            P("parts", None),
        ),
        out_specs=P(("parts", "seq"), "head"),
        check_vma=False,
    )
```

```python
from functools import partial
import math

import jax
import jax.numpy as jnp
from jax import lax
from jax.experimental import pallas as pl
from jax.experimental.pallas import tpu as pltpu
from jax.sharding import PartitionSpec as P

epsilon = 1e-06
VMEM_LIMIT = 32 * 1024 * 1024
LIGHT = pl.CostEstimate(flops=1024, bytes_accessed=1024, transcendentals=0)
FAR = -(2.0**100)
NT = (((1,), (1,)), ((), ()))
NN = (((1,), (0,)), ((), ()))


def frequencies(lane, half_width):
    steps = lax.rem(lane, half_width).astype(jnp.float32)
    return jnp.exp(steps * (-math.log(10000.0) / half_width))


def swapped_bits(slot):
    return (slot & ~3) | (slot & 1) << 1 | (slot & 2) >> 1


def distance_of(slot, core, half_places):
    if half_places < 4:
        return slot
    return jnp.where(core == 0, slot, swapped_bits(slot))


def prepare_kernel(q_width, kv_width, slot_count, place_ref, latents_ref, gain_ref, out_ref):
    rows = latents_ref.shape[1]
    rope_width = latents_ref.shape[0] - q_width - kv_width
    half_width = rope_width // 2

    def normalized(low, width):
        part = latents_ref[low : low + width, :].astype(jnp.float32)
        scale = lax.rsqrt(jnp.mean(part * part, axis=0, keepdims=True) + epsilon)
        return (jnp.transpose(part * scale) * gain_ref[:, low : low + width]).astype(jnp.bfloat16)

    out_ref[:, :q_width] = normalized(0, q_width)
    out_ref[:, q_width : q_width + kv_width] = normalized(q_width, kv_width)
    spare = out_ref.shape[1] - q_width - kv_width - rope_width
    token_ids = lax.broadcasted_iota(jnp.int32, (1, rows), 1) + place_ref[1] * rows
    slot_ids = lax.broadcasted_iota(jnp.int32, (spare, rows), 0)
    begin, start, inside = jnp.zeros_like(token_ids), jnp.int32(0), jnp.zeros((spare, rows), jnp.float32)
    for slot in range(slot_count):
        stop = start + place_ref[2 + place_ref[0] * slot_count + slot]
        begin = jnp.where(token_ids >= start, start, begin)
        member = jnp.where((token_ids >= start) & (token_ids < stop), 1.0, 0.0)
        inside = jnp.where(slot_ids == slot, member, inside)
        start = stop
    position = (token_ids - begin).astype(jnp.float32)
    angle = position * frequencies(lax.broadcasted_iota(jnp.int32, (half_width, rows), 0), half_width)
    cosine, sine = jnp.cos(angle), jnp.sin(angle)
    rope = latents_ref[q_width + kv_width :, :].astype(jnp.float32)
    first, second = rope[:half_width], rope[half_width:]
    turned = jnp.concatenate([first * cosine - second * sine, second * cosine + first * sine, inside], axis=0)
    out_ref[:, q_width + kv_width :] = jnp.transpose(turned).astype(jnp.bfloat16)


def prepare(latents, gains, q_width, kv_width, slot_count, place):
    rows = latents.shape[0]
    rope_width = latents.shape[1] - q_width - kv_width
    width = q_width + kv_width + -(-(rope_width + slot_count) // 128) * 128
    vmem = pl.BlockSpec(memory_space=pltpu.VMEM)
    return pl.pallas_call(
        partial(prepare_kernel, q_width, kv_width, slot_count),
        out_shape=jax.ShapeDtypeStruct((rows, width), jnp.bfloat16),
        in_specs=[pl.BlockSpec(memory_space=pltpu.SMEM), vmem, vmem],
        out_specs=vmem,
        compiler_params=pltpu.CompilerParams(vmem_limit_bytes=VMEM_LIMIT),
        cost_estimate=LIGHT,
        name="prepare",
    )(place, jnp.transpose(latents), gains[None, :])


def pick_kernel(index_ref, source_ref, out_ref):
    out_ref[...] = source_ref[...]


def pick(source, index, block, axis):
    shape = list(source.shape)
    shape[axis] = block
    out_shape = shape
    position = lambda step, index_ref: tuple(index_ref[0] if at == axis else 0 for at in range(len(shape)))
    return pl.pallas_call(
        pick_kernel,
        grid_spec=pltpu.PrefetchScalarGridSpec(
            num_scalar_prefetch=1,
            grid=(1,),
            in_specs=[pl.BlockSpec(tuple(shape), position)],
            out_specs=pl.BlockSpec(tuple(out_shape), lambda step, index_ref: (0,) * len(out_shape)),
        ),
        out_shape=jax.ShapeDtypeStruct(tuple(out_shape), source.dtype),
        compiler_params=pltpu.CompilerParams(vmem_limit_bytes=VMEM_LIMIT),
        cost_estimate=LIGHT,
        name="pick",
    )(jnp.reshape(index, (1,)).astype(jnp.int32), source)


def attend_group(sizes, chosen, tokens_ref, scratch, out_refs):
    heads, q_width, kv_width, nope_width, rope_width, value_width = sizes
    query_width, pair_width = nope_width + rope_width, nope_width + value_width
    query_ref, key_ref, value_ref, turn_ref, bias_ref = scratch
    out_heads = heads // len(out_refs)
    tokens = tokens_ref.shape[0]
    rows = bias_ref.shape[0]
    half_width = rope_width // 2
    group_heads = nope_width // rope_width
    score_scale = query_width**-0.5 * math.log2(math.e)
    lane = lax.broadcasted_iota(jnp.int32, (tokens, nope_width), 1)
    is_first = lax.rem(lane, rope_width) < half_width
    is_rope = lane < rope_width
    rope_low = q_width + kv_width
    apart = jnp.where(is_rope, 0.0, (1.0 - tokens_ref[:, rope_low:].astype(jnp.float32)) * FAR)

    def dot(left, right, dims):
        return lax.dot_general(left, right, dims, preferred_element_type=jnp.float32)

    def project(some):
        picked = [chosen[head] for head in some]
        while len(picked) < group_heads:
            picked.append(picked[-1])

        def query(low, high, picked):
            parts = [query_weight_ref[number, low:high, :] for query_weight_ref, _, number in picked]
            return dot(tokens_ref[:, :q_width], jnp.concatenate(parts, axis=0), NT)

        rope = query(nope_width, query_width, picked)
        nope = query(0, nope_width, picked[: len(some)])
        latent = tokens_ref[:, q_width:rope_low]
        pairs = [weight_ref[:, number * pair_width : (number + 1) * pair_width] for _, weight_ref, number in picked]
        pair = dot(latent, jnp.concatenate(pairs[: len(some)], axis=1), NN)
        swapped = jnp.where(is_first, pltpu.roll(rope, nope_width - half_width, 1), pltpu.roll(rope, half_width, 1))
        turned = (rope * turn_ref[:, :nope_width] + swapped * turn_ref[:, nope_width:]) * score_scale
        for index, head in enumerate(some):
            low = 2 * head * nope_width
            part = nope[:, index * nope_width : (index + 1) * nope_width]
            query_ref[:, low : low + nope_width] = (part * score_scale).astype(jnp.bfloat16)
            moved = pltpu.roll(turned, nope_width - index * rope_width, 1) if index else turned
            query_ref[:, low + nope_width : low + 2 * nope_width] = jnp.where(is_rope, moved, apart).astype(jnp.bfloat16)
            both = pair[:, index * pair_width : (index + 1) * pair_width].astype(jnp.bfloat16)
            key_ref[:, head * nope_width : (head + 1) * nope_width] = both[:, :nope_width]
            value_ref[head, :, :value_width] = both[:, nope_width:]

    def score(head, half):
        low, high = half * rows, (half + 1) * rows
        queries = query_ref[low:high, 2 * head * nope_width : (2 * head + 2) * nope_width]
        shared = tokens_ref[:high, rope_low:]
        keys = jnp.concatenate([key_ref[:high, head * nope_width : (head + 1) * nope_width], shared], axis=1)
        return dot(queries, keys, NT)

    def soften(half, scores):
        low = half * rows
        last = scores[:, low:] + bias_ref[...]
        scores = jnp.concatenate([scores[:, :low], last], axis=1) if half else last
        return jnp.exp2(scores - jnp.max(scores, axis=1, keepdims=True)).astype(jnp.bfloat16)

    def mix(head, half, terms):
        low, high = half * rows, (half + 1) * rows
        mixed = dot(terms, value_ref[head, :high, :], NN)
        column = head % out_heads * value_width
        out_refs[head // out_heads][low:high, column : column + value_width] = (
            mixed[:, :value_width] / mixed[:, value_width:]
        ).astype(jnp.bfloat16)

    batches = [list(range(heads))[low : low + group_heads] for low in range(0, heads, group_heads)]
    project(batches[0])
    yield
    terms = None
    for number, batch in enumerate(batches):
        scores = score(batch[0], 0)
        if number + 1 < len(batches):
            project(batches[number + 1])
        else:
            yield
        for head in batch:
            for half in range(2):
                ahead = (head, 1) if half == 0 else (head + 1, 0)
                following = score(*ahead) if ahead[0] in batch else None
                held = soften(half, scores)
                if terms is not None:
                    mix(*terms)
                terms = (head, half, held)
                scores = following
    yield
    mix(*terms)


def attend_groups(works):
    works = list(works)
    for index, work in enumerate(works):
        if index == 0:
            next(work)
        next(work)
        if index + 1 < len(works):
            next(works[index + 1])
        for rest in work:
            pass


def set_up(scratch, first=True):
    value_ref, bias_ref = scratch[2], scratch[4]
    rows = bias_ref.shape[0]
    heads, tokens, width = value_ref.shape
    if first:
        row_ids = lax.broadcasted_iota(jnp.int32, (rows, rows), 0)
        col_ids = lax.broadcasted_iota(jnp.int32, (rows, rows), 1)
        bias_ref[...] = jnp.where(col_ids <= row_ids, 0.0, -jnp.inf)
    for head in range(heads):
        value_ref[head, :, width // 2 :] = jnp.ones((tokens, width // 2), jnp.bfloat16)


def set_turn(group, slot_count, place_ref, table_ref, turn_ref):
    block = turn_ref.shape[0] // slot_count
    starts, start = [], jnp.int32(0)
    for index in range(slot_count):
        starts.append(start)
        start = start + place_ref[2 + group * slot_count + index]
    for index in range(slot_count):
        begin = jnp.int32(0)
        for entry in starts:
            begin = jnp.where(entry <= index * block, entry, begin)
        position = pl.multiple_of(index * block - begin, block)
        turn_ref[index * block : (index + 1) * block, :] = table_ref[pl.ds(position, block), :]


def near_kernel(sizes, slot_count, slot, half_places, place_ref, table_ref, query_weight_ref, pair_weight_ref, same_ref, other_ref, out_ref, tokens_ref, *scratch):
    core = place_ref[1]
    group = place_ref[0] ^ distance_of(slot, core, half_places)
    rows = same_ref.shape[0]
    tokens_ref[pl.ds(pl.multiple_of(core * rows, rows), rows), :] = same_ref[...]
    tokens_ref[pl.ds(pl.multiple_of((1 - core) * rows, rows), rows), :] = other_ref[...]
    set_up(scratch)
    set_turn(group, slot_count, place_ref, table_ref, scratch[3])
    chosen = [(query_weight_ref, pair_weight_ref, head) for head in range(sizes[0])]
    attend_groups([attend_group(sizes, chosen, tokens_ref, scratch, [out_ref])])


def far_kernel(sizes, slot_count, numbers, half_places, parts, arrays, place_ref, table_ref, *refs):
    slots = len(numbers)
    query_refs, pair_refs, refs = refs[:arrays], refs[arrays : 2 * arrays], refs[2 * arrays :]
    token_refs, out_refs, refs = refs[:slots], refs[slots : slots + sum(parts)], refs[slots + sum(parts) :]
    bias_ref, refs = refs[0], refs[1:]
    chosen = [(*both, number) for both in zip(query_refs, pair_refs) for number in range(both[0].shape[0])]
    works, first = [], 0
    for slot in range(slots):
        scratch = [*refs[4 * slot : 4 * slot + 4], bias_ref]
        set_up(scratch, slot == 0)
        group = place_ref[0] ^ distance_of(numbers[slot], place_ref[1], half_places)
        set_turn(group, slot_count, place_ref, table_ref, scratch[3])
        works.append(attend_group(sizes, chosen, token_refs[slot], scratch, out_refs[first : first + parts[slot]]))
        first += parts[slot]
    attend_groups(works)


def scratch_for(sizes, tokens):
    heads, q_width, kv_width, nope_width, rope_width, value_width = sizes
    return [
        pltpu.VMEM((tokens, 2 * heads * nope_width), jnp.bfloat16),
        pltpu.VMEM((tokens, heads * nope_width), jnp.bfloat16),
        pltpu.VMEM((heads, tokens, 2 * value_width), jnp.bfloat16),
        pltpu.VMEM((tokens, 2 * nope_width), jnp.float32),
        pltpu.VMEM((tokens // 2, tokens // 2), jnp.float32),
    ]


def attend_near(sizes, slot_count, slot, half_places, place, table, query_weight, pair_weight, same, other):
    rows, width = same.shape
    heads, value_width = sizes[0], sizes[-1]
    vmem = pl.BlockSpec(memory_space=pltpu.VMEM)
    return pl.pallas_call(
        partial(near_kernel, sizes, slot_count, slot, half_places),
        out_shape=[
            jax.ShapeDtypeStruct((2 * rows, heads * value_width), jnp.bfloat16),
            jax.ShapeDtypeStruct((2 * rows, width), jnp.bfloat16),
        ],
        in_specs=[pl.BlockSpec(memory_space=pltpu.SMEM)] + [vmem] * 5,
        out_specs=[vmem, vmem],
        scratch_shapes=scratch_for(sizes, 2 * rows),
        compiler_params=pltpu.CompilerParams(vmem_limit_bytes=VMEM_LIMIT),
        cost_estimate=LIGHT,
        name="attend_near",
    )(place, table, query_weight, pair_weight, same, other)


def attend_far(sizes, slot_count, numbers, half_places, parts, place, table, queries, pairs, groups):
    tokens = groups[0].shape[0]
    slots, heads, value_width = len(groups), sizes[0], sizes[-1]
    vmem = pl.BlockSpec(memory_space=pltpu.VMEM)
    own = scratch_for(sizes, tokens)
    shapes = [jax.ShapeDtypeStruct((tokens, heads // part * value_width), jnp.bfloat16) for part in parts for _ in range(part)]
    results = pl.pallas_call(
        partial(far_kernel, sizes, slot_count, numbers, half_places, parts, len(queries)),
        out_shape=shapes,
        in_specs=[pl.BlockSpec(memory_space=pltpu.SMEM)] + [vmem] * (1 + 2 * len(queries) + slots),
        out_specs=[vmem] * len(shapes),
        scratch_shapes=own[4:] + own[:4] * slots,
        compiler_params=pltpu.CompilerParams(vmem_limit_bytes=VMEM_LIMIT),
        cost_estimate=LIGHT,
        name="attend_far",
    )(place, table, *queries, *pairs, *groups)
    return [results[sum(parts[:slot]) : sum(parts[: slot + 1])] for slot in range(slots)]


def place_kernel(width, count, offsets_ref, *refs):
    pieces, out_ref, sems = refs[:count], refs[-2], refs[-1]
    copies = []
    for piece in pieces:
        for low in range(0, piece.shape[1], width):
            index = len(copies)
            columns = pl.ds(pl.multiple_of(offsets_ref[index], 128), width)
            copies.append(pltpu.make_async_copy(piece.at[:, low : low + width], out_ref.at[:, columns], sems.at[index]))
            copies[-1].start()
    for copy in copies:
        copy.wait()


def place_pieces(pieces, offsets, width, out_width, held=None):
    count = len(pieces)
    any_space = pl.BlockSpec(memory_space=pl.ANY)
    operands = [jnp.stack(offsets).astype(jnp.int32), *pieces]
    specs = [pl.BlockSpec(memory_space=pltpu.SMEM)] + [pl.BlockSpec(memory_space=pltpu.VMEM)] * count
    aliases = {}
    if held is not None:
        aliases = {len(operands): 0}
        operands.append(held)
        specs.append(any_space)
    return pl.pallas_call(
        partial(place_kernel, width, count),
        out_shape=jax.ShapeDtypeStruct((pieces[0].shape[0], out_width), pieces[0].dtype),
        in_specs=specs,
        out_specs=any_space,
        scratch_shapes=[pltpu.SemaphoreType.DMA((len(offsets),))],
        input_output_aliases=aliases,
        compiler_params=pltpu.CompilerParams(vmem_limit_bytes=VMEM_LIMIT),
        cost_estimate=LIGHT,
        name="place_pieces",
    )(*operands)


def after(value, *earlier):
    return lax.optimization_barrier((value, *earlier))[0]


def shards(latents, q_gain, kv_gain, q_weight, kv_weight, lengths):
    q_width, kv_width = q_gain.shape[0], kv_gain.shape[0]
    rope_width = latents.shape[1] - q_width - kv_width
    places = lax.axis_size("seq")
    parts = lax.axis_size("parts")
    half_places = places // 2
    place = lax.axis_index("seq")
    core = lax.axis_index("head")
    part = lax.axis_index("parts")
    tokens = 2 * latents.shape[0]
    local_heads = q_weight.shape[2]
    pair_width = kv_weight.shape[3]
    nope_width = q_weight.shape[3] - rope_width
    value_width = pair_width - nope_width
    block_width = local_heads * value_width
    sizes = (q_width, kv_width, nope_width, rope_width, value_width)

    def away(slot):
        return place ^ distance_of(slot, core, half_places)

    def opposite(value):
        return lax.ppermute(value, "seq", [(s, s ^ half_places) for s in range(places)])

    def across(value, slot):
        other_slot = slot if half_places < 4 else swapped_bits(slot)
        pairs = [(2 * s + c, 2 * (s ^ distance) + c) for s in range(places) for c, distance in enumerate((slot, other_slot))]
        return lax.ppermute(value, ("seq", "head"), pairs)

    def sibling(value):
        return lax.ppermute(value, "head", [(0, 1), (1, 0)])

    def other_part(value):
        return lax.ppermute(value, "parts", [(p, p ^ 1) for p in range(parts)])

    slot_count = lengths.shape[1]
    gains = jnp.concatenate([q_gain, kv_gain])
    spot = jnp.concatenate([jnp.stack([place, core]).astype(jnp.int32), jnp.reshape(lengths, -1)])
    own_query = jnp.transpose(q_weight[0], (1, 2, 0))
    own_pair = jnp.reshape(kv_weight[0], (kv_width, local_heads * pair_width))
    positions = jnp.arange(tokens, dtype=jnp.int32)[:, None].astype(jnp.float32)
    lanes = jnp.arange(nope_width, dtype=jnp.int32)[None, :]
    angles = positions * frequencies(lanes, rope_width // 2)
    signs = jnp.where(lax.rem(lanes, rope_width) < rope_width // 2, -1.0, 1.0)
    table = jnp.concatenate([jnp.cos(angles), jnp.sin(angles) * signs], axis=1)
    share = 2 if parts % 2 == 0 and local_heads % 2 == 0 else 1
    per_part = local_heads // share
    side = lax.rem(part, share)

    sent_pair = pick(own_pair, side, per_part * pair_width, 1)
    sent_query = pick(own_query, side, per_part, 0)
    latent = prepare(latents, gains, q_width, kv_width, slot_count, spot)
    same, other = [latent], [sibling(latent)]
    for distance in range(1, half_places):
        same.append(across(latent, distance) if distance & (distance - 1) == 0 else None)
    far_query = opposite(sent_query)
    far_pair = opposite(after(sent_pair, far_query))

    joined = []

    def near(distance, *earlier):
        mixed, tokens_joined = attend_near(
            (local_heads, *sizes),
            slot_count,
            distance,
            half_places,
            spot,
            table,
            own_query,
            own_pair,
            after(same[distance], *earlier),
            other[distance],
        )
        joined.append(tokens_joined)
        return mixed

    mixed = near(0)
    arrived = [mixed]
    direct = [entry for entry in same[1:] if entry is not None]
    partner = [slot if half_places < 4 else swapped_bits(slot) for slot in range(half_places)]
    for distance in range(1, half_places):
        if same[distance] is None:
            low_bit = distance & -distance
            same[distance] = across(after(same[distance ^ low_bit], mixed), low_bit)
    for distance in range(1, half_places):
        if distance & (distance - 1) == 0:
            other.append(sibling(after(same[partner[distance]], mixed, far_query, *direct)))
        else:
            other.append(None)
    crossed_query = [other_part(after(far_query, mixed))] if share == 2 else []
    for distance in range(1, half_places):
        if other[distance] is None:
            other[distance] = sibling(after(same[partner[distance]], mixed, far_pair, *crossed_query))
        mixed = near(distance, mixed)
        arrived.append(across(mixed, distance))
    placed = []
    for distance in range(half_places):
        base = away(distance) * block_width
        placed.append((arrived[distance], [base + head * value_width for head in range(local_heads)]))

    out_width = places * block_width

    def flush(held):
        offsets = [offset for piece, starts in placed for offset in starts]
        held = place_pieces([piece for piece, starts in placed], offsets, value_width, out_width, held)
        placed.clear()
        return held

    queries, pairs = [far_query], [far_pair]
    numbers = [side * per_part + index for index in range(per_part)]
    if share == 2:
        queries.append(crossed_query[0])
        pairs.append(other_part(far_pair))
        numbers += [(1 - side) * per_part + index for index in range(per_part)]
    late, gates = [], []
    for distances in (list(range(half_places // 2, half_places)), list(range(1, half_places // 2)), [0]):
        if not distances:
            continue
        parts_of = [share if 0 < distance < half_places // 2 else 1 for distance in distances]
        mixed_some = attend_far(
            (len(numbers), *sizes),
            slot_count,
            distances,
            half_places,
            parts_of,
            after(spot, mixed, *gates),
            table,
            queries,
            pairs,
            [joined[distance] for distance in distances],
        )
        mixed, gates = mixed_some[0][0], [] if gates else arrived[1:]
        for distance, pieces in zip(distances, mixed_some):
            base = (away(distance) ^ half_places) * block_width
            each = len(numbers) // len(pieces)
            for index, piece in enumerate(pieces):
                spans = [base + number * value_width for number in numbers[index * each : (index + 1) * each]]
                (late if distance else placed).append((across(piece, distance) if distance else piece, spans))
    held = flush(None)
    placed.extend(late)
    held = flush(held)
    return held


def solution(mesh):
    return jax.shard_map(
        shards,
        mesh=mesh,
        in_specs=(
            P(("parts", "seq", "head"), None),
            P(),
            P(),
            P("head", None, "seq", None),
            P("head", None, "seq", None),
            P("parts", None),
        ),
        out_specs=P(("parts", "seq"), "head"),
        check_vma=False,
    )
```

```python
from functools import partial
import math

import jax
import jax.numpy as jnp
from jax import lax
from jax.experimental import pallas as pl
from jax.experimental.pallas import tpu as pltpu
from jax.sharding import PartitionSpec as P

epsilon = 1e-06
VMEM_LIMIT = 14 * 1024 * 1024
VMEM_SMALL = 8 * 1024 * 1024
LIGHT = pl.CostEstimate(flops=1024, bytes_accessed=1024, transcendentals=0)
FAR = -(2.0**100)
NT = (((1,), (1,)), ((), ()))
NN = (((1,), (0,)), ((), ()))


def frequencies(lane, half_width):
    steps = lax.rem(lane, half_width).astype(jnp.float32)
    return jnp.exp(steps * (-math.log(10000.0) / half_width))


def swapped_bits(slot):
    return (slot & ~3) | (slot & 1) << 1 | (slot & 2) >> 1


def distance_of(slot, core, half_places):
    if half_places < 4:
        return slot
    return jnp.where(core == 0, slot, swapped_bits(slot))


def prepare_kernel(q_width, kv_width, slot_count, place_ref, latents_ref, gain_ref, out_ref):
    rows = latents_ref.shape[1]
    rope_width = latents_ref.shape[0] - q_width - kv_width
    half_width = rope_width // 2

    def normalized(low, width):
        part = latents_ref[low : low + width, :].astype(jnp.float32)
        scale = lax.rsqrt(jnp.mean(part * part, axis=0, keepdims=True) + epsilon)
        return (jnp.transpose(part * scale) * gain_ref[:, low : low + width]).astype(jnp.bfloat16)

    out_ref[:, :q_width] = normalized(0, q_width)
    out_ref[:, q_width : q_width + kv_width] = normalized(q_width, kv_width)
    spare = out_ref.shape[1] - q_width - kv_width - rope_width
    token_ids = lax.broadcasted_iota(jnp.int32, (1, rows), 1) + place_ref[1] * rows
    slot_ids = lax.broadcasted_iota(jnp.int32, (spare, rows), 0)
    begin, start, inside = jnp.zeros_like(token_ids), jnp.int32(0), jnp.zeros((spare, rows), jnp.float32)
    for slot in range(slot_count):
        stop = start + place_ref[2 + place_ref[0] * slot_count + slot]
        begin = jnp.where(token_ids >= start, start, begin)
        member = jnp.where((token_ids >= start) & (token_ids < stop), 1.0, 0.0)
        inside = jnp.where(slot_ids == slot, member, inside)
        start = stop
    position = (token_ids - begin).astype(jnp.float32)
    angle = position * frequencies(lax.broadcasted_iota(jnp.int32, (half_width, rows), 0), half_width)
    cosine, sine = jnp.cos(angle), jnp.sin(angle)
    rope = latents_ref[q_width + kv_width :, :].astype(jnp.float32)
    first, second = rope[:half_width], rope[half_width:]
    turned = jnp.concatenate([first * cosine - second * sine, second * cosine + first * sine, inside], axis=0)
    out_ref[:, q_width + kv_width :] = jnp.transpose(turned).astype(jnp.bfloat16)


def prepare(latents, gains, q_width, kv_width, slot_count, place):
    rows = latents.shape[0]
    rope_width = latents.shape[1] - q_width - kv_width
    width = q_width + kv_width + -(-(rope_width + slot_count) // 128) * 128
    vmem = pl.BlockSpec(memory_space=pltpu.VMEM)
    return pl.pallas_call(
        partial(prepare_kernel, q_width, kv_width, slot_count),
        out_shape=jax.ShapeDtypeStruct((rows, width), jnp.bfloat16),
        in_specs=[pl.BlockSpec(memory_space=pltpu.SMEM), vmem, vmem],
        out_specs=vmem,
        compiler_params=pltpu.CompilerParams(vmem_limit_bytes=VMEM_SMALL),
        cost_estimate=LIGHT,
        name="prepare",
    )(place, jnp.transpose(latents), gains[None, :])


def pick_kernel(index_ref, source_ref, out_ref):
    out_ref[...] = source_ref[...]


def pick(source, index, block, axis):
    shape = list(source.shape)
    shape[axis] = block
    out_shape = shape
    position = lambda step, index_ref: tuple(index_ref[0] if at == axis else 0 for at in range(len(shape)))
    return pl.pallas_call(
        pick_kernel,
        grid_spec=pltpu.PrefetchScalarGridSpec(
            num_scalar_prefetch=1,
            grid=(1,),
            in_specs=[pl.BlockSpec(tuple(shape), position)],
            out_specs=pl.BlockSpec(tuple(out_shape), lambda step, index_ref: (0,) * len(out_shape)),
        ),
        out_shape=jax.ShapeDtypeStruct(tuple(out_shape), source.dtype),
        compiler_params=pltpu.CompilerParams(vmem_limit_bytes=VMEM_SMALL),
        cost_estimate=LIGHT,
        name="pick",
    )(jnp.reshape(index, (1,)).astype(jnp.int32), source)


def attend_group(sizes, chosen, tokens_ref, scratch, out_refs):
    heads, q_width, kv_width, nope_width, rope_width, value_width = sizes
    query_width, pair_width = nope_width + rope_width, nope_width + value_width
    query_ref, key_ref, value_ref, turn_ref, bias_ref = scratch
    out_heads = heads // len(out_refs)
    tokens = tokens_ref.shape[0]
    rows = bias_ref.shape[0]
    half_width = rope_width // 2
    group_heads = nope_width // rope_width
    score_scale = query_width**-0.5 * math.log2(math.e)
    lane = lax.broadcasted_iota(jnp.int32, (tokens, nope_width), 1)
    is_first = lax.rem(lane, rope_width) < half_width
    is_rope = lane < rope_width
    rope_low = q_width + kv_width
    apart = jnp.where(is_rope, 0.0, (1.0 - tokens_ref[:, rope_low:].astype(jnp.float32)) * FAR)

    def dot(left, right, dims):
        return lax.dot_general(left, right, dims, preferred_element_type=jnp.float32)

    def project(some):
        picked = [chosen[head] for head in some]
        while len(picked) < group_heads:
            picked.append(picked[-1])

        def query(low, high, picked):
            parts = [query_weight_ref[number, low:high, :] for query_weight_ref, _, number in picked]
            return dot(tokens_ref[:, :q_width], jnp.concatenate(parts, axis=0), NT)

        rope = query(nope_width, query_width, picked)
        nope = query(0, nope_width, picked[: len(some)])
        latent = tokens_ref[:, q_width:rope_low]
        pairs = [weight_ref[:, number * pair_width : (number + 1) * pair_width] for _, weight_ref, number in picked]
        pair = dot(latent, jnp.concatenate(pairs[: len(some)], axis=1), NN)
        swapped = jnp.where(is_first, pltpu.roll(rope, nope_width - half_width, 1), pltpu.roll(rope, half_width, 1))
        turned = (rope * turn_ref[:, :nope_width] + swapped * turn_ref[:, nope_width:]) * score_scale
        for index, head in enumerate(some):
            low = 2 * head * nope_width
            part = nope[:, index * nope_width : (index + 1) * nope_width]
            query_ref[:, low : low + nope_width] = (part * score_scale).astype(jnp.bfloat16)
            moved = pltpu.roll(turned, nope_width - index * rope_width, 1) if index else turned
            query_ref[:, low + nope_width : low + 2 * nope_width] = jnp.where(is_rope, moved, apart).astype(jnp.bfloat16)
            both = pair[:, index * pair_width : (index + 1) * pair_width].astype(jnp.bfloat16)
            key_ref[:, head * nope_width : (head + 1) * nope_width] = both[:, :nope_width]
            value_ref[head, :, :value_width] = both[:, nope_width:]

    def score(head, half):
        low, high = half * rows, (half + 1) * rows
        queries = query_ref[low:high, 2 * head * nope_width : (2 * head + 2) * nope_width]
        shared = tokens_ref[:high, rope_low:]
        keys = jnp.concatenate([key_ref[:high, head * nope_width : (head + 1) * nope_width], shared], axis=1)
        return dot(queries, keys, NT)

    def soften(half, scores):
        low = half * rows
        last = scores[:, low:] + bias_ref[...]
        scores = jnp.concatenate([scores[:, :low], last], axis=1) if half else last
        return jnp.exp2(scores - jnp.max(scores, axis=1, keepdims=True)).astype(jnp.bfloat16)

    def mix(head, half, terms):
        low, high = half * rows, (half + 1) * rows
        mixed = dot(terms, value_ref[head, :high, :], NN)
        column = head % out_heads * value_width
        out_refs[head // out_heads][low:high, column : column + value_width] = (
            mixed[:, :value_width] / mixed[:, value_width:]
        ).astype(jnp.bfloat16)

    batches = [list(range(heads))[low : low + group_heads] for low in range(0, heads, group_heads)]
    project(batches[0])
    yield
    terms = None
    for number, batch in enumerate(batches):
        scores = score(batch[0], 0)
        if number + 1 < len(batches):
            project(batches[number + 1])
        else:
            yield
        for head in batch:
            for half in range(2):
                ahead = (head, 1) if half == 0 else (head + 1, 0)
                following = score(*ahead) if ahead[0] in batch else None
                held = soften(half, scores)
                if terms is not None:
                    mix(*terms)
                terms = (head, half, held)
                scores = following
    yield
    mix(*terms)


def attend_groups(works):
    works = list(works)
    for index, work in enumerate(works):
        if index == 0:
            next(work)
        next(work)
        if index + 1 < len(works):
            next(works[index + 1])
        for rest in work:
            pass


def set_up(scratch, first=True):
    value_ref, bias_ref = scratch[2], scratch[4]
    rows = bias_ref.shape[0]
    heads, tokens, width = value_ref.shape
    if first:
        row_ids = lax.broadcasted_iota(jnp.int32, (rows, rows), 0)
        col_ids = lax.broadcasted_iota(jnp.int32, (rows, rows), 1)
        bias_ref[...] = jnp.where(col_ids <= row_ids, 0.0, -jnp.inf)
    for head in range(heads):
        value_ref[head, :, width // 2 :] = jnp.ones((tokens, width // 2), jnp.bfloat16)


def set_turn(group, slot_count, place_ref, table_ref, turn_ref):
    block = turn_ref.shape[0] // slot_count
    starts, start = [], jnp.int32(0)
    for index in range(slot_count):
        starts.append(start)
        start = start + place_ref[2 + group * slot_count + index]
    for index in range(slot_count):
        begin = jnp.int32(0)
        for entry in starts:
            begin = jnp.where(entry <= index * block, entry, begin)
        position = pl.multiple_of(index * block - begin, block)
        turn_ref[index * block : (index + 1) * block, :] = table_ref[pl.ds(position, block), :]


def near_kernel(sizes, slot_count, slot, half_places, place_ref, table_ref, query_weight_ref, pair_weight_ref, same_ref, other_ref, out_ref, tokens_ref, *scratch):
    core = place_ref[1]
    group = place_ref[0] ^ distance_of(slot, core, half_places)
    rows = same_ref.shape[0]
    tokens_ref[pl.ds(pl.multiple_of(core * rows, rows), rows), :] = same_ref[...]
    tokens_ref[pl.ds(pl.multiple_of((1 - core) * rows, rows), rows), :] = other_ref[...]
    set_up(scratch)
    set_turn(group, slot_count, place_ref, table_ref, scratch[3])
    chosen = [(query_weight_ref, pair_weight_ref, head) for head in range(sizes[0])]
    attend_groups([attend_group(sizes, chosen, tokens_ref, scratch, [out_ref])])


def far_kernel(sizes, slot_count, numbers, half_places, parts, arrays, place_ref, table_ref, *refs):
    slots = len(numbers)
    query_refs, pair_refs, refs = refs[:arrays], refs[arrays : 2 * arrays], refs[2 * arrays :]
    token_refs, out_refs, refs = refs[:slots], refs[slots : slots + sum(parts)], refs[slots + sum(parts) :]
    bias_ref, refs = refs[0], refs[1:]
    chosen = [(*both, number) for both in zip(query_refs, pair_refs) for number in range(both[0].shape[0])]
    works, first = [], 0
    for slot in range(slots):
        scratch = [*refs[4 * slot : 4 * slot + 4], bias_ref]
        set_up(scratch, slot == 0)
        group = place_ref[0] ^ distance_of(numbers[slot], place_ref[1], half_places)
        set_turn(group, slot_count, place_ref, table_ref, scratch[3])
        works.append(attend_group(sizes, chosen, token_refs[slot], scratch, out_refs[first : first + parts[slot]]))
        first += parts[slot]
    attend_groups(works)


def scratch_for(sizes, tokens):
    heads, q_width, kv_width, nope_width, rope_width, value_width = sizes
    return [
        pltpu.VMEM((tokens, 2 * heads * nope_width), jnp.bfloat16),
        pltpu.VMEM((tokens, heads * nope_width), jnp.bfloat16),
        pltpu.VMEM((heads, tokens, 2 * value_width), jnp.bfloat16),
        pltpu.VMEM((tokens, 2 * nope_width), jnp.float32),
        pltpu.VMEM((tokens // 2, tokens // 2), jnp.float32),
    ]


def attend_near(sizes, slot_count, slot, half_places, place, table, query_weight, pair_weight, same, other):
    rows, width = same.shape
    heads, value_width = sizes[0], sizes[-1]
    vmem = pl.BlockSpec(memory_space=pltpu.VMEM)
    return pl.pallas_call(
        partial(near_kernel, sizes, slot_count, slot, half_places),
        out_shape=[
            jax.ShapeDtypeStruct((2 * rows, heads * value_width), jnp.bfloat16),
            jax.ShapeDtypeStruct((2 * rows, width), jnp.bfloat16),
        ],
        in_specs=[pl.BlockSpec(memory_space=pltpu.SMEM)] + [vmem] * 5,
        out_specs=[vmem, vmem],
        scratch_shapes=scratch_for(sizes, 2 * rows),
        compiler_params=pltpu.CompilerParams(vmem_limit_bytes=VMEM_LIMIT),
        cost_estimate=LIGHT,
        name="attend_near",
    )(place, table, query_weight, pair_weight, same, other)


def attend_far(sizes, slot_count, numbers, half_places, parts, place, table, queries, pairs, groups):
    tokens = groups[0].shape[0]
    slots, heads, value_width = len(groups), sizes[0], sizes[-1]
    vmem = pl.BlockSpec(memory_space=pltpu.VMEM)
    own = scratch_for(sizes, tokens)
    shapes = [jax.ShapeDtypeStruct((tokens, heads // part * value_width), jnp.bfloat16) for part in parts for _ in range(part)]
    results = pl.pallas_call(
        partial(far_kernel, sizes, slot_count, numbers, half_places, parts, len(queries)),
        out_shape=shapes,
        in_specs=[pl.BlockSpec(memory_space=pltpu.SMEM)] + [vmem] * (1 + 2 * len(queries) + slots),
        out_specs=[vmem] * len(shapes),
        scratch_shapes=own[4:] + own[:4] * slots,
        compiler_params=pltpu.CompilerParams(vmem_limit_bytes=VMEM_LIMIT),
        cost_estimate=LIGHT,
        name="attend_far",
    )(place, table, *queries, *pairs, *groups)
    return [results[sum(parts[:slot]) : sum(parts[: slot + 1])] for slot in range(slots)]


def place_kernel(width, count, offsets_ref, *refs):
    pieces, out_ref, sems = refs[:count], refs[-2], refs[-1]
    copies = []
    for piece in pieces:
        for low in range(0, piece.shape[1], width):
            index = len(copies)
            columns = pl.ds(pl.multiple_of(offsets_ref[index], 128), width)
            copies.append(pltpu.make_async_copy(piece.at[:, low : low + width], out_ref.at[:, columns], sems.at[index]))
            copies[-1].start()
    for copy in copies:
        copy.wait()


def place_pieces(pieces, offsets, width, out_width, held=None):
    count = len(pieces)
    any_space = pl.BlockSpec(memory_space=pl.ANY)
    operands = [jnp.stack(offsets).astype(jnp.int32), *pieces]
    specs = [pl.BlockSpec(memory_space=pltpu.SMEM)] + [pl.BlockSpec(memory_space=pltpu.VMEM)] * count
    aliases = {}
    if held is not None:
        aliases = {len(operands): 0}
        operands.append(held)
        specs.append(any_space)
    return pl.pallas_call(
        partial(place_kernel, width, count),
        out_shape=jax.ShapeDtypeStruct((pieces[0].shape[0], out_width), pieces[0].dtype),
        in_specs=specs,
        out_specs=any_space,
        scratch_shapes=[pltpu.SemaphoreType.DMA((len(offsets),))],
        input_output_aliases=aliases,
        compiler_params=pltpu.CompilerParams(vmem_limit_bytes=VMEM_SMALL),
        cost_estimate=LIGHT,
        name="place_pieces",
    )(*operands)


def after(value, *earlier):
    return lax.optimization_barrier((value, *earlier))[0]


def shards(latents, q_gain, kv_gain, q_weight, kv_weight, lengths):
    q_width, kv_width = q_gain.shape[0], kv_gain.shape[0]
    rope_width = latents.shape[1] - q_width - kv_width
    places = lax.axis_size("seq")
    parts = lax.axis_size("parts")
    half_places = places // 2
    place = lax.axis_index("seq")
    core = lax.axis_index("head")
    part = lax.axis_index("parts")
    tokens = 2 * latents.shape[0]
    local_heads = q_weight.shape[2]
    pair_width = kv_weight.shape[3]
    nope_width = q_weight.shape[3] - rope_width
    value_width = pair_width - nope_width
    block_width = local_heads * value_width
    sizes = (q_width, kv_width, nope_width, rope_width, value_width)

    def away(slot):
        return place ^ distance_of(slot, core, half_places)

    def opposite(value):
        return lax.ppermute(value, "seq", [(s, s ^ half_places) for s in range(places)])

    def across(value, slot):
        other_slot = slot if half_places < 4 else swapped_bits(slot)
        pairs = [(2 * s + c, 2 * (s ^ distance) + c) for s in range(places) for c, distance in enumerate((slot, other_slot))]
        return lax.ppermute(value, ("seq", "head"), pairs)

    def sibling(value):
        return lax.ppermute(value, "head", [(0, 1), (1, 0)])

    def other_part(value):
        return lax.ppermute(value, "parts", [(p, p ^ 1) for p in range(parts)])

    slot_count = lengths.shape[1]
    gains = jnp.concatenate([q_gain, kv_gain])
    spot = jnp.concatenate([jnp.stack([place, core]).astype(jnp.int32), jnp.reshape(lengths, -1)])
    own_query = jnp.transpose(q_weight[0], (1, 2, 0))
    own_pair = jnp.reshape(kv_weight[0], (kv_width, local_heads * pair_width))
    positions = jnp.arange(tokens, dtype=jnp.int32)[:, None].astype(jnp.float32)
    lanes = jnp.arange(nope_width, dtype=jnp.int32)[None, :]
    angles = positions * frequencies(lanes, rope_width // 2)
    signs = jnp.where(lax.rem(lanes, rope_width) < rope_width // 2, -1.0, 1.0)
    table = jnp.concatenate([jnp.cos(angles), jnp.sin(angles) * signs], axis=1)
    share = 2 if parts % 2 == 0 and local_heads % 2 == 0 else 1
    per_part = local_heads // share
    side = lax.rem(part, share)

    sent_pair = pick(own_pair, side, per_part * pair_width, 1)
    sent_query = pick(own_query, side, per_part, 0)
    latent = prepare(latents, gains, q_width, kv_width, slot_count, spot)
    same, other = [latent], [sibling(latent)]
    for distance in range(1, half_places):
        same.append(across(latent, distance) if distance & (distance - 1) == 0 else None)
    far_query = opposite(sent_query)
    far_pair = opposite(after(sent_pair, far_query))

    joined = []

    def near(distance, *earlier):
        mixed, tokens_joined = attend_near(
            (local_heads, *sizes),
            slot_count,
            distance,
            half_places,
            spot,
            table,
            own_query,
            own_pair,
            after(same[distance], *earlier),
            other[distance],
        )
        joined.append(tokens_joined)
        return mixed

    mixed = near(0)
    arrived = [mixed]
    direct = [entry for entry in same[1:] if entry is not None]
    partner = [slot if half_places < 4 else swapped_bits(slot) for slot in range(half_places)]
    for distance in range(1, half_places):
        if same[distance] is None:
            low_bit = distance & -distance
            same[distance] = across(after(same[distance ^ low_bit], mixed), low_bit)
    for distance in range(1, half_places):
        if distance & (distance - 1) == 0:
            other.append(sibling(after(same[partner[distance]], mixed, far_query, *direct)))
        else:
            other.append(None)
    crossed_query = [other_part(after(far_query, mixed))] if share == 2 else []
    for distance in range(1, half_places):
        if other[distance] is None:
            other[distance] = sibling(after(same[partner[distance]], mixed, far_pair, *crossed_query))
        mixed = near(distance, mixed)
        arrived.append(across(mixed, distance))
    placed = []
    for distance in range(half_places):
        base = away(distance) * block_width
        placed.append((arrived[distance], [base + head * value_width for head in range(local_heads)]))

    out_width = places * block_width

    def flush(held):
        offsets = [offset for piece, starts in placed for offset in starts]
        held = place_pieces([piece for piece, starts in placed], offsets, value_width, out_width, held)
        placed.clear()
        return held

    queries, pairs = [far_query], [far_pair]
    numbers = [side * per_part + index for index in range(per_part)]
    if share == 2:
        queries.append(crossed_query[0])
        pairs.append(other_part(far_pair))
        numbers += [(1 - side) * per_part + index for index in range(per_part)]
    late, gates = [], []
    for distances in (list(range(half_places // 2, half_places)), list(range(1, half_places // 2)), [0]):
        if not distances:
            continue
        parts_of = [share if 0 < distance < half_places // 2 else 1 for distance in distances]
        mixed_some = attend_far(
            (len(numbers), *sizes),
            slot_count,
            distances,
            half_places,
            parts_of,
            after(spot, mixed, *gates),
            table,
            queries,
            pairs,
            [joined[distance] for distance in distances],
        )
        mixed, gates = mixed_some[0][0], [] if gates else arrived[1:]
        for distance, pieces in zip(distances, mixed_some):
            base = (away(distance) ^ half_places) * block_width
            each = len(numbers) // len(pieces)
            for index, piece in enumerate(pieces):
                spans = [base + number * value_width for number in numbers[index * each : (index + 1) * each]]
                (late if distance else placed).append((across(piece, distance) if distance else piece, spans))
    held = flush(None)
    placed.extend(late)
    held = flush(held)
    return held


def solution(mesh):
    return jax.shard_map(
        shards,
        mesh=mesh,
        in_specs=(
            P(("parts", "seq", "head"), None),
            P(),
            P(),
            P("head", None, "seq", None),
            P("head", None, "seq", None),
            P("parts", None),
        ),
        out_specs=P(("parts", "seq"), "head"),
        check_vma=False,
    )
```

```python
from functools import partial
import math

import jax
import jax.numpy as jnp
from jax import lax
from jax.experimental import pallas as pl
from jax.experimental.pallas import tpu as pltpu
from jax.sharding import PartitionSpec as P

epsilon = 1e-06
VMEM_LIMIT = 32 * 1024 * 1024
LIGHT = pl.CostEstimate(flops=1024, bytes_accessed=1024, transcendentals=0)
FAR = -(2.0**100)
NT = (((1,), (1,)), ((), ()))
NN = (((1,), (0,)), ((), ()))


def frequencies(lane, half_width):
    steps = lax.rem(lane, half_width).astype(jnp.float32)
    return jnp.exp(steps * (-math.log(10000.0) / half_width))


def swapped_bits(slot):
    return (slot & ~3) | (slot & 1) << 1 | (slot & 2) >> 1


def distance_of(slot, core, half_places):
    if half_places < 4:
        return slot
    return jnp.where(core == 0, slot, swapped_bits(slot))


def prepare_kernel(q_width, kv_width, slot_count, place_ref, latents_ref, gain_ref, out_ref):
    rows = latents_ref.shape[1]
    rope_width = latents_ref.shape[0] - q_width - kv_width
    half_width = rope_width // 2

    def normalized(low, width):
        part = latents_ref[low : low + width, :].astype(jnp.float32)
        scale = lax.rsqrt(jnp.mean(part * part, axis=0, keepdims=True) + epsilon)
        return (jnp.transpose(part * scale) * gain_ref[:, low : low + width]).astype(jnp.bfloat16)

    out_ref[:, :q_width] = normalized(0, q_width)
    out_ref[:, q_width : q_width + kv_width] = normalized(q_width, kv_width)
    spare = out_ref.shape[1] - q_width - kv_width - rope_width
    token_ids = lax.broadcasted_iota(jnp.int32, (1, rows), 1) + place_ref[1] * rows
    slot_ids = lax.broadcasted_iota(jnp.int32, (spare, rows), 0)
    begin, start, inside = jnp.zeros_like(token_ids), jnp.int32(0), jnp.zeros((spare, rows), jnp.float32)
    for slot in range(slot_count):
        stop = start + place_ref[2 + place_ref[0] * slot_count + slot]
        begin = jnp.where(token_ids >= start, start, begin)
        member = jnp.where((token_ids >= start) & (token_ids < stop), 1.0, 0.0)
        inside = jnp.where(slot_ids == slot, member, inside)
        start = stop
    position = (token_ids - begin).astype(jnp.float32)
    angle = position * frequencies(lax.broadcasted_iota(jnp.int32, (half_width, rows), 0), half_width)
    cosine, sine = jnp.cos(angle), jnp.sin(angle)
    rope = latents_ref[q_width + kv_width :, :].astype(jnp.float32)
    first, second = rope[:half_width], rope[half_width:]
    turned = jnp.concatenate([first * cosine - second * sine, second * cosine + first * sine, inside], axis=0)
    out_ref[:, q_width + kv_width :] = jnp.transpose(turned).astype(jnp.bfloat16)


def prepare(latents, gains, q_width, kv_width, slot_count, place):
    rows = latents.shape[0]
    rope_width = latents.shape[1] - q_width - kv_width
    width = q_width + kv_width + -(-(rope_width + slot_count) // 128) * 128
    vmem = pl.BlockSpec(memory_space=pltpu.VMEM)
    return pl.pallas_call(
        partial(prepare_kernel, q_width, kv_width, slot_count),
        out_shape=jax.ShapeDtypeStruct((rows, width), jnp.bfloat16),
        in_specs=[pl.BlockSpec(memory_space=pltpu.SMEM), vmem, vmem],
        out_specs=vmem,
        compiler_params=pltpu.CompilerParams(vmem_limit_bytes=VMEM_LIMIT),
        cost_estimate=LIGHT,
        name="prepare",
    )(place, jnp.transpose(latents), gains[None, :])


def pick_kernel(index_ref, source_ref, out_ref):
    out_ref[...] = source_ref[...]


def pick(source, index, block, axis):
    shape = list(source.shape)
    shape[axis] = block
    out_shape = shape
    position = lambda step, index_ref: tuple(index_ref[0] if at == axis else 0 for at in range(len(shape)))
    return pl.pallas_call(
        pick_kernel,
        grid_spec=pltpu.PrefetchScalarGridSpec(
            num_scalar_prefetch=1,
            grid=(1,),
            in_specs=[pl.BlockSpec(tuple(shape), position)],
            out_specs=pl.BlockSpec(tuple(out_shape), lambda step, index_ref: (0,) * len(out_shape)),
        ),
        out_shape=jax.ShapeDtypeStruct(tuple(out_shape), source.dtype),
        compiler_params=pltpu.CompilerParams(vmem_limit_bytes=VMEM_LIMIT),
        cost_estimate=LIGHT,
        name="pick",
    )(jnp.reshape(index, (1,)).astype(jnp.int32), source)


def attend_group(sizes, chosen, tokens_ref, scratch, out_refs):
    heads, q_width, kv_width, nope_width, rope_width, value_width = sizes
    query_width, pair_width = nope_width + rope_width, nope_width + value_width
    query_ref, key_ref, value_ref, turn_ref, bias_ref = scratch
    out_heads = heads // len(out_refs)
    tokens = tokens_ref.shape[0]
    rows = bias_ref.shape[0]
    half_width = rope_width // 2
    group_heads = nope_width // rope_width
    score_scale = query_width**-0.5 * math.log2(math.e)
    lane = lax.broadcasted_iota(jnp.int32, (tokens, nope_width), 1)
    is_first = lax.rem(lane, rope_width) < half_width
    is_rope = lane < rope_width
    rope_low = q_width + kv_width
    apart = jnp.where(is_rope, 0.0, (1.0 - tokens_ref[:, rope_low:].astype(jnp.float32)) * FAR)

    def dot(left, right, dims):
        return lax.dot_general(left, right, dims, preferred_element_type=jnp.float32)

    def project(some):
        picked = [chosen[head] for head in some]
        while len(picked) < group_heads:
            picked.append(picked[-1])

        def query(low, high, picked):
            parts = [query_weight_ref[number, low:high, :] for query_weight_ref, _, number in picked]
            return dot(tokens_ref[:, :q_width], jnp.concatenate(parts, axis=0), NT)

        rope = query(nope_width, query_width, picked)
        nope = query(0, nope_width, picked[: len(some)])
        latent = tokens_ref[:, q_width:rope_low]
        pairs = [weight_ref[:, number * pair_width : (number + 1) * pair_width] for _, weight_ref, number in picked]
        pair = dot(latent, jnp.concatenate(pairs[: len(some)], axis=1), NN)
        swapped = jnp.where(is_first, pltpu.roll(rope, nope_width - half_width, 1), pltpu.roll(rope, half_width, 1))
        turned = (rope * turn_ref[:, :nope_width] + swapped * turn_ref[:, nope_width:]) * score_scale
        for index, head in enumerate(some):
            low = 2 * head * nope_width
            part = nope[:, index * nope_width : (index + 1) * nope_width]
            query_ref[:, low : low + nope_width] = (part * score_scale).astype(jnp.bfloat16)
            moved = pltpu.roll(turned, nope_width - index * rope_width, 1) if index else turned
            query_ref[:, low + nope_width : low + 2 * nope_width] = jnp.where(is_rope, moved, apart).astype(jnp.bfloat16)
            both = pair[:, index * pair_width : (index + 1) * pair_width].astype(jnp.bfloat16)
            key_ref[:, head * nope_width : (head + 1) * nope_width] = both[:, :nope_width]
            value_ref[head, :, :value_width] = both[:, nope_width:]

    def score(head, half):
        low, high = half * rows, (half + 1) * rows
        queries = query_ref[low:high, 2 * head * nope_width : (2 * head + 2) * nope_width]
        shared = tokens_ref[:high, rope_low:]
        keys = jnp.concatenate([key_ref[:high, head * nope_width : (head + 1) * nope_width], shared], axis=1)
        return dot(queries, keys, NT)

    def soften(half, scores):
        low = half * rows
        last = scores[:, low:] + bias_ref[...]
        scores = jnp.concatenate([scores[:, :low], last], axis=1) if half else last
        return jnp.exp2(scores - jnp.max(scores, axis=1, keepdims=True)).astype(jnp.bfloat16)

    def mix(head, half, terms):
        low, high = half * rows, (half + 1) * rows
        mixed = dot(terms, value_ref[head, :high, :], NN)
        column = head % out_heads * value_width
        out_refs[head // out_heads][low:high, column : column + value_width] = (
            mixed[:, :value_width] / mixed[:, value_width:]
        ).astype(jnp.bfloat16)

    batches = [list(range(heads))[low : low + group_heads] for low in range(0, heads, group_heads)]
    project(batches[0])
    yield
    terms = None
    for number, batch in enumerate(batches):
        scores = score(batch[0], 0)
        if number + 1 < len(batches):
            project(batches[number + 1])
        else:
            yield
        for head in batch:
            for half in range(2):
                ahead = (head, 1) if half == 0 else (head + 1, 0)
                following = score(*ahead) if ahead[0] in batch else None
                held = soften(half, scores)
                if terms is not None:
                    mix(*terms)
                terms = (head, half, held)
                scores = following
    yield
    mix(*terms)


def attend_groups(works):
    works = list(works)
    for index, work in enumerate(works):
        if index == 0:
            next(work)
        next(work)
        if index + 1 < len(works):
            next(works[index + 1])
        for rest in work:
            pass


def set_up(scratch, first=True):
    value_ref, bias_ref = scratch[2], scratch[4]
    rows = bias_ref.shape[0]
    heads, tokens, width = value_ref.shape
    if first:
        row_ids = lax.broadcasted_iota(jnp.int32, (rows, rows), 0)
        col_ids = lax.broadcasted_iota(jnp.int32, (rows, rows), 1)
        bias_ref[...] = jnp.where(col_ids <= row_ids, 0.0, -jnp.inf)
    for head in range(heads):
        value_ref[head, :, width // 2 :] = jnp.ones((tokens, width // 2), jnp.bfloat16)


def set_turn(group, slot_count, place_ref, table_ref, turn_ref):
    block = turn_ref.shape[0] // slot_count
    starts, start = [], jnp.int32(0)
    for index in range(slot_count):
        starts.append(start)
        start = start + place_ref[2 + group * slot_count + index]
    for index in range(slot_count):
        begin = jnp.int32(0)
        for entry in starts:
            begin = jnp.where(entry <= index * block, entry, begin)
        position = pl.multiple_of(index * block - begin, block)
        turn_ref[index * block : (index + 1) * block, :] = table_ref[pl.ds(position, block), :]


def near_kernel(sizes, slot_count, slot, half_places, parts, place_ref, table_ref, query_weight_ref, pair_weight_ref, same_ref, other_ref, *refs):
    out_refs, tokens_ref, scratch = refs[:parts], refs[parts], refs[parts + 1 :]
    core = place_ref[1]
    group = place_ref[0] ^ distance_of(slot, core, half_places)
    rows = same_ref.shape[0]
    tokens_ref[pl.ds(pl.multiple_of(core * rows, rows), rows), :] = same_ref[...]
    tokens_ref[pl.ds(pl.multiple_of((1 - core) * rows, rows), rows), :] = other_ref[...]
    set_up(scratch)
    set_turn(group, slot_count, place_ref, table_ref, scratch[3])
    chosen = [(query_weight_ref, pair_weight_ref, head) for head in range(sizes[0])]
    attend_groups([attend_group(sizes, chosen, tokens_ref, scratch, out_refs)])


def far_kernel(sizes, slot_count, numbers, half_places, parts, arrays, place_ref, table_ref, *refs):
    slots = len(numbers)
    query_refs, pair_refs, refs = refs[:arrays], refs[arrays : 2 * arrays], refs[2 * arrays :]
    token_refs, out_refs, refs = refs[:slots], refs[slots : slots + sum(parts)], refs[slots + sum(parts) :]
    bias_ref, refs = refs[0], refs[1:]
    chosen = [(*both, number) for both in zip(query_refs, pair_refs) for number in range(both[0].shape[0])]
    works, first = [], 0
    for slot in range(slots):
        scratch = [*refs[4 * slot : 4 * slot + 4], bias_ref]
        set_up(scratch, slot == 0)
        group = place_ref[0] ^ distance_of(numbers[slot], place_ref[1], half_places)
        set_turn(group, slot_count, place_ref, table_ref, scratch[3])
        works.append(attend_group(sizes, chosen, token_refs[slot], scratch, out_refs[first : first + parts[slot]]))
        first += parts[slot]
    attend_groups(works)


def scratch_for(sizes, tokens):
    heads, q_width, kv_width, nope_width, rope_width, value_width = sizes
    return [
        pltpu.VMEM((tokens, 2 * heads * nope_width), jnp.bfloat16),
        pltpu.VMEM((tokens, heads * nope_width), jnp.bfloat16),
        pltpu.VMEM((heads, tokens, 2 * value_width), jnp.bfloat16),
        pltpu.VMEM((tokens, 2 * nope_width), jnp.float32),
        pltpu.VMEM((tokens // 2, tokens // 2), jnp.float32),
    ]


def attend_near(sizes, slot_count, slot, half_places, parts, place, table, query_weight, pair_weight, same, other):
    rows, width = same.shape
    heads, value_width = sizes[0], sizes[-1]
    vmem = pl.BlockSpec(memory_space=pltpu.VMEM)
    return pl.pallas_call(
        partial(near_kernel, sizes, slot_count, slot, half_places, parts),
        out_shape=[jax.ShapeDtypeStruct((2 * rows, heads // parts * value_width), jnp.bfloat16)] * parts
        + [jax.ShapeDtypeStruct((2 * rows, width), jnp.bfloat16)],
        in_specs=[pl.BlockSpec(memory_space=pltpu.SMEM)] + [vmem] * 5,
        out_specs=[vmem] * (parts + 1),
        scratch_shapes=scratch_for(sizes, 2 * rows),
        compiler_params=pltpu.CompilerParams(vmem_limit_bytes=VMEM_LIMIT),
        cost_estimate=LIGHT,
        name="attend_near",
    )(place, table, query_weight, pair_weight, same, other)


def attend_far(sizes, slot_count, numbers, half_places, parts, place, table, queries, pairs, groups):
    tokens = groups[0].shape[0]
    slots, heads, value_width = len(groups), sizes[0], sizes[-1]
    vmem = pl.BlockSpec(memory_space=pltpu.VMEM)
    own = scratch_for(sizes, tokens)
    shapes = [jax.ShapeDtypeStruct((tokens, heads // part * value_width), jnp.bfloat16) for part in parts for _ in range(part)]
    results = pl.pallas_call(
        partial(far_kernel, sizes, slot_count, numbers, half_places, parts, len(queries)),
        out_shape=shapes,
        in_specs=[pl.BlockSpec(memory_space=pltpu.SMEM)] + [vmem] * (1 + 2 * len(queries) + slots),
        out_specs=[vmem] * len(shapes),
        scratch_shapes=own[4:] + own[:4] * slots,
        compiler_params=pltpu.CompilerParams(vmem_limit_bytes=VMEM_LIMIT),
        cost_estimate=LIGHT,
        name="attend_far",
    )(place, table, *queries, *pairs, *groups)
    return [results[sum(parts[:slot]) : sum(parts[: slot + 1])] for slot in range(slots)]


def place_kernel(width, count, offsets_ref, *refs):
    pieces, out_ref, held, in_sems, out_sems = refs[:count], refs[-3 - count], refs[-2 - count : -2], refs[-2], refs[-1]
    fetches, copies = [], []
    for index, (piece, held_ref) in enumerate(zip(pieces, held)):
        fetches.append(pltpu.make_async_copy(piece, held_ref, in_sems.at[index]))
        fetches[-1].start()
    for fetch, held_ref in zip(fetches, held):
        fetch.wait()
        for low in range(0, held_ref.shape[1], width):
            index = len(copies)
            columns = pl.ds(pl.multiple_of(offsets_ref[index], 128), width)
            source = held_ref.at[:, low : low + width]
            copies.append(pltpu.make_async_copy(source, out_ref.at[:, columns], out_sems.at[index]))
            copies[-1].start()
    for copy in copies:
        copy.wait()


def place_pieces(pieces, offsets, width, out_width, held=None):
    count = len(pieces)
    any_space = pl.BlockSpec(memory_space=pl.ANY)
    operands = [jnp.stack(offsets).astype(jnp.int32), *pieces]
    aliases = {}
    if held is not None:
        aliases = {len(operands): 0}
        operands.append(held)
    return pl.pallas_call(
        partial(place_kernel, width, count),
        out_shape=jax.ShapeDtypeStruct((pieces[0].shape[0], out_width), pieces[0].dtype),
        in_specs=[pl.BlockSpec(memory_space=pltpu.SMEM)] + [any_space] * (len(operands) - 1),
        out_specs=any_space,
        scratch_shapes=[pltpu.VMEM(piece.shape, piece.dtype) for piece in pieces]
        + [pltpu.SemaphoreType.DMA((count,)), pltpu.SemaphoreType.DMA((len(offsets),))],
        input_output_aliases=aliases,
        compiler_params=pltpu.CompilerParams(vmem_limit_bytes=VMEM_LIMIT),
        cost_estimate=LIGHT,
        name="place_pieces",
    )(*operands)


def after(value, *earlier):
    return lax.optimization_barrier((value, *earlier))[0]


def shards(latents, q_gain, kv_gain, q_weight, kv_weight, lengths):
    q_width, kv_width = q_gain.shape[0], kv_gain.shape[0]
    rope_width = latents.shape[1] - q_width - kv_width
    places = lax.axis_size("seq")
    parts = lax.axis_size("parts")
    half_places = places // 2
    place = lax.axis_index("seq")
    core = lax.axis_index("head")
    part = lax.axis_index("parts")
    tokens = 2 * latents.shape[0]
    local_heads = q_weight.shape[2]
    pair_width = kv_weight.shape[3]
    nope_width = q_weight.shape[3] - rope_width
    value_width = pair_width - nope_width
    block_width = local_heads * value_width
    sizes = (q_width, kv_width, nope_width, rope_width, value_width)

    def away(slot):
        return place ^ distance_of(slot, core, half_places)

    def opposite(value):
        return lax.ppermute(value, "seq", [(s, s ^ half_places) for s in range(places)])

    def across(value, slot):
        other_slot = slot if half_places < 4 else swapped_bits(slot)
        pairs = [(2 * s + c, 2 * (s ^ distance) + c) for s in range(places) for c, distance in enumerate((slot, other_slot))]
        return lax.ppermute(value, ("seq", "head"), pairs)

    def sibling(value):
        return lax.ppermute(value, "head", [(0, 1), (1, 0)])

    def other_part(value):
        return lax.ppermute(value, "parts", [(p, p ^ 1) for p in range(parts)])

    slot_count = lengths.shape[1]
    gains = jnp.concatenate([q_gain, kv_gain])
    spot = jnp.concatenate([jnp.stack([place, core]).astype(jnp.int32), jnp.reshape(lengths, -1)])
    own_query = jnp.transpose(q_weight[0], (1, 2, 0))
    own_pair = jnp.reshape(kv_weight[0], (kv_width, local_heads * pair_width))
    positions = jnp.arange(tokens, dtype=jnp.int32)[:, None].astype(jnp.float32)
    lanes = jnp.arange(nope_width, dtype=jnp.int32)[None, :]
    angles = positions * frequencies(lanes, rope_width // 2)
    signs = jnp.where(lax.rem(lanes, rope_width) < rope_width // 2, -1.0, 1.0)
    table = jnp.concatenate([jnp.cos(angles), jnp.sin(angles) * signs], axis=1)
    share = 2 if parts % 2 == 0 and local_heads % 2 == 0 else 1
    per_part = local_heads // share
    side = lax.rem(part, share)

    sent_pair = pick(own_pair, side, per_part * pair_width, 1)
    sent_query = pick(own_query, side, per_part, 0)
    latent = prepare(latents, gains, q_width, kv_width, slot_count, spot)
    same, other = [latent], [sibling(latent)]
    for distance in range(1, half_places):
        same.append(across(latent, distance) if distance & (distance - 1) == 0 else None)
    far_query = opposite(sent_query)
    far_pair = opposite(after(sent_pair, far_query))

    joined = []

    def near(distance, *earlier):
        parts_of = share if distance == 1 else 1
        *mixed, tokens_joined = attend_near(
            (local_heads, *sizes),
            slot_count,
            distance,
            half_places,
            parts_of,
            spot,
            table,
            own_query,
            own_pair,
            after(same[distance], *earlier),
            other[distance],
        )
        joined.append(tokens_joined)
        return mixed

    mixed = near(0)
    arrived = [mixed]
    mixed = mixed[0]
    direct = [entry for entry in same[1:] if entry is not None]
    partner = [slot if half_places < 4 else swapped_bits(slot) for slot in range(half_places)]
    for distance in range(1, half_places):
        if same[distance] is None:
            low_bit = distance & -distance
            same[distance] = across(after(same[distance ^ low_bit], mixed), low_bit)
    for distance in range(1, half_places):
        if distance & (distance - 1) == 0:
            other.append(sibling(after(same[partner[distance]], mixed, far_query, *direct)))
        else:
            other.append(None)
    crossed_query = [other_part(after(far_query, mixed))] if share == 2 else []
    for distance in range(1, half_places):
        if other[distance] is None:
            other[distance] = sibling(after(same[partner[distance]], mixed, far_pair, *crossed_query, *early))
        pieces = near(distance, mixed)
        mixed = pieces[-1]
        arrived.append([across(piece, distance) for piece in pieces])
        early = arrived[1]
    placed = []
    for distance in range(half_places):
        base = away(distance) * block_width
        each = local_heads // len(arrived[distance])
        for index, piece in enumerate(arrived[distance]):
            placed.append((piece, [base + (index * each + head) * value_width for head in range(each)]))

    out_width = places * block_width

    def flush(held):
        offsets = [offset for piece, starts in placed for offset in starts]
        held = place_pieces([piece for piece, starts in placed], offsets, value_width, out_width, held)
        placed.clear()
        return held

    queries, pairs = [far_query], [far_pair]
    numbers = [side * per_part + index for index in range(per_part)]
    if share == 2:
        queries.append(crossed_query[0])
        pairs.append(other_part(far_pair))
        numbers += [(1 - side) * per_part + index for index in range(per_part)]
    late, gates = [], []
    for distances in (list(range(half_places // 2, half_places)), list(range(1, half_places // 2)) + [0]):
        parts_of = [share if 0 < distance < half_places // 2 else 1 for distance in distances]
        mixed_some = attend_far(
            (len(numbers), *sizes),
            slot_count,
            distances,
            half_places,
            parts_of,
            after(spot, mixed, *gates),
            table,
            queries,
            pairs,
            [joined[distance] for distance in distances],
        )
        mixed, gates = mixed_some[0][0], [piece for pieces in arrived[1:] for piece in pieces]
        for distance, pieces in zip(distances, mixed_some):
            base = (away(distance) ^ half_places) * block_width
            each = len(numbers) // len(pieces)
            for index, piece in enumerate(pieces):
                spans = [base + number * value_width for number in numbers[index * each : (index + 1) * each]]
                late.append((across(piece, distance) if distance else piece, spans))
    held = flush(None)
    placed.extend(late)
    held = flush(held)
    return held


def solution(mesh):
    return jax.shard_map(
        shards,
        mesh=mesh,
        in_specs=(
            P(("parts", "seq", "head"), None),
            P(),
            P(),
            P("head", None, "seq", None),
            P("head", None, "seq", None),
            P("parts", None),
        ),
        out_specs=P(("parts", "seq"), "head"),
        check_vma=False,
    )
```

```python
from functools import partial
import math

import jax
import jax.numpy as jnp
from jax import lax
from jax.experimental import pallas as pl
from jax.experimental.pallas import tpu as pltpu
from jax.sharding import PartitionSpec as P

epsilon = 1e-06
VMEM_LIMIT = 32 * 1024 * 1024
LIGHT = pl.CostEstimate(flops=1024, bytes_accessed=1024, transcendentals=0)
FAR = -(2.0**100)
NT = (((1,), (1,)), ((), ()))
NN = (((1,), (0,)), ((), ()))


def frequencies(lane, half_width):
    steps = lax.rem(lane, half_width).astype(jnp.float32)
    return jnp.exp(steps * (-math.log(10000.0) / half_width))


def swapped_bits(slot):
    return (slot & ~3) | (slot & 1) << 1 | (slot & 2) >> 1


def distance_of(slot, core, half_places):
    if half_places < 4:
        return slot
    return jnp.where(core == 0, slot, swapped_bits(slot))


def prepare_kernel(q_width, kv_width, slot_count, place_ref, latents_ref, gain_ref, out_ref):
    rows = latents_ref.shape[1]
    rope_width = latents_ref.shape[0] - q_width - kv_width
    half_width = rope_width // 2

    def normalized(low, width):
        part = latents_ref[low : low + width, :].astype(jnp.float32)
        scale = lax.rsqrt(jnp.mean(part * part, axis=0, keepdims=True) + epsilon)
        return (jnp.transpose(part * scale) * gain_ref[:, low : low + width]).astype(jnp.bfloat16)

    out_ref[:, :q_width] = normalized(0, q_width)
    out_ref[:, q_width : q_width + kv_width] = normalized(q_width, kv_width)
    spare = out_ref.shape[1] - q_width - kv_width - rope_width
    token_ids = lax.broadcasted_iota(jnp.int32, (1, rows), 1) + place_ref[1] * rows
    slot_ids = lax.broadcasted_iota(jnp.int32, (spare, rows), 0)
    begin, start, inside = jnp.zeros_like(token_ids), jnp.int32(0), jnp.zeros((spare, rows), jnp.float32)
    for slot in range(slot_count):
        stop = start + place_ref[2 + place_ref[0] * slot_count + slot]
        begin = jnp.where(token_ids >= start, start, begin)
        member = jnp.where((token_ids >= start) & (token_ids < stop), 1.0, 0.0)
        inside = jnp.where(slot_ids == slot, member, inside)
        start = stop
    position = (token_ids - begin).astype(jnp.float32)
    angle = position * frequencies(lax.broadcasted_iota(jnp.int32, (half_width, rows), 0), half_width)
    cosine, sine = jnp.cos(angle), jnp.sin(angle)
    rope = latents_ref[q_width + kv_width :, :].astype(jnp.float32)
    first, second = rope[:half_width], rope[half_width:]
    turned = jnp.concatenate([first * cosine - second * sine, second * cosine + first * sine, inside], axis=0)
    out_ref[:, q_width + kv_width :] = jnp.transpose(turned).astype(jnp.bfloat16)


def prepare(latents, gains, q_width, kv_width, slot_count, place):
    rows = latents.shape[0]
    rope_width = latents.shape[1] - q_width - kv_width
    width = q_width + kv_width + -(-(rope_width + slot_count) // 128) * 128
    vmem = pl.BlockSpec(memory_space=pltpu.VMEM)
    return pl.pallas_call(
        partial(prepare_kernel, q_width, kv_width, slot_count),
        out_shape=jax.ShapeDtypeStruct((rows, width), jnp.bfloat16),
        in_specs=[pl.BlockSpec(memory_space=pltpu.SMEM), vmem, vmem],
        out_specs=vmem,
        compiler_params=pltpu.CompilerParams(vmem_limit_bytes=VMEM_LIMIT),
        cost_estimate=LIGHT,
        name="prepare",
    )(place, jnp.transpose(latents), gains[None, :])


def pick_kernel(index_ref, source_ref, out_ref):
    out_ref[...] = source_ref[...]


def pick(source, index, block, axis):
    shape = list(source.shape)
    shape[axis] = block
    out_shape = shape
    position = lambda step, index_ref: tuple(index_ref[0] if at == axis else 0 for at in range(len(shape)))
    return pl.pallas_call(
        pick_kernel,
        grid_spec=pltpu.PrefetchScalarGridSpec(
            num_scalar_prefetch=1,
            grid=(1,),
            in_specs=[pl.BlockSpec(tuple(shape), position)],
            out_specs=pl.BlockSpec(tuple(out_shape), lambda step, index_ref: (0,) * len(out_shape)),
        ),
        out_shape=jax.ShapeDtypeStruct(tuple(out_shape), source.dtype),
        compiler_params=pltpu.CompilerParams(vmem_limit_bytes=VMEM_LIMIT),
        cost_estimate=LIGHT,
        name="pick",
    )(jnp.reshape(index, (1,)).astype(jnp.int32), source)


def attend_group(sizes, chosen, tokens_ref, scratch, out_refs):
    heads, q_width, kv_width, nope_width, rope_width, value_width = sizes
    query_width, pair_width = nope_width + rope_width, nope_width + value_width
    query_ref, key_ref, value_ref, turn_ref, bias_ref = scratch
    out_heads = heads // len(out_refs)
    tokens = tokens_ref.shape[0]
    rows = bias_ref.shape[0]
    half_width = rope_width // 2
    group_heads = nope_width // rope_width
    score_scale = query_width**-0.5 * math.log2(math.e)
    lane = lax.broadcasted_iota(jnp.int32, (tokens, nope_width), 1)
    is_first = lax.rem(lane, rope_width) < half_width
    is_rope = lane < rope_width
    rope_low = q_width + kv_width
    apart = jnp.where(is_rope, 0.0, (1.0 - tokens_ref[:, rope_low:].astype(jnp.float32)) * FAR)

    def dot(left, right, dims):
        return lax.dot_general(left, right, dims, preferred_element_type=jnp.float32)

    def project(some):
        picked = [chosen[head] for head in some]
        while len(picked) < group_heads:
            picked.append(picked[-1])

        def query(low, high, picked):
            parts = [query_weight_ref[number, low:high, :] for query_weight_ref, _, number in picked]
            return dot(tokens_ref[:, :q_width], jnp.concatenate(parts, axis=0), NT)

        rope = query(nope_width, query_width, picked)
        nope = query(0, nope_width, picked[: len(some)])
        latent = tokens_ref[:, q_width:rope_low]
        pairs = [weight_ref[:, number * pair_width : (number + 1) * pair_width] for _, weight_ref, number in picked]
        pair = dot(latent, jnp.concatenate(pairs[: len(some)], axis=1), NN)
        swapped = jnp.where(is_first, pltpu.roll(rope, nope_width - half_width, 1), pltpu.roll(rope, half_width, 1))
        turned = (rope * turn_ref[:, :nope_width] + swapped * turn_ref[:, nope_width:]) * score_scale
        for index, head in enumerate(some):
            low = 2 * head * nope_width
            part = nope[:, index * nope_width : (index + 1) * nope_width]
            query_ref[:, low : low + nope_width] = (part * score_scale).astype(jnp.bfloat16)
            moved = pltpu.roll(turned, nope_width - index * rope_width, 1) if index else turned
            query_ref[:, low + nope_width : low + 2 * nope_width] = jnp.where(is_rope, moved, apart).astype(jnp.bfloat16)
            both = pair[:, index * pair_width : (index + 1) * pair_width].astype(jnp.bfloat16)
            key_ref[:, head * nope_width : (head + 1) * nope_width] = both[:, :nope_width]
            value_ref[head, :, :value_width] = both[:, nope_width:]

    def score(head, half):
        low, high = half * rows, (half + 1) * rows
        queries = query_ref[low:high, 2 * head * nope_width : (2 * head + 2) * nope_width]
        shared = tokens_ref[:high, rope_low:]
        keys = jnp.concatenate([key_ref[:high, head * nope_width : (head + 1) * nope_width], shared], axis=1)
        return dot(queries, keys, NT)

    def soften(half, scores):
        low = half * rows
        last = scores[:, low:] + bias_ref[...]
        scores = jnp.concatenate([scores[:, :low], last], axis=1) if half else last
        return jnp.exp2(scores - jnp.max(scores, axis=1, keepdims=True)).astype(jnp.bfloat16)

    def mix(head, half, terms):
        low, high = half * rows, (half + 1) * rows
        mixed = dot(terms, value_ref[head, :high, :], NN)
        column = head % out_heads * value_width
        out_refs[head // out_heads][low:high, column : column + value_width] = (
            mixed[:, :value_width] / mixed[:, value_width:]
        ).astype(jnp.bfloat16)

    batches = [list(range(heads))[low : low + group_heads] for low in range(0, heads, group_heads)]
    project(batches[0])
    yield
    terms = None
    for number, batch in enumerate(batches):
        scores = score(batch[0], 0)
        if number + 1 < len(batches):
            project(batches[number + 1])
        else:
            yield
        for head in batch:
            for half in range(2):
                ahead = (head, 1) if half == 0 else (head + 1, 0)
                following = score(*ahead) if ahead[0] in batch else None
                held = soften(half, scores)
                if terms is not None:
                    mix(*terms)
                terms = (head, half, held)
                scores = following
    yield
    mix(*terms)


def attend_groups(works):
    works = list(works)
    for index, work in enumerate(works):
        if index == 0:
            next(work)
        next(work)
        if index + 1 < len(works):
            next(works[index + 1])
        for rest in work:
            pass


def set_up(scratch, first=True):
    value_ref, bias_ref = scratch[2], scratch[4]
    rows = bias_ref.shape[0]
    heads, tokens, width = value_ref.shape
    if first:
        row_ids = lax.broadcasted_iota(jnp.int32, (rows, rows), 0)
        col_ids = lax.broadcasted_iota(jnp.int32, (rows, rows), 1)
        bias_ref[...] = jnp.where(col_ids <= row_ids, 0.0, -jnp.inf)
    for head in range(heads):
        value_ref[head, :, width // 2 :] = jnp.ones((tokens, width // 2), jnp.bfloat16)


def set_turn(group, slot_count, place_ref, table_ref, turn_ref):
    block = turn_ref.shape[0] // slot_count
    starts, start = [], jnp.int32(0)
    for index in range(slot_count):
        starts.append(start)
        start = start + place_ref[2 + group * slot_count + index]
    for index in range(slot_count):
        begin = jnp.int32(0)
        for entry in starts:
            begin = jnp.where(entry <= index * block, entry, begin)
        position = pl.multiple_of(index * block - begin, block)
        turn_ref[index * block : (index + 1) * block, :] = table_ref[pl.ds(position, block), :]


def near_kernel(sizes, slot_count, slot, half_places, place_ref, table_ref, query_weight_ref, pair_weight_ref, same_ref, other_ref, out_ref, tokens_ref, *scratch):
    core = place_ref[1]
    group = place_ref[0] ^ distance_of(slot, core, half_places)
    rows = same_ref.shape[0]
    tokens_ref[pl.ds(pl.multiple_of(core * rows, rows), rows), :] = same_ref[...]
    tokens_ref[pl.ds(pl.multiple_of((1 - core) * rows, rows), rows), :] = other_ref[...]
    set_up(scratch)
    set_turn(group, slot_count, place_ref, table_ref, scratch[3])
    chosen = [(query_weight_ref, pair_weight_ref, head) for head in range(sizes[0])]
    attend_groups([attend_group(sizes, chosen, tokens_ref, scratch, [out_ref])])


def far_kernel(sizes, slot_count, numbers, half_places, parts, arrays, place_ref, table_ref, *refs):
    slots = len(numbers)
    query_refs, pair_refs, refs = refs[:arrays], refs[arrays : 2 * arrays], refs[2 * arrays :]
    token_refs, out_refs, refs = refs[:slots], refs[slots : slots + sum(parts)], refs[slots + sum(parts) :]
    bias_ref, refs = refs[0], refs[1:]
    chosen = [(*both, number) for both in zip(query_refs, pair_refs) for number in range(both[0].shape[0])]
    works, first = [], 0
    for slot in range(slots):
        scratch = [*refs[4 * slot : 4 * slot + 4], bias_ref]
        set_up(scratch, slot == 0)
        group = place_ref[0] ^ distance_of(numbers[slot], place_ref[1], half_places)
        set_turn(group, slot_count, place_ref, table_ref, scratch[3])
        works.append(attend_group(sizes, chosen, token_refs[slot], scratch, out_refs[first : first + parts[slot]]))
        first += parts[slot]
    attend_groups(works)


def scratch_for(sizes, tokens):
    heads, q_width, kv_width, nope_width, rope_width, value_width = sizes
    return [
        pltpu.VMEM((tokens, 2 * heads * nope_width), jnp.bfloat16),
        pltpu.VMEM((tokens, heads * nope_width), jnp.bfloat16),
        pltpu.VMEM((heads, tokens, 2 * value_width), jnp.bfloat16),
        pltpu.VMEM((tokens, 2 * nope_width), jnp.float32),
        pltpu.VMEM((tokens // 2, tokens // 2), jnp.float32),
    ]


def attend_near(sizes, slot_count, slot, half_places, place, table, query_weight, pair_weight, same, other):
    rows, width = same.shape
    heads, value_width = sizes[0], sizes[-1]
    vmem = pl.BlockSpec(memory_space=pltpu.VMEM)
    return pl.pallas_call(
        partial(near_kernel, sizes, slot_count, slot, half_places),
        out_shape=[
            jax.ShapeDtypeStruct((2 * rows, heads * value_width), jnp.bfloat16),
            jax.ShapeDtypeStruct((2 * rows, width), jnp.bfloat16),
        ],
        in_specs=[pl.BlockSpec(memory_space=pltpu.SMEM)] + [vmem] * 5,
        out_specs=[vmem, vmem],
        scratch_shapes=scratch_for(sizes, 2 * rows),
        compiler_params=pltpu.CompilerParams(vmem_limit_bytes=VMEM_LIMIT),
        cost_estimate=LIGHT,
        name="attend_near",
    )(place, table, query_weight, pair_weight, same, other)


def attend_far(sizes, slot_count, numbers, half_places, parts, place, table, queries, pairs, groups):
    tokens = groups[0].shape[0]
    slots, heads, value_width = len(groups), sizes[0], sizes[-1]
    vmem = pl.BlockSpec(memory_space=pltpu.VMEM)
    own = scratch_for(sizes, tokens)
    shapes = [jax.ShapeDtypeStruct((tokens, heads // part * value_width), jnp.bfloat16) for part in parts for _ in range(part)]
    results = pl.pallas_call(
        partial(far_kernel, sizes, slot_count, numbers, half_places, parts, len(queries)),
        out_shape=shapes,
        in_specs=[pl.BlockSpec(memory_space=pltpu.SMEM)] + [vmem] * (1 + 2 * len(queries) + slots),
        out_specs=[vmem] * len(shapes),
        scratch_shapes=own[4:] + own[:4] * slots,
        compiler_params=pltpu.CompilerParams(vmem_limit_bytes=VMEM_LIMIT),
        cost_estimate=LIGHT,
        name="attend_far",
    )(place, table, *queries, *pairs, *groups)
    return [results[sum(parts[:slot]) : sum(parts[: slot + 1])] for slot in range(slots)]


def place_kernel(width, count, offsets_ref, *refs):
    pieces, out_ref, sems = refs[:count], refs[-2], refs[-1]
    copies = []
    for piece in pieces:
        for low in range(0, piece.shape[1], width):
            index = len(copies)
            columns = pl.ds(pl.multiple_of(offsets_ref[index], 128), width)
            copies.append(pltpu.make_async_copy(piece.at[:, low : low + width], out_ref.at[:, columns], sems.at[index]))
            copies[-1].start()
    for copy in copies:
        copy.wait()


def place_pieces(pieces, offsets, width, out_width, held=None):
    count = len(pieces)
    any_space = pl.BlockSpec(memory_space=pl.ANY)
    operands = [jnp.stack(offsets).astype(jnp.int32), *pieces]
    specs = [pl.BlockSpec(memory_space=pltpu.SMEM)] + [pl.BlockSpec(memory_space=pltpu.VMEM)] * count
    aliases = {}
    if held is not None:
        aliases = {len(operands): 0}
        operands.append(held)
        specs.append(any_space)
    return pl.pallas_call(
        partial(place_kernel, width, count),
        out_shape=jax.ShapeDtypeStruct((pieces[0].shape[0], out_width), pieces[0].dtype),
        in_specs=specs,
        out_specs=any_space,
        scratch_shapes=[pltpu.SemaphoreType.DMA((len(offsets),))],
        input_output_aliases=aliases,
        compiler_params=pltpu.CompilerParams(vmem_limit_bytes=VMEM_LIMIT),
        cost_estimate=LIGHT,
        name="place_pieces",
    )(*operands)


def after(value, *earlier):
    return lax.optimization_barrier((value, *earlier))[0]


def shards(latents, q_gain, kv_gain, q_weight, kv_weight, lengths):
    q_width, kv_width = q_gain.shape[0], kv_gain.shape[0]
    rope_width = latents.shape[1] - q_width - kv_width
    places = lax.axis_size("seq")
    parts = lax.axis_size("parts")
    half_places = places // 2
    place = lax.axis_index("seq")
    core = lax.axis_index("head")
    part = lax.axis_index("parts")
    tokens = 2 * latents.shape[0]
    local_heads = q_weight.shape[2]
    pair_width = kv_weight.shape[3]
    nope_width = q_weight.shape[3] - rope_width
    value_width = pair_width - nope_width
    block_width = local_heads * value_width
    sizes = (q_width, kv_width, nope_width, rope_width, value_width)

    def away(slot):
        return place ^ distance_of(slot, core, half_places)

    def opposite(value):
        return lax.ppermute(value, "seq", [(s, s ^ half_places) for s in range(places)])

    def across(value, slot):
        other_slot = slot if half_places < 4 else swapped_bits(slot)
        pairs = [(2 * s + c, 2 * (s ^ distance) + c) for s in range(places) for c, distance in enumerate((slot, other_slot))]
        return lax.ppermute(value, ("seq", "head"), pairs)

    def sibling(value):
        return lax.ppermute(value, "head", [(0, 1), (1, 0)])

    def other_part(value):
        return lax.ppermute(value, "parts", [(p, p ^ 1) for p in range(parts)])

    slot_count = lengths.shape[1]
    gains = jnp.concatenate([q_gain, kv_gain])
    spot = jnp.concatenate([jnp.stack([place, core]).astype(jnp.int32), jnp.reshape(lengths, -1)])
    own_query = jnp.transpose(q_weight[0], (1, 2, 0))
    own_pair = jnp.reshape(kv_weight[0], (kv_width, local_heads * pair_width))
    positions = jnp.arange(tokens, dtype=jnp.int32)[:, None].astype(jnp.float32)
    lanes = jnp.arange(nope_width, dtype=jnp.int32)[None, :]
    angles = positions * frequencies(lanes, rope_width // 2)
    signs = jnp.where(lax.rem(lanes, rope_width) < rope_width // 2, -1.0, 1.0)
    table = jnp.concatenate([jnp.cos(angles), jnp.sin(angles) * signs], axis=1)
    share = 2 if parts % 2 == 0 and local_heads % 2 == 0 else 1
    per_part = local_heads // share
    side = lax.rem(part, share)

    sent_pair = pick(own_pair, side, per_part * pair_width, 1)
    sent_query = pick(own_query, side, per_part, 0)
    latent = prepare(latents, gains, q_width, kv_width, slot_count, spot)
    same, other = [latent], [sibling(latent)]
    for distance in range(1, half_places):
        same.append(across(latent, distance) if distance & (distance - 1) == 0 else None)
    far_query = opposite(sent_query)
    far_pair = opposite(after(sent_pair, far_query))

    joined = []

    def near(distance, *earlier):
        mixed, tokens_joined = attend_near(
            (local_heads, *sizes),
            slot_count,
            distance,
            half_places,
            spot,
            table,
            own_query,
            own_pair,
            after(same[distance], *earlier),
            other[distance],
        )
        joined.append(tokens_joined)
        return mixed

    mixed = near(0)
    arrived = [mixed]
    direct = [entry for entry in same[1:] if entry is not None]
    partner = [slot if half_places < 4 else swapped_bits(slot) for slot in range(half_places)]
    for distance in range(1, half_places):
        if same[distance] is None:
            low_bit = distance & -distance
            same[distance] = across(after(same[distance ^ low_bit], mixed), low_bit)
    for distance in range(1, half_places):
        if distance & (distance - 1) == 0:
            other.append(sibling(after(same[partner[distance]], mixed, far_query, *direct)))
        else:
            other.append(None)
    crossed_query = [other_part(after(far_query, mixed))] if share == 2 else []
    for distance in range(1, half_places):
        if other[distance] is None:
            other[distance] = sibling(after(same[partner[distance]], mixed, far_pair))
        mixed = near(distance, mixed, *(crossed_query if distance + 1 == half_places else []))
        arrived.append(across(mixed, distance))
    placed = []
    for distance in range(half_places):
        base = away(distance) * block_width
        placed.append((arrived[distance], [base + head * value_width for head in range(local_heads)]))

    out_width = places * block_width

    def flush(held):
        offsets = [offset for piece, starts in placed for offset in starts]
        held = place_pieces([piece for piece, starts in placed], offsets, value_width, out_width, held)
        placed.clear()
        return held

    queries, pairs = [far_query], [far_pair]
    numbers = [side * per_part + index for index in range(per_part)]
    if share == 2:
        queries.append(crossed_query[0])
        pairs.append(other_part(far_pair))
        numbers += [(1 - side) * per_part + index for index in range(per_part)]
    late, gates = [], []
    for distances in (list(range(half_places // 2, half_places)), list(range(1, half_places // 2)) + [0]):
        parts_of = [share if 0 < distance < half_places // 2 else 1 for distance in distances]
        mixed_some = attend_far(
            (len(numbers), *sizes),
            slot_count,
            distances,
            half_places,
            parts_of,
            after(spot, mixed, *gates),
            table,
            queries,
            pairs,
            [joined[distance] for distance in distances],
        )
        mixed, gates = mixed_some[0][0], arrived[1:]
        for distance, pieces in zip(distances, mixed_some):
            base = (away(distance) ^ half_places) * block_width
            each = len(numbers) // len(pieces)
            for index, piece in enumerate(pieces):
                spans = [base + number * value_width for number in numbers[index * each : (index + 1) * each]]
                (late if distance else placed).append((across(piece, distance) if distance else piece, spans))
    held = flush(None)
    placed.extend(late)
    held = flush(held)
    return held


def solution(mesh):
    return jax.shard_map(
        shards,
        mesh=mesh,
        in_specs=(
            P(("parts", "seq", "head"), None),
            P(),
            P(),
            P("head", None, "seq", None),
            P("head", None, "seq", None),
            P("parts", None),
        ),
        out_specs=P(("parts", "seq"), "head"),
        check_vma=False,
    )
```

```python
from functools import partial
import math

import jax
import jax.numpy as jnp
from jax import lax
from jax.experimental import pallas as pl
from jax.experimental.pallas import tpu as pltpu
from jax.sharding import PartitionSpec as P

epsilon = 1e-06
VMEM_LIMIT = 32 * 1024 * 1024
LIGHT = pl.CostEstimate(flops=1024, bytes_accessed=1024, transcendentals=0)
FAR = -(2.0**100)
NT = (((1,), (1,)), ((), ()))
NN = (((1,), (0,)), ((), ()))


def frequencies(lane, half_width):
    steps = lax.rem(lane, half_width).astype(jnp.float32)
    return jnp.exp(steps * (-math.log(10000.0) / half_width))


def swapped_bits(slot):
    return (slot & ~3) | (slot & 1) << 1 | (slot & 2) >> 1


def distance_of(slot, core, half_places):
    if half_places < 4:
        return slot
    return jnp.where(core == 0, slot, swapped_bits(slot))


def prepare_kernel(q_width, kv_width, slot_count, place_ref, latents_ref, gain_ref, out_ref):
    rows = latents_ref.shape[1]
    rope_width = latents_ref.shape[0] - q_width - kv_width
    half_width = rope_width // 2

    def normalized(low, width):
        part = latents_ref[low : low + width, :].astype(jnp.float32)
        scale = lax.rsqrt(jnp.mean(part * part, axis=0, keepdims=True) + epsilon)
        return (jnp.transpose(part * scale) * gain_ref[:, low : low + width]).astype(jnp.bfloat16)

    out_ref[:, :q_width] = normalized(0, q_width)
    out_ref[:, q_width : q_width + kv_width] = normalized(q_width, kv_width)
    spare = out_ref.shape[1] - q_width - kv_width - rope_width
    token_ids = lax.broadcasted_iota(jnp.int32, (1, rows), 1) + place_ref[1] * rows
    slot_ids = lax.broadcasted_iota(jnp.int32, (spare, rows), 0)
    begin, start, inside = jnp.zeros_like(token_ids), jnp.int32(0), jnp.zeros((spare, rows), jnp.float32)
    for slot in range(slot_count):
        stop = start + place_ref[2 + place_ref[0] * slot_count + slot]
        begin = jnp.where(token_ids >= start, start, begin)
        member = jnp.where((token_ids >= start) & (token_ids < stop), 1.0, 0.0)
        inside = jnp.where(slot_ids == slot, member, inside)
        start = stop
    position = (token_ids - begin).astype(jnp.float32)
    angle = position * frequencies(lax.broadcasted_iota(jnp.int32, (half_width, rows), 0), half_width)
    cosine, sine = jnp.cos(angle), jnp.sin(angle)
    rope = latents_ref[q_width + kv_width :, :].astype(jnp.float32)
    first, second = rope[:half_width], rope[half_width:]
    turned = jnp.concatenate([first * cosine - second * sine, second * cosine + first * sine, inside], axis=0)
    out_ref[:, q_width + kv_width :] = jnp.transpose(turned).astype(jnp.bfloat16)


def prepare(latents, gains, q_width, kv_width, slot_count, place):
    rows = latents.shape[0]
    rope_width = latents.shape[1] - q_width - kv_width
    width = q_width + kv_width + -(-(rope_width + slot_count) // 128) * 128
    vmem = pl.BlockSpec(memory_space=pltpu.VMEM)
    return pl.pallas_call(
        partial(prepare_kernel, q_width, kv_width, slot_count),
        out_shape=jax.ShapeDtypeStruct((rows, width), jnp.bfloat16),
        in_specs=[pl.BlockSpec(memory_space=pltpu.SMEM), vmem, vmem],
        out_specs=vmem,
        compiler_params=pltpu.CompilerParams(vmem_limit_bytes=VMEM_LIMIT),
        cost_estimate=LIGHT,
        name="prepare",
    )(place, jnp.transpose(latents), gains[None, :])


def pick_kernel(index_ref, source_ref, out_ref):
    out_ref[...] = source_ref[...]


def pick(source, index, block, axis):
    shape = list(source.shape)
    shape[axis] = block
    out_shape = shape
    position = lambda step, index_ref: tuple(index_ref[0] if at == axis else 0 for at in range(len(shape)))
    return pl.pallas_call(
        pick_kernel,
        grid_spec=pltpu.PrefetchScalarGridSpec(
            num_scalar_prefetch=1,
            grid=(1,),
            in_specs=[pl.BlockSpec(tuple(shape), position)],
            out_specs=pl.BlockSpec(tuple(out_shape), lambda step, index_ref: (0,) * len(out_shape)),
        ),
        out_shape=jax.ShapeDtypeStruct(tuple(out_shape), source.dtype),
        compiler_params=pltpu.CompilerParams(vmem_limit_bytes=VMEM_LIMIT),
        cost_estimate=LIGHT,
        name="pick",
    )(jnp.reshape(index, (1,)).astype(jnp.int32), source)


def attend_group(sizes, chosen, tokens_ref, scratch, out_refs):
    heads, q_width, kv_width, nope_width, rope_width, value_width = sizes
    query_width, pair_width = nope_width + rope_width, nope_width + value_width
    query_ref, key_ref, value_ref, turn_ref, bias_ref = scratch
    out_heads = heads // len(out_refs)
    tokens = tokens_ref.shape[0]
    rows = bias_ref.shape[0]
    half_width = rope_width // 2
    group_heads = nope_width // rope_width
    score_scale = query_width**-0.5 * math.log2(math.e)
    lane = lax.broadcasted_iota(jnp.int32, (tokens, nope_width), 1)
    is_first = lax.rem(lane, rope_width) < half_width
    is_rope = lane < rope_width
    rope_low = q_width + kv_width
    apart = jnp.where(is_rope, 0.0, (1.0 - tokens_ref[:, rope_low:].astype(jnp.float32)) * FAR)

    def dot(left, right, dims):
        return lax.dot_general(left, right, dims, preferred_element_type=jnp.float32)

    def query(low, high, picked):
        parts = [query_weight_ref[number, low:high, :] for query_weight_ref, _, number in picked]
        return dot(tokens_ref[:, :q_width], jnp.concatenate(parts, axis=0), NT)

    def turn_all():
        picked = list(chosen)
        while len(picked) % group_heads:
            picked.append(picked[-1])
        ropes = query(nope_width, query_width, picked)
        for first in range(0, heads, group_heads):
            rope = ropes[:, first * rope_width : (first + group_heads) * rope_width]
            swapped = jnp.where(is_first, pltpu.roll(rope, nope_width - half_width, 1), pltpu.roll(rope, half_width, 1))
            turned = (rope * turn_ref[:, :nope_width] + swapped * turn_ref[:, nope_width:]) * score_scale
            for index in range(min(group_heads, heads - first)):
                low = (2 * (first + index) + 1) * nope_width
                moved = pltpu.roll(turned, nope_width - index * rope_width, 1) if index else turned
                query_ref[:, low : low + nope_width] = jnp.where(is_rope, moved, apart).astype(jnp.bfloat16)

    def project(some):
        picked = [chosen[head] for head in some]
        nope = query(0, nope_width, picked)
        latent = tokens_ref[:, q_width:rope_low]
        pairs = [weight_ref[:, number * pair_width : (number + 1) * pair_width] for _, weight_ref, number in picked]
        pair = dot(latent, jnp.concatenate(pairs, axis=1), NN)
        for index, head in enumerate(some):
            low = 2 * head * nope_width
            part = nope[:, index * nope_width : (index + 1) * nope_width]
            query_ref[:, low : low + nope_width] = (part * score_scale).astype(jnp.bfloat16)
            both = pair[:, index * pair_width : (index + 1) * pair_width].astype(jnp.bfloat16)
            key_ref[:, head * nope_width : (head + 1) * nope_width] = both[:, :nope_width]
            value_ref[head, :, :value_width] = both[:, nope_width:]

    def score(head, half):
        low, high = half * rows, (half + 1) * rows
        queries = query_ref[low:high, 2 * head * nope_width : (2 * head + 2) * nope_width]
        shared = tokens_ref[:high, rope_low:]
        keys = jnp.concatenate([key_ref[:high, head * nope_width : (head + 1) * nope_width], shared], axis=1)
        return dot(queries, keys, NT)

    def soften(half, scores):
        low = half * rows
        last = scores[:, low:] + bias_ref[...]
        scores = jnp.concatenate([scores[:, :low], last], axis=1) if half else last
        return jnp.exp2(scores - jnp.max(scores, axis=1, keepdims=True)).astype(jnp.bfloat16)

    def mix(head, half, terms):
        low, high = half * rows, (half + 1) * rows
        mixed = dot(terms, value_ref[head, :high, :], NN)
        column = head % out_heads * value_width
        out_refs[head // out_heads][low:high, column : column + value_width] = (
            mixed[:, :value_width] / mixed[:, value_width:]
        ).astype(jnp.bfloat16)

    batches = [list(range(heads))[low : low + group_heads] for low in range(0, heads, group_heads)]
    turn_all()
    project(batches[0])
    yield
    terms = None
    for number, batch in enumerate(batches):
        scores = score(batch[0], 0)
        if number + 1 < len(batches):
            project(batches[number + 1])
        else:
            yield
        for head in batch:
            for half in range(2):
                ahead = (head, 1) if half == 0 else (head + 1, 0)
                following = score(*ahead) if ahead[0] in batch else None
                held = soften(half, scores)
                if terms is not None:
                    mix(*terms)
                terms = (head, half, held)
                scores = following
    yield
    mix(*terms)


def attend_groups(works):
    works = list(works)
    for index, work in enumerate(works):
        if index == 0:
            next(work)
        next(work)
        if index + 1 < len(works):
            next(works[index + 1])
        for rest in work:
            pass


def set_up(scratch, first=True):
    value_ref, bias_ref = scratch[2], scratch[4]
    rows = bias_ref.shape[0]
    heads, tokens, width = value_ref.shape
    if first:
        row_ids = lax.broadcasted_iota(jnp.int32, (rows, rows), 0)
        col_ids = lax.broadcasted_iota(jnp.int32, (rows, rows), 1)
        bias_ref[...] = jnp.where(col_ids <= row_ids, 0.0, -jnp.inf)
    for head in range(heads):
        value_ref[head, :, width // 2 :] = jnp.ones((tokens, width // 2), jnp.bfloat16)


def set_turn(group, slot_count, place_ref, table_ref, turn_ref):
    block = turn_ref.shape[0] // slot_count
    starts, start = [], jnp.int32(0)
    for index in range(slot_count):
        starts.append(start)
        start = start + place_ref[2 + group * slot_count + index]
    for index in range(slot_count):
        begin = jnp.int32(0)
        for entry in starts:
            begin = jnp.where(entry <= index * block, entry, begin)
        position = pl.multiple_of(index * block - begin, block)
        turn_ref[index * block : (index + 1) * block, :] = table_ref[pl.ds(position, block), :]


def near_kernel(sizes, slot_count, slot, half_places, place_ref, table_ref, query_weight_ref, pair_weight_ref, same_ref, other_ref, out_ref, tokens_ref, *scratch):
    core = place_ref[1]
    group = place_ref[0] ^ distance_of(slot, core, half_places)
    rows = same_ref.shape[0]
    tokens_ref[pl.ds(pl.multiple_of(core * rows, rows), rows), :] = same_ref[...]
    tokens_ref[pl.ds(pl.multiple_of((1 - core) * rows, rows), rows), :] = other_ref[...]
    set_up(scratch)
    set_turn(group, slot_count, place_ref, table_ref, scratch[3])
    chosen = [(query_weight_ref, pair_weight_ref, head) for head in range(sizes[0])]
    attend_groups([attend_group(sizes, chosen, tokens_ref, scratch, [out_ref])])


def far_kernel(sizes, slot_count, numbers, half_places, parts, arrays, place_ref, table_ref, *refs):
    slots = len(numbers)
    query_refs, pair_refs, refs = refs[:arrays], refs[arrays : 2 * arrays], refs[2 * arrays :]
    token_refs, out_refs, refs = refs[:slots], refs[slots : slots + sum(parts)], refs[slots + sum(parts) :]
    bias_ref, refs = refs[0], refs[1:]
    chosen = [(*both, number) for both in zip(query_refs, pair_refs) for number in range(both[0].shape[0])]
    works, first = [], 0
    for slot in range(slots):
        scratch = [*refs[4 * slot : 4 * slot + 4], bias_ref]
        set_up(scratch, slot == 0)
        group = place_ref[0] ^ distance_of(numbers[slot], place_ref[1], half_places)
        set_turn(group, slot_count, place_ref, table_ref, scratch[3])
        works.append(attend_group(sizes, chosen, token_refs[slot], scratch, out_refs[first : first + parts[slot]]))
        first += parts[slot]
    attend_groups(works)


def scratch_for(sizes, tokens):
    heads, q_width, kv_width, nope_width, rope_width, value_width = sizes
    return [
        pltpu.VMEM((tokens, 2 * heads * nope_width), jnp.bfloat16),
        pltpu.VMEM((tokens, heads * nope_width), jnp.bfloat16),
        pltpu.VMEM((heads, tokens, 2 * value_width), jnp.bfloat16),
        pltpu.VMEM((tokens, 2 * nope_width), jnp.float32),
        pltpu.VMEM((tokens // 2, tokens // 2), jnp.float32),
    ]


def attend_near(sizes, slot_count, slot, half_places, place, table, query_weight, pair_weight, same, other):
    rows, width = same.shape
    heads, value_width = sizes[0], sizes[-1]
    vmem = pl.BlockSpec(memory_space=pltpu.VMEM)
    return pl.pallas_call(
        partial(near_kernel, sizes, slot_count, slot, half_places),
        out_shape=[
            jax.ShapeDtypeStruct((2 * rows, heads * value_width), jnp.bfloat16),
            jax.ShapeDtypeStruct((2 * rows, width), jnp.bfloat16),
        ],
        in_specs=[pl.BlockSpec(memory_space=pltpu.SMEM)] + [vmem] * 5,
        out_specs=[vmem, vmem],
        scratch_shapes=scratch_for(sizes, 2 * rows),
        compiler_params=pltpu.CompilerParams(vmem_limit_bytes=VMEM_LIMIT),
        cost_estimate=LIGHT,
        name="attend_near",
    )(place, table, query_weight, pair_weight, same, other)


def attend_far(sizes, slot_count, numbers, half_places, parts, place, table, queries, pairs, groups):
    tokens = groups[0].shape[0]
    slots, heads, value_width = len(groups), sizes[0], sizes[-1]
    vmem = pl.BlockSpec(memory_space=pltpu.VMEM)
    own = scratch_for(sizes, tokens)
    shapes = [jax.ShapeDtypeStruct((tokens, heads // part * value_width), jnp.bfloat16) for part in parts for _ in range(part)]
    results = pl.pallas_call(
        partial(far_kernel, sizes, slot_count, numbers, half_places, parts, len(queries)),
        out_shape=shapes,
        in_specs=[pl.BlockSpec(memory_space=pltpu.SMEM)] + [vmem] * (1 + 2 * len(queries) + slots),
        out_specs=[vmem] * len(shapes),
        scratch_shapes=own[4:] + own[:4] * slots,
        compiler_params=pltpu.CompilerParams(vmem_limit_bytes=VMEM_LIMIT),
        cost_estimate=LIGHT,
        name="attend_far",
    )(place, table, *queries, *pairs, *groups)
    return [results[sum(parts[:slot]) : sum(parts[: slot + 1])] for slot in range(slots)]


def place_kernel(width, count, offsets_ref, *refs):
    pieces, out_ref, sems = refs[:count], refs[-2], refs[-1]
    copies = []
    for piece in pieces:
        for low in range(0, piece.shape[1], width):
            index = len(copies)
            columns = pl.ds(pl.multiple_of(offsets_ref[index], 128), width)
            copies.append(pltpu.make_async_copy(piece.at[:, low : low + width], out_ref.at[:, columns], sems.at[index]))
            copies[-1].start()
    for copy in copies:
        copy.wait()


def place_pieces(pieces, offsets, width, out_width, held=None):
    count = len(pieces)
    any_space = pl.BlockSpec(memory_space=pl.ANY)
    operands = [jnp.stack(offsets).astype(jnp.int32), *pieces]
    specs = [pl.BlockSpec(memory_space=pltpu.SMEM)] + [pl.BlockSpec(memory_space=pltpu.VMEM)] * count
    aliases = {}
    if held is not None:
        aliases = {len(operands): 0}
        operands.append(held)
        specs.append(any_space)
    return pl.pallas_call(
        partial(place_kernel, width, count),
        out_shape=jax.ShapeDtypeStruct((pieces[0].shape[0], out_width), pieces[0].dtype),
        in_specs=specs,
        out_specs=any_space,
        scratch_shapes=[pltpu.SemaphoreType.DMA((len(offsets),))],
        input_output_aliases=aliases,
        compiler_params=pltpu.CompilerParams(vmem_limit_bytes=VMEM_LIMIT),
        cost_estimate=LIGHT,
        name="place_pieces",
    )(*operands)


def after(value, *earlier):
    return lax.optimization_barrier((value, *earlier))[0]


def shards(latents, q_gain, kv_gain, q_weight, kv_weight, lengths):
    q_width, kv_width = q_gain.shape[0], kv_gain.shape[0]
    rope_width = latents.shape[1] - q_width - kv_width
    places = lax.axis_size("seq")
    parts = lax.axis_size("parts")
    half_places = places // 2
    place = lax.axis_index("seq")
    core = lax.axis_index("head")
    part = lax.axis_index("parts")
    tokens = 2 * latents.shape[0]
    local_heads = q_weight.shape[2]
    pair_width = kv_weight.shape[3]
    nope_width = q_weight.shape[3] - rope_width
    value_width = pair_width - nope_width
    block_width = local_heads * value_width
    sizes = (q_width, kv_width, nope_width, rope_width, value_width)

    def away(slot):
        return place ^ distance_of(slot, core, half_places)

    def opposite(value):
        return lax.ppermute(value, "seq", [(s, s ^ half_places) for s in range(places)])

    def across(value, slot):
        other_slot = slot if half_places < 4 else swapped_bits(slot)
        pairs = [(2 * s + c, 2 * (s ^ distance) + c) for s in range(places) for c, distance in enumerate((slot, other_slot))]
        return lax.ppermute(value, ("seq", "head"), pairs)

    def sibling(value):
        return lax.ppermute(value, "head", [(0, 1), (1, 0)])

    def other_part(value):
        return lax.ppermute(value, "parts", [(p, p ^ 1) for p in range(parts)])

    slot_count = lengths.shape[1]
    gains = jnp.concatenate([q_gain, kv_gain])
    spot = jnp.concatenate([jnp.stack([place, core]).astype(jnp.int32), jnp.reshape(lengths, -1)])
    own_query = jnp.transpose(q_weight[0], (1, 2, 0))
    own_pair = jnp.reshape(kv_weight[0], (kv_width, local_heads * pair_width))
    positions = jnp.arange(tokens, dtype=jnp.int32)[:, None].astype(jnp.float32)
    lanes = jnp.arange(nope_width, dtype=jnp.int32)[None, :]
    angles = positions * frequencies(lanes, rope_width // 2)
    signs = jnp.where(lax.rem(lanes, rope_width) < rope_width // 2, -1.0, 1.0)
    table = jnp.concatenate([jnp.cos(angles), jnp.sin(angles) * signs], axis=1)
    share = 2 if parts % 2 == 0 and local_heads % 2 == 0 else 1
    per_part = local_heads // share
    side = lax.rem(part, share)

    sent_pair = pick(own_pair, side, per_part * pair_width, 1)
    sent_query = pick(own_query, side, per_part, 0)
    latent = prepare(latents, gains, q_width, kv_width, slot_count, spot)
    same, other = [latent], [sibling(latent)]
    for distance in range(1, half_places):
        same.append(across(latent, distance) if distance & (distance - 1) == 0 else None)
    far_query = opposite(sent_query)
    far_pair = opposite(after(sent_pair, far_query))

    joined = []

    def near(distance, *earlier):
        mixed, tokens_joined = attend_near(
            (local_heads, *sizes),
            slot_count,
            distance,
            half_places,
            spot,
            table,
            own_query,
            own_pair,
            after(same[distance], *earlier),
            other[distance],
        )
        joined.append(tokens_joined)
        return mixed

    mixed = near(0)
    arrived = [mixed]
    direct = [entry for entry in same[1:] if entry is not None]
    partner = [slot if half_places < 4 else swapped_bits(slot) for slot in range(half_places)]
    for distance in range(1, half_places):
        if same[distance] is None:
            low_bit = distance & -distance
            same[distance] = across(after(same[distance ^ low_bit], mixed), low_bit)
    for distance in range(1, half_places):
        if distance & (distance - 1) == 0:
            other.append(sibling(after(same[partner[distance]], mixed, far_query, *direct)))
        else:
            other.append(None)
    crossed_query = [other_part(after(far_query, mixed))] if share == 2 else []
    for distance in range(1, half_places):
        if other[distance] is None:
            other[distance] = sibling(after(same[partner[distance]], mixed, far_pair, *crossed_query))
        mixed = near(distance, mixed)
        arrived.append(across(mixed, distance))
    placed = []
    for distance in range(half_places):
        base = away(distance) * block_width
        placed.append((arrived[distance], [base + head * value_width for head in range(local_heads)]))

    out_width = places * block_width

    def flush(held):
        offsets = [offset for piece, starts in placed for offset in starts]
        held = place_pieces([piece for piece, starts in placed], offsets, value_width, out_width, held)
        placed.clear()
        return held

    queries, pairs = [far_query], [far_pair]
    numbers = [side * per_part + index for index in range(per_part)]
    if share == 2:
        queries.append(crossed_query[0])
        pairs.append(other_part(far_pair))
        numbers += [(1 - side) * per_part + index for index in range(per_part)]
    late, gates = [], []
    for distances in (list(range(half_places // 2, half_places)), list(range(1, half_places // 2)) + [0]):
        parts_of = [share if 0 < distance < half_places // 2 else 1 for distance in distances]
        mixed_some = attend_far(
            (len(numbers), *sizes),
            slot_count,
            distances,
            half_places,
            parts_of,
            after(spot, mixed, *gates),
            table,
            queries,
            pairs,
            [joined[distance] for distance in distances],
        )
        mixed, gates = mixed_some[0][0], arrived[1:]
        for distance, pieces in zip(distances, mixed_some):
            base = (away(distance) ^ half_places) * block_width
            each = len(numbers) // len(pieces)
            for index, piece in enumerate(pieces):
                spans = [base + number * value_width for number in numbers[index * each : (index + 1) * each]]
                (late if distance else placed).append((across(piece, distance) if distance else piece, spans))
    held = flush(None)
    placed.extend(late)
    held = flush(held)
    return held


def solution(mesh):
    return jax.shard_map(
        shards,
        mesh=mesh,
        in_specs=(
            P(("parts", "seq", "head"), None),
            P(),
            P(),
            P("head", None, "seq", None),
            P("head", None, "seq", None),
            P("parts", None),
        ),
        out_specs=P(("parts", "seq"), "head"),
        check_vma=False,
    )
```

```python
from functools import partial
import math

import jax
import jax.numpy as jnp
from jax import lax
from jax.experimental import pallas as pl
from jax.experimental.pallas import tpu as pltpu
from jax.sharding import PartitionSpec as P

epsilon = 1e-06
VMEM_LIMIT = 32 * 1024 * 1024
LIGHT = pl.CostEstimate(flops=1024, bytes_accessed=1024, transcendentals=0)
FAR = -(2.0**100)
NT = (((1,), (1,)), ((), ()))
NN = (((1,), (0,)), ((), ()))


def frequencies(lane, half_width):
    steps = lax.rem(lane, half_width).astype(jnp.float32)
    return jnp.exp(steps * (-math.log(10000.0) / half_width))


def swapped_bits(slot):
    return (slot & ~3) | (slot & 1) << 1 | (slot & 2) >> 1


def distance_of(slot, core, half_places):
    if half_places < 4:
        return slot
    return jnp.where(core == 0, slot, swapped_bits(slot))


def prepare_kernel(q_width, kv_width, slot_count, place_ref, latents_ref, gain_ref, out_ref):
    rows = latents_ref.shape[1]
    rope_width = latents_ref.shape[0] - q_width - kv_width
    half_width = rope_width // 2

    def normalized(low, width):
        part = latents_ref[low : low + width, :].astype(jnp.float32)
        scale = lax.rsqrt(jnp.mean(part * part, axis=0, keepdims=True) + epsilon)
        return (jnp.transpose(part * scale) * gain_ref[:, low : low + width]).astype(jnp.bfloat16)

    out_ref[:, :q_width] = normalized(0, q_width)
    out_ref[:, q_width : q_width + kv_width] = normalized(q_width, kv_width)
    spare = out_ref.shape[1] - q_width - kv_width - rope_width
    token_ids = lax.broadcasted_iota(jnp.int32, (1, rows), 1) + place_ref[1] * rows
    slot_ids = lax.broadcasted_iota(jnp.int32, (spare, rows), 0)
    begin, start, inside = jnp.zeros_like(token_ids), jnp.int32(0), jnp.zeros((spare, rows), jnp.float32)
    for slot in range(slot_count):
        stop = start + place_ref[2 + place_ref[0] * slot_count + slot]
        begin = jnp.where(token_ids >= start, start, begin)
        member = jnp.where((token_ids >= start) & (token_ids < stop), 1.0, 0.0)
        inside = jnp.where(slot_ids == slot, member, inside)
        start = stop
    position = (token_ids - begin).astype(jnp.float32)
    angle = position * frequencies(lax.broadcasted_iota(jnp.int32, (half_width, rows), 0), half_width)
    cosine, sine = jnp.cos(angle), jnp.sin(angle)
    rope = latents_ref[q_width + kv_width :, :].astype(jnp.float32)
    first, second = rope[:half_width], rope[half_width:]
    turned = jnp.concatenate([first * cosine - second * sine, second * cosine + first * sine, inside], axis=0)
    out_ref[:, q_width + kv_width :] = jnp.transpose(turned).astype(jnp.bfloat16)


def prepare(latents, gains, q_width, kv_width, slot_count, place):
    rows = latents.shape[0]
    rope_width = latents.shape[1] - q_width - kv_width
    width = q_width + kv_width + -(-(rope_width + slot_count) // 128) * 128
    vmem = pl.BlockSpec(memory_space=pltpu.VMEM)
    return pl.pallas_call(
        partial(prepare_kernel, q_width, kv_width, slot_count),
        out_shape=jax.ShapeDtypeStruct((rows, width), jnp.bfloat16),
        in_specs=[pl.BlockSpec(memory_space=pltpu.SMEM), vmem, vmem],
        out_specs=vmem,
        compiler_params=pltpu.CompilerParams(vmem_limit_bytes=VMEM_LIMIT),
        cost_estimate=LIGHT,
        name="prepare",
    )(place, jnp.transpose(latents), gains[None, :])


def pick_kernel(index_ref, source_ref, out_ref):
    out_ref[...] = source_ref[...]


def pick(source, index, block, axis):
    shape = list(source.shape)
    shape[axis] = block
    out_shape = shape
    position = lambda step, index_ref: tuple(index_ref[0] if at == axis else 0 for at in range(len(shape)))
    return pl.pallas_call(
        pick_kernel,
        grid_spec=pltpu.PrefetchScalarGridSpec(
            num_scalar_prefetch=1,
            grid=(1,),
            in_specs=[pl.BlockSpec(tuple(shape), position)],
            out_specs=pl.BlockSpec(tuple(out_shape), lambda step, index_ref: (0,) * len(out_shape)),
        ),
        out_shape=jax.ShapeDtypeStruct(tuple(out_shape), source.dtype),
        compiler_params=pltpu.CompilerParams(vmem_limit_bytes=VMEM_LIMIT),
        cost_estimate=LIGHT,
        name="pick",
    )(jnp.reshape(index, (1,)).astype(jnp.int32), source)


def attend_group(sizes, chosen, tokens_ref, scratch, out_refs):
    heads, q_width, kv_width, nope_width, rope_width, value_width = sizes
    query_width, pair_width = nope_width + rope_width, nope_width + value_width
    query_ref, key_ref, value_ref, turn_ref, bias_ref = scratch
    out_heads = heads // len(out_refs)
    tokens = tokens_ref.shape[0]
    rows = bias_ref.shape[0]
    half_width = rope_width // 2
    group_heads = nope_width // rope_width
    score_scale = query_width**-0.5 * math.log2(math.e)
    lane = lax.broadcasted_iota(jnp.int32, (tokens, nope_width), 1)
    is_first = lax.rem(lane, rope_width) < half_width
    is_rope = lane < rope_width
    rope_low = q_width + kv_width
    apart = jnp.where(is_rope, 0.0, (1.0 - tokens_ref[:, rope_low:].astype(jnp.float32)) * FAR)

    def dot(left, right, dims):
        return lax.dot_general(left, right, dims, preferred_element_type=jnp.float32)

    def query(low, high, picked):
        parts = [query_weight_ref[number, low:high, :] for query_weight_ref, _, number in picked]
        return dot(tokens_ref[:, :q_width], jnp.concatenate(parts, axis=0), NT)

    def turn_all():
        picked = list(chosen)
        while len(picked) % group_heads:
            picked.append(picked[-1])
        ropes = query(nope_width, query_width, picked)
        for first in range(0, heads, group_heads):
            rope = ropes[:, first * rope_width : (first + group_heads) * rope_width]
            swapped = jnp.where(is_first, pltpu.roll(rope, nope_width - half_width, 1), pltpu.roll(rope, half_width, 1))
            turned = (rope * turn_ref[:, :nope_width] + swapped * turn_ref[:, nope_width:]) * score_scale
            for index in range(min(group_heads, heads - first)):
                low = (2 * (first + index) + 1) * nope_width
                moved = pltpu.roll(turned, nope_width - index * rope_width, 1) if index else turned
                query_ref[:, low : low + nope_width] = jnp.where(is_rope, moved, apart).astype(jnp.bfloat16)

    def project(some):
        picked = [chosen[head] for head in some]
        nope = query(0, nope_width, picked)
        latent = tokens_ref[:, q_width:rope_low]
        pairs = [weight_ref[:, number * pair_width : (number + 1) * pair_width] for _, weight_ref, number in picked]
        pair = dot(latent, jnp.concatenate(pairs, axis=1), NN)
        for index, head in enumerate(some):
            low = 2 * head * nope_width
            part = nope[:, index * nope_width : (index + 1) * nope_width]
            query_ref[:, low : low + nope_width] = (part * score_scale).astype(jnp.bfloat16)
            both = pair[:, index * pair_width : (index + 1) * pair_width].astype(jnp.bfloat16)
            key_ref[:, head * nope_width : (head + 1) * nope_width] = both[:, :nope_width]
            value_ref[head, :, :value_width] = both[:, nope_width:]

    def score(head, half):
        low, high = half * rows, (half + 1) * rows
        queries = query_ref[low:high, 2 * head * nope_width : (2 * head + 2) * nope_width]
        shared = tokens_ref[:high, rope_low:]
        keys = jnp.concatenate([key_ref[:high, head * nope_width : (head + 1) * nope_width], shared], axis=1)
        return dot(queries, keys, NT)

    def soften(half, scores):
        low = half * rows
        last = scores[:, low:] + bias_ref[...]
        scores = jnp.concatenate([scores[:, :low], last], axis=1) if half else last
        return jnp.exp2(scores - jnp.max(scores, axis=1, keepdims=True)).astype(jnp.bfloat16)

    def mix(head, half, terms):
        low, high = half * rows, (half + 1) * rows
        mixed = dot(terms, value_ref[head, :high, :], NN)
        column = head % out_heads * value_width
        out_refs[head // out_heads][low:high, column : column + value_width] = (
            mixed[:, :value_width] / mixed[:, value_width:]
        ).astype(jnp.bfloat16)

    batches = [list(range(heads))[low : low + group_heads] for low in range(0, heads, group_heads)]
    turn_all()
    project(batches[0])
    yield
    terms = None
    for number, batch in enumerate(batches):
        scores = score(batch[0], 0)
        if number + 1 < len(batches):
            project(batches[number + 1])
        else:
            yield
        for head in batch:
            for half in range(2):
                ahead = (head, 1) if half == 0 else (head + 1, 0)
                following = score(*ahead) if ahead[0] in batch else None
                held = soften(half, scores)
                if terms is not None:
                    mix(*terms)
                terms = (head, half, held)
                scores = following
    yield
    mix(*terms)


def attend_groups(works):
    works = list(works)
    for index, work in enumerate(works):
        if index == 0:
            next(work)
        next(work)
        if index + 1 < len(works):
            next(works[index + 1])
        for rest in work:
            pass


def set_up(scratch, first=True):
    value_ref, bias_ref = scratch[2], scratch[4]
    rows = bias_ref.shape[0]
    heads, tokens, width = value_ref.shape
    if first:
        row_ids = lax.broadcasted_iota(jnp.int32, (rows, rows), 0)
        col_ids = lax.broadcasted_iota(jnp.int32, (rows, rows), 1)
        bias_ref[...] = jnp.where(col_ids <= row_ids, 0.0, -jnp.inf)
    for head in range(heads):
        value_ref[head, :, width // 2 :] = jnp.ones((tokens, width // 2), jnp.bfloat16)


def set_turn(group, slot_count, place_ref, table_ref, turn_ref):
    block = turn_ref.shape[0] // slot_count
    starts, start = [], jnp.int32(0)
    for index in range(slot_count):
        starts.append(start)
        start = start + place_ref[2 + group * slot_count + index]
    for index in range(slot_count):
        begin = jnp.int32(0)
        for entry in starts:
            begin = jnp.where(entry <= index * block, entry, begin)
        position = pl.multiple_of(index * block - begin, block)
        turn_ref[index * block : (index + 1) * block, :] = table_ref[pl.ds(position, block), :]


def near_kernel(sizes, slot_count, slot, half_places, place_ref, table_ref, query_weight_ref, pair_weight_ref, same_ref, other_ref, out_ref, tokens_ref, *scratch):
    core = place_ref[1]
    group = place_ref[0] ^ distance_of(slot, core, half_places)
    rows = same_ref.shape[0]
    tokens_ref[pl.ds(pl.multiple_of(core * rows, rows), rows), :] = same_ref[...]
    tokens_ref[pl.ds(pl.multiple_of((1 - core) * rows, rows), rows), :] = other_ref[...]
    set_up(scratch)
    set_turn(group, slot_count, place_ref, table_ref, scratch[3])
    chosen = [(query_weight_ref, pair_weight_ref, head) for head in range(sizes[0])]
    attend_groups([attend_group(sizes, chosen, tokens_ref, scratch, [out_ref])])


def far_kernel(sizes, slot_count, numbers, half_places, parts, arrays, place_ref, table_ref, *refs):
    slots = len(numbers)
    query_refs, pair_refs, refs = refs[:arrays], refs[arrays : 2 * arrays], refs[2 * arrays :]
    token_refs, out_refs, refs = refs[:slots], refs[slots : slots + sum(parts)], refs[slots + sum(parts) :]
    bias_ref, refs = refs[0], refs[1:]
    chosen = [(*both, number) for both in zip(query_refs, pair_refs) for number in range(both[0].shape[0])]
    works, first = [], 0
    for slot in range(slots):
        scratch = [*refs[4 * slot : 4 * slot + 4], bias_ref]
        set_up(scratch, slot == 0)
        group = place_ref[0] ^ distance_of(numbers[slot], place_ref[1], half_places)
        set_turn(group, slot_count, place_ref, table_ref, scratch[3])
        works.append(attend_group(sizes, chosen, token_refs[slot], scratch, out_refs[first : first + parts[slot]]))
        first += parts[slot]
    attend_groups(works)


def scratch_for(sizes, tokens):
    heads, q_width, kv_width, nope_width, rope_width, value_width = sizes
    return [
        pltpu.VMEM((tokens, 2 * heads * nope_width), jnp.bfloat16),
        pltpu.VMEM((tokens, heads * nope_width), jnp.bfloat16),
        pltpu.VMEM((heads, tokens, 2 * value_width), jnp.bfloat16),
        pltpu.VMEM((tokens, 2 * nope_width), jnp.float32),
        pltpu.VMEM((tokens // 2, tokens // 2), jnp.float32),
    ]


def attend_near(sizes, slot_count, slot, half_places, place, table, query_weight, pair_weight, same, other):
    rows, width = same.shape
    heads, value_width = sizes[0], sizes[-1]
    vmem = pl.BlockSpec(memory_space=pltpu.VMEM)
    return pl.pallas_call(
        partial(near_kernel, sizes, slot_count, slot, half_places),
        out_shape=[
            jax.ShapeDtypeStruct((2 * rows, heads * value_width), jnp.bfloat16),
            jax.ShapeDtypeStruct((2 * rows, width), jnp.bfloat16),
        ],
        in_specs=[pl.BlockSpec(memory_space=pltpu.SMEM)] + [vmem] * 5,
        out_specs=[vmem, vmem],
        scratch_shapes=scratch_for(sizes, 2 * rows),
        compiler_params=pltpu.CompilerParams(vmem_limit_bytes=VMEM_LIMIT),
        cost_estimate=LIGHT,
        name="attend_near",
    )(place, table, query_weight, pair_weight, same, other)


def attend_far(sizes, slot_count, numbers, half_places, parts, place, table, queries, pairs, groups):
    tokens = groups[0].shape[0]
    slots, heads, value_width = len(groups), sizes[0], sizes[-1]
    vmem = pl.BlockSpec(memory_space=pltpu.VMEM)
    own = scratch_for(sizes, tokens)
    shapes = [jax.ShapeDtypeStruct((tokens, heads // part * value_width), jnp.bfloat16) for part in parts for _ in range(part)]
    results = pl.pallas_call(
        partial(far_kernel, sizes, slot_count, numbers, half_places, parts, len(queries)),
        out_shape=shapes,
        in_specs=[pl.BlockSpec(memory_space=pltpu.SMEM)] + [vmem] * (1 + 2 * len(queries) + slots),
        out_specs=[vmem] * len(shapes),
        scratch_shapes=own[4:] + own[:4] * slots,
        compiler_params=pltpu.CompilerParams(vmem_limit_bytes=VMEM_LIMIT),
        cost_estimate=LIGHT,
        name="attend_far",
    )(place, table, *queries, *pairs, *groups)
    return [results[sum(parts[:slot]) : sum(parts[: slot + 1])] for slot in range(slots)]


def place_kernel(width, count, offsets_ref, *refs):
    pieces, out_ref, sems = refs[:count], refs[-2], refs[-1]
    copies = []
    for piece in pieces:
        for low in range(0, piece.shape[1], width):
            index = len(copies)
            columns = pl.ds(pl.multiple_of(offsets_ref[index], 128), width)
            copies.append(pltpu.make_async_copy(piece.at[:, low : low + width], out_ref.at[:, columns], sems.at[index]))
            copies[-1].start()
    for copy in copies:
        copy.wait()


def place_pieces(pieces, offsets, width, out_width, held=None):
    count = len(pieces)
    any_space = pl.BlockSpec(memory_space=pl.ANY)
    operands = [jnp.stack(offsets).astype(jnp.int32), *pieces]
    specs = [pl.BlockSpec(memory_space=pltpu.SMEM)] + [pl.BlockSpec(memory_space=pltpu.VMEM)] * count
    aliases = {}
    if held is not None:
        aliases = {len(operands): 0}
        operands.append(held)
        specs.append(any_space)
    return pl.pallas_call(
        partial(place_kernel, width, count),
        out_shape=jax.ShapeDtypeStruct((pieces[0].shape[0], out_width), pieces[0].dtype),
        in_specs=specs,
        out_specs=any_space,
        scratch_shapes=[pltpu.SemaphoreType.DMA((len(offsets),))],
        input_output_aliases=aliases,
        compiler_params=pltpu.CompilerParams(vmem_limit_bytes=VMEM_LIMIT),
        cost_estimate=LIGHT,
        name="place_pieces",
    )(*operands)


def after(value, *earlier):
    return lax.optimization_barrier((value, *earlier))[0]


def shards(latents, q_gain, kv_gain, q_weight, kv_weight, lengths):
    q_width, kv_width = q_gain.shape[0], kv_gain.shape[0]
    rope_width = latents.shape[1] - q_width - kv_width
    places = lax.axis_size("seq")
    parts = lax.axis_size("parts")
    half_places = places // 2
    place = lax.axis_index("seq")
    core = lax.axis_index("head")
    part = lax.axis_index("parts")
    tokens = 2 * latents.shape[0]
    local_heads = q_weight.shape[2]
    pair_width = kv_weight.shape[3]
    nope_width = q_weight.shape[3] - rope_width
    value_width = pair_width - nope_width
    block_width = local_heads * value_width
    sizes = (q_width, kv_width, nope_width, rope_width, value_width)

    def away(slot):
        return place ^ distance_of(slot, core, half_places)

    def opposite(value):
        return lax.ppermute(value, "seq", [(s, s ^ half_places) for s in range(places)])

    def across(value, slot):
        other_slot = slot if half_places < 4 else swapped_bits(slot)
        pairs = [(2 * s + c, 2 * (s ^ distance) + c) for s in range(places) for c, distance in enumerate((slot, other_slot))]
        return lax.ppermute(value, ("seq", "head"), pairs)

    def sibling(value):
        return lax.ppermute(value, "head", [(0, 1), (1, 0)])

    def other_part(value):
        return lax.ppermute(value, "parts", [(p, p ^ 1) for p in range(parts)])

    slot_count = lengths.shape[1]
    gains = jnp.concatenate([q_gain, kv_gain])
    spot = jnp.concatenate([jnp.stack([place, core]).astype(jnp.int32), jnp.reshape(lengths, -1)])
    own_query = jnp.transpose(q_weight[0], (1, 2, 0))
    own_pair = jnp.reshape(kv_weight[0], (kv_width, local_heads * pair_width))
    positions = jnp.arange(tokens, dtype=jnp.int32)[:, None].astype(jnp.float32)
    lanes = jnp.arange(nope_width, dtype=jnp.int32)[None, :]
    angles = positions * frequencies(lanes, rope_width // 2)
    signs = jnp.where(lax.rem(lanes, rope_width) < rope_width // 2, -1.0, 1.0)
    table = jnp.concatenate([jnp.cos(angles), jnp.sin(angles) * signs], axis=1)
    share = 2 if parts % 2 == 0 and local_heads % 2 == 0 else 1
    per_part = local_heads // share
    side = lax.rem(part, share)

    sent_pair = pick(own_pair, side, per_part * pair_width, 1)
    sent_query = pick(own_query, side, per_part, 0)
    latent = prepare(latents, gains, q_width, kv_width, slot_count, spot)
    same, other = [latent], [sibling(latent)]
    for distance in range(1, half_places):
        same.append(across(latent, distance) if distance & (distance - 1) == 0 else None)
    far_query = opposite(sent_query)
    far_pair = opposite(after(sent_pair, far_query))

    joined = []

    def near(distance, *earlier):
        mixed, tokens_joined = attend_near(
            (local_heads, *sizes),
            slot_count,
            distance,
            half_places,
            spot,
            table,
            own_query,
            own_pair,
            after(same[distance], *earlier),
            other[distance],
        )
        joined.append(tokens_joined)
        return mixed

    mixed = near(0)
    arrived = [mixed]
    direct = [entry for entry in same[1:] if entry is not None]
    partner = [slot if half_places < 4 else swapped_bits(slot) for slot in range(half_places)]
    for distance in range(1, half_places):
        if same[distance] is None:
            low_bit = distance & -distance
            same[distance] = across(after(same[distance ^ low_bit], mixed), low_bit)
    for distance in range(1, half_places):
        if distance & (distance - 1) == 0:
            other.append(sibling(after(same[partner[distance]], mixed, far_query, *direct)))
        else:
            other.append(None)
    crossed_query = [other_part(after(far_query, mixed))] if share == 2 else []
    for distance in range(1, half_places):
        if other[distance] is None:
            other[distance] = sibling(after(same[partner[distance]], mixed, far_pair))
        mixed = near(distance, mixed, *(crossed_query if distance + 1 == half_places else []))
        arrived.append(across(mixed, distance))
    placed = []
    for distance in range(half_places):
        base = away(distance) * block_width
        placed.append((arrived[distance], [base + head * value_width for head in range(local_heads)]))

    out_width = places * block_width

    def flush(held):
        offsets = [offset for piece, starts in placed for offset in starts]
        held = place_pieces([piece for piece, starts in placed], offsets, value_width, out_width, held)
        placed.clear()
        return held

    queries, pairs = [far_query], [far_pair]
    numbers = [side * per_part + index for index in range(per_part)]
    if share == 2:
        queries.append(crossed_query[0])
        pairs.append(other_part(far_pair))
        numbers += [(1 - side) * per_part + index for index in range(per_part)]
    late, gates = [], []
    for distances in (list(range(half_places // 2, half_places)), list(range(1, half_places // 2)) + [0]):
        parts_of = [share if 0 < distance < half_places // 2 else 1 for distance in distances]
        mixed_some = attend_far(
            (len(numbers), *sizes),
            slot_count,
            distances,
            half_places,
            parts_of,
            after(spot, mixed, *gates),
            table,
            queries,
            pairs,
            [joined[distance] for distance in distances],
        )
        mixed, gates = mixed_some[0][0], arrived[1:]
        for distance, pieces in zip(distances, mixed_some):
            base = (away(distance) ^ half_places) * block_width
            each = len(numbers) // len(pieces)
            for index, piece in enumerate(pieces):
                spans = [base + number * value_width for number in numbers[index * each : (index + 1) * each]]
                (late if distance else placed).append((across(piece, distance) if distance else piece, spans))
    held = flush(None)
    placed.extend(late)
    held = flush(held)
    return held


def solution(mesh):
    return jax.shard_map(
        shards,
        mesh=mesh,
        in_specs=(
            P(("parts", "seq", "head"), None),
            P(),
            P(),
            P("head", None, "seq", None),
            P("head", None, "seq", None),
            P("parts", None),
        ),
        out_specs=P(("parts", "seq"), "head"),
        check_vma=False,
    )
```
